32 devices in a mesh: prow: 4 (over x, core), pcol: 8 (over z, y).
Axes of the slice: x: 2, y: 2, z: 4, core: 2. Of those that a mesh axis runs over, the one named last changes fastest.
Arguments:
- diag_block: float32 [512, 512], P('prow'), as said below
- panel_cols: float32 [8192, 512], P(('prow', 'pcol')), may hold values from -3 to 3
- trailing: float32 [8192, 8192], P('prow', 'pcol'), may hold values from -6 to 6
- geno_top: float32 [512, 2048], P('prow', 'pcol'), may hold values from -6 to 6
- geno_rest: float32 [8192, 2048], P('prow', 'pcol'), may hold values from -6 to 6
- pheno_top: float32 [512], P('prow'), may hold values from -6 to 6
- pheno_rest: float32 [8192], P('prow'), may hold values from -6 to 6
Outputs:
- updated_block: float32 [8192, 8192], P('prow', 'pcol')
- panel_factor: float32 [8192, 512], P(('prow', 'pcol'))
- white_geno: float32 [8192, 2048], P('prow', 'pcol')
- score_stat: float32 [2048], P('pcol')
- info_stat: float32 [2048], P('pcol')
The draws below stay inside these ranges and needn't reach their ends.
Inputs may be any that keep to these rules, and one draw needn't show every extreme that they name: diag_block is symmetric and positive definite; its diagonal entries lie between 3 and 4.5 and its off-diagonal entries have magnitude at most 0.8.
All inputs are finite; a program needn't handle non-finite values.
Results may differ from the reference program's by a relative error of at most 0.000096.
Values sent between devices are 32-bit elements; how exact they have to be, the bound alone decides.
A program may use at most 64 MiB of HBM per device.

```python
import jax
import jax.numpy as jnp
from jax import lax

NB = 512
ROWS = 8192
VARIANTS = 2048


def draw_diag_block(key, part):
    key_scale, key_noise, key_diag = jax.random.split(key, 3)
    row_scales = jax.random.uniform(key_scale, (NB,), jnp.float32, 0.6, 1.25)
    noise_vals = jax.random.uniform(key_noise, (NB, NB), jnp.float32, -1.0, 1.0)
    positions = jnp.arange(NB).astype(jnp.float32)
    reach = jnp.float32(NB) / 16.0
    kernel = jnp.exp(-jnp.abs(positions[:, None] - positions[None, :]) / reach)
    coupled = 0.5 * row_scales[:, None] * row_scales[None, :] * kernel
    rough = 0.15 * (noise_vals + noise_vals.T) / jnp.float32(NB)
    diag_vals = jax.random.uniform(key_diag, (NB,), jnp.float32, 3.0, 4.5)
    identity = jnp.eye(NB, dtype=jnp.float32)
    return (coupled + rough) * (1.0 - identity) + identity * diag_vals[:, None]


def steps_of(key, dims, shards, low, top_value):
    def one(dim, parts):
        heights = jax.random.uniform(jax.random.fold_in(jax.random.fold_in(key, 6), dim), (parts,), jnp.float32, low / len(shards), top_value / len(shards))
        return jnp.repeat(jnp.exp(heights), dims[dim] // parts).reshape((-1,) + (1,) * (len(dims) - dim - 1))

    level = one(*shards[0])
    for cut in shards[1:]:
        level = level * one(*cut)
    return level


def centred(rng, extent, scale, bound, cuts=(), held_as=jnp.bfloat16):
    array = jax.random.normal(rng, extent, jnp.float32) * scale
    if len(cuts) > 0:
        array = steps_of(rng, extent, cuts, -0.22, 0.18) * array
    return jnp.clip(array, min=-bound, max=bound).astype(held_as)


def setup_inputs(seed: int = 0) -> dict:
    key_of = jax.random.split(jax.random.key(seed), 8)
    return {
        "diag_block": draw_diag_block(jax.random.fold_in(key_of[7], 71), 0),
        "panel_cols": centred(key_of[1], (ROWS, NB), 0.2, 3.0, ((0, 32),), jnp.float32),
        "trailing": centred(key_of[2], (ROWS, ROWS), 1.0, 6.0, ((0, 4), (1, 8)), jnp.float32),
        "geno_top": centred(key_of[3], (NB, VARIANTS), 1.0, 6.0, ((0, 4), (1, 8)), jnp.float32),
        "geno_rest": centred(key_of[4], (ROWS, VARIANTS), 1.0, 6.0, ((0, 4), (1, 8)), jnp.float32),
        "pheno_top": centred(key_of[5], (NB,), 1.0, 6.0, ((0, 4),), jnp.float32),
        "pheno_rest": centred(key_of[6], (ROWS,), 1.0, 6.0, ((0, 4),), jnp.float32),
    }


def reference(diag_block, panel_cols, trailing, geno_top, geno_rest, pheno_top, pheno_rest):
    highest = lax.Precision.HIGHEST
    factor = jnp.linalg.cholesky(diag_block)
    panel_factor = lax.linalg.triangular_solve(factor, panel_cols, left_side=False, lower=True, transpose_a=True)
    updated_block = trailing - jnp.dot(panel_factor, panel_factor.T, precision=highest)
    top_white = lax.linalg.triangular_solve(factor, geno_top, left_side=True, lower=True)
    pheno_white_top = lax.linalg.triangular_solve(factor, pheno_top[:, None], left_side=True, lower=True)[:, 0]
    white_geno = geno_rest - jnp.dot(panel_factor, top_white, precision=highest)
    pheno_white = pheno_rest - jnp.dot(panel_factor, pheno_white_top, precision=highest)
    count = NB + ROWS
    score_stat = (jnp.dot(pheno_white, white_geno, precision=highest) + jnp.dot(pheno_white_top, top_white, precision=highest)) / jnp.sqrt(jnp.float32(count))
    info_stat = (lax.optimization_barrier(jnp.sum(white_geno * white_geno, axis=0)) + lax.optimization_barrier(jnp.sum(top_white * top_white, axis=0))) / jnp.float32(count)
    return (updated_block, panel_factor, white_geno, score_stat, info_stat)
```

```python
import functools

import jax
import jax.numpy as jnp
from jax import lax
from jax.experimental import pallas as pl
from jax.experimental.pallas import tpu as pltpu
from jax.sharding import PartitionSpec as P

MESH = pl.DeviceIdType.MESH
HIGHEST = lax.Precision.HIGHEST
TILE = 16
PARTS = 4
BLOCK = 128


def split3(value):
    hi = value.astype(jnp.bfloat16).astype(jnp.float32)
    rest = value - hi
    mid = rest.astype(jnp.bfloat16).astype(jnp.float32)
    return hi, mid, rest - mid


def tile_step(m_ref, step):
    start = pl.multiple_of(step * TILE, TILE)
    left = m_ref[pl.ds(start, TILE), :BLOCK]
    right = m_ref[pl.ds(start, TILE), BLOCK:]
    rolled = pltpu.roll(left, lax.rem(BLOCK - start, BLOCK), 1)
    cols = [jnp.broadcast_to(rolled[:, k : k + 1], (TILE, BLOCK)) for k in range(TILE)]
    rows = lax.broadcasted_iota(jnp.int32, (TILE, BLOCK), 0)
    lanes = lax.broadcasted_iota(jnp.int32, (TILE, BLOCK), 1)
    pivots = jnp.zeros_like(left)
    for j in range(TILE):
        pivot = jnp.broadcast_to(cols[j][j : j + 1, :], (TILE, BLOCK))
        inv = pl.reciprocal(pivot, approx=True)
        inv = inv * (2.0 - pivot * inv)
        below = jnp.where(rows > j, cols[j], 0.0)
        pivots = jnp.where(rows == j, pivot, pivots)

        def work(value):
            return value - below * (jnp.broadcast_to(value[j : j + 1, :], (TILE, BLOCK)) * inv)

        for k in range(j + 1, TILE):
            cols[k] = work(cols[k])
        left, right = work(left), work(right)
    scale = lax.rsqrt(pivots)
    scale = scale * (1.5 - (0.5 * pivots) * scale * scale)
    left, right = left * scale, right * scale
    m_ref[pl.ds(start, TILE), :BLOCK] = left
    m_ref[pl.ds(start, TILE), BLOCK:] = right
    both = jnp.concatenate([left, right], axis=1)
    mult = jnp.where(lanes >= start + TILE, left, 0.0)
    a0, a1, a2 = split3(mult)
    b0, b1, b2 = split3(both)
    lhs = jnp.concatenate([a0, a0, a1, a0, a1, a2], axis=0).astype(jnp.bfloat16)
    rhs = jnp.concatenate([b0, b1, b0, b2, b1, b0], axis=0).astype(jnp.bfloat16)
    m_ref[...] -= lax.dot_general(
        lhs, rhs, (((0,), (0,)), ((), ())), preferred_element_type=jnp.float32
    )


def dot_t(a, b):
    return lax.dot_general(
        a, b, (((0,), (0,)), ((), ())), precision=HIGHEST, preferred_element_type=jnp.float32
    )


def dot_n(a, b):
    return jnp.dot(a, b, precision=HIGHEST, preferred_element_type=jnp.float32)


def invert(a_ref, w_ref, m_ref, events):
    width = a_ref.shape[0]
    blocks = width // BLOCK
    tiles = BLOCK // TILE
    w_ref[...] = jnp.zeros_like(w_ref)
    eye = (
        lax.broadcasted_iota(jnp.int32, (BLOCK, BLOCK), 0)
        == lax.broadcasted_iota(jnp.int32, (BLOCK, BLOCK), 1)
    ).astype(jnp.float32)
    slot = 0
    for k in range(blocks):
        lo, hi = k * BLOCK, (k + 1) * BLOCK
        m_ref[:, :BLOCK] = a_ref[lo:hi, lo:hi]
        m_ref[:, BLOCK:] = eye
        for part in range(PARTS):

            def body(step, carry):
                tile_step(m_ref, step)
                return carry

            lax.fori_loop(part * tiles // PARTS, (part + 1) * tiles // PARTS, body, 0)
            if part < PARTS - 1:
                if slot < len(events):
                    events[slot]()
                slot += 1
        own = m_ref[:, BLOCK:]
        if k > 0:
            w_ref[lo:hi, :lo] = dot_n(own, w_ref[lo:hi, :lo])
        w_ref[lo:hi, lo:hi] = own
        if k < blocks - 1:
            upper = dot_n(own, a_ref[lo:hi, hi:])
            a_ref[hi:, hi:] -= dot_t(upper, upper)
            w_ref[hi:, :hi] -= dot_t(upper, w_ref[lo:hi, :hi])
        if slot < len(events):
            events[slot]()
        slot += 1
    while slot < len(events):
        events[slot]()
        slot += 1


LAST = ((1,), (1,))
INNER = ((1,), (0,))


def split2(value):
    hi = value.astype(jnp.bfloat16)
    return hi, (value - hi.astype(jnp.float32)).astype(jnp.bfloat16)


def dot3(a, b, dims):
    left = jnp.concatenate([a[0], a[0], a[1]], axis=dims[0][0])
    right = jnp.concatenate([b[0], b[1], b[0]], axis=dims[1][0])
    return lax.dot_general(left, right, (dims, ((), ())), preferred_element_type=jnp.float32)


def column(row):
    return jnp.transpose(jnp.broadcast_to(row, (BLOCK, row.shape[1])))


def weighted(weights, values):
    wide = jnp.concatenate([weights] * (values.shape[1] // BLOCK), axis=1)
    return jnp.sum(wide * values, axis=0, keepdims=True)


def main_kernel(
    ly, lz, group,
    diag_in, top_in, pheno_in, panel_in, trailing_in, geno_in, rest_in,
    u_out, white_out, own_out, total_out,
    a_ref, m_ref, w_ref, row_buf, col_buf, top_buf, pheno_buf, rest_buf,
    row_hi, row_lo, y_hi, y_lo, g_hi, g_lo, w_hi, w_lo, wt_hi, wt_lo, ai_hi, ai_lo,
    stat, stat_buf,
    small_send, small_recv, row_send, row_recv, col_send, col_recv, stat_send, stat_recv, local_sem,
):
    r, c = lax.axis_index("prow"), lax.axis_index("pcol")
    z, y = c // ly, lax.rem(c, ly)
    sib = r + 1 - 2 * lax.rem(r, 2)
    cross = r + 2 - 4 * (r // 2)
    diag_x = sib + 2 - 4 * (sib // 2)
    other = z * ly + (1 - y)
    rows_piece, width = panel_in.shape
    half = rows_piece // 2
    pieces = row_buf.shape[0] // rows_piece
    variants = top_in.shape[1]
    col_parts = col_buf.shape[0] // rows_piece
    root = c // group
    first = lax.rem(c, group) * col_parts
    is_root = root == r
    root_cross = root + 2 - 4 * (root // 2)
    low_end, high_end = z == 0, z == lz - 1

    barrier = pltpu.get_barrier_semaphore()

    def greet(row, col):
        pl.semaphore_signal(barrier, inc=1, device_id={"prow": row, "pcol": col}, device_id_type=MESH)

    greet(sib, c)
    greet(cross, c)
    greet(diag_x, c)
    greet(r, other)

    @pl.when(z > 0)
    def _():
        greet(r, c - ly)

    @pl.when(z < lz - 1)
    def _():
        greet(r, c + ly)

    pl.semaphore_wait(barrier, 4 + jnp.minimum(z, 1) + jnp.minimum(lz - 1 - z, 1))

    def remote(src, dst, send, recv, row, col):
        return pltpu.make_async_remote_copy(
            src_ref=src, dst_ref=dst, send_sem=send, recv_sem=recv,
            device_id={"prow": row, "pcol": col}, device_id_type=MESH,
        )

    def each(items, act):
        for item in items:
            if item[0] is True:
                act(item)
            elif item[0] is not False:
                pl.when(item[0])(functools.partial(act, item))

    def start_all(sends):
        each(sends, lambda item: item[1]().start())

    def sent_all(sends):
        each(sends, lambda item: item[1]().wait_send())

    height = diag_in.shape[0]
    side = 2 * height
    mine, theirs = (r // 2) * side, (cross // 2) * side

    def band(q):
        return pl.ds(pl.multiple_of(q * height, height), height)

    def small(kind, lane):
        part = cross if lane == 2 else r
        if kind == 0:
            if lane == 0:
                src, dst = diag_in, a_ref.at[band(r), :]
            else:
                cols = pl.ds(pl.multiple_of(theirs if lane == 2 else mine, side), side)
                dst = a_ref.at[band(part), cols]
                src = dst if lane == 2 else diag_in.at[:, cols]
        else:
            buf = (None, top_buf, pheno_buf)[kind]
            dst = buf.at[part]
            src = dst if lane == 2 else (None, top_in, pheno_in)[kind]
        return remote(
            src, dst, small_send.at[kind, lane], small_recv.at[kind, part],
            cross if lane == 1 else sib, c,
        )

    def small_wait(kind, part):
        if kind == 0:
            dst = a_ref.at[band(part), :]
            if part is not sib:
                dst = a_ref.at[band(part), pl.ds(pl.multiple_of(theirs, side), side)]
        else:
            dst = (None, top_buf, pheno_buf)[kind].at[part]
        remote(dst, dst, small_send.at[kind, 0], small_recv.at[kind, part], sib, c).wait_recv()

    def chunk(b, h):
        return row_buf.at[pl.ds(pl.multiple_of((2 * b + h) * half, half), half), :]

    def own_half(h):
        return panel_in.at[pl.ds(h * half, half), :]

    def row_copy(way, b, h, own=False):
        target = (c + ly, c - ly, other)[way]
        return lambda: remote(
            own_half(h) if own else chunk(b, h), chunk(b, h),
            row_send.at[way, 2 * b + h], row_recv.at[2 * b + h], r, target,
        )

    def row_wait(b, h):
        remote(chunk(b, h), chunk(b, h), row_send.at[0, 0], row_recv.at[2 * b + h], r, other).wait_recv()

    def col_at(i, h):
        return col_buf.at[pl.ds(pl.multiple_of((2 * i + h) * half, half), half), :]

    def col_copies(b, h, own):
        i = b - first
        src = own_half(h) if own else chunk(b, h)
        k = 2 * i + h
        return (
            remote(src, col_at(i, h), col_send.at[0, k], col_recv.at[k], cross, c),
            remote(src, col_at(i, h), col_send.at[1, k], col_recv.at[k], sib, c),
            pltpu.make_async_copy(src, col_at(i, h), local_sem.at[k]),
        )

    def col_start(b, h, own=False):
        @pl.when(is_root & (b >= first) & (b < first + col_parts))
        def _():
            for copy in col_copies(b, h, own):
                copy.start()

    def own_sends(h):
        return [
            (True, row_copy(2, c, h, True)),
            (z < lz - 1, row_copy(0, c, h, True)),
            (z > 0, row_copy(1, c, h, True)),
        ]

    def hop_arrivals(d, h):
        low, high = c - d * ly, c + d * ly
        return [
            (z >= d, low, h, [
                (z < lz - 1, row_copy(0, low, h)),
                (True if h == 0 else z != d, row_copy(2, low, h)),
            ]),
            (z + d < lz, high, h, [
                (z > 0, row_copy(1, high, h)),
                (True if h == 0 else z + d != lz - 1, row_copy(2, high, h)),
            ]),
        ]

    def across_arrivals(d, h):
        if d == 0:
            sends = []
            if h == 1 and lz > 1:
                sends = [(low_end, row_copy(0, other, h)), (high_end, row_copy(1, other, h))]
            return [(True, other, h, sends)]
        return [
            (z >= d if h == 0 else z > d, other - d * ly, h, []),
            (z + d < lz if h == 0 else z + d < lz - 1, other + d * ly, h, []),
        ]

    def far_arrivals(d):
        low, high = 1 - y, (lz - 1) * ly + 1 - y
        return [
            (z == d, low, 1, [(z < lz - 1, row_copy(0, low, 1))]),
            (z == lz - 1 - d, high, 1, [(z > 0, row_copy(1, high, 1))]),
        ]

    def arrive(items):
        def act(item):
            _, b, h, sends = item
            row_wait(b, h)
            start_all(sends)
            col_start(b, h)

        each(items, act)

    def finish(items):
        each(items, lambda item: sent_all(item[3]))

    small(0, 0).start()
    small(0, 1).start()
    diag_copy = pltpu.make_async_copy(diag_in, a_ref.at[band(r), :], local_sem.at[2 * col_parts])
    diag_copy.start()
    for h in range(2):
        start_all(own_sends(h))
    for kind in (1, 2):
        small(kind, 1).start()
        small(kind, 0).start()
    own_copies = [
        pltpu.make_async_copy(own_half(h), chunk(c, h), local_sem.at[2 * col_parts + 1 + h]) for h in range(2)
    ]
    others = [
        pltpu.make_async_copy(src, dst, local_sem.at[2 * col_parts + 3 + k])
        for k, (src, dst) in enumerate((
            (top_in, top_buf.at[r]), (pheno_in, pheno_buf.at[r]), (rest_in, rest_buf),
            (geno_in, white_out), (trailing_in, u_out),
        ))
    ]
    for copy in own_copies + others:
        copy.start()
    for h in range(2):
        col_start(c, h, True)
    small_wait(0, cross)
    small(0, 2).start()
    small_wait(0, sib)
    small_wait(0, diag_x)
    diag_copy.wait()
    small(0, 2).wait_send()

    @pl.when(r >= 2)
    def _():
        a_ref[:side, side:] = jnp.transpose(a_ref[side:, :side])

    def top_event():
        for kind in (1, 2):
            small_wait(kind, cross)
            small(kind, 2).start()

    def nothing():
        pass

    last = 2 * (lz - 1)

    def event(t):
        def run():
            if t <= last:
                arrive(hop_arrivals((t + 1) // 2, (t - 1) % 2))
            if t % 2 == 1 and t // 2 >= 1:
                arrive(far_arrivals(t // 2))
            if t == 2:
                arrive(across_arrivals(0, 0))
                arrive(across_arrivals(0, 1))
            if t >= 4 and (t - 2) // 2 < lz:
                arrive(across_arrivals((t - 2) // 2, t % 2))

        return run

    count = 2 * lz
    events = [nothing] * 16
    events[2], events[3], events[6] = event(1), top_event, event(2)
    events[10], events[14] = event(3), event(4)
    invert(a_ref, w_ref, m_ref, events)

    def prepare():
        for kind in (1, 2):
            small_wait(kind, sib)
            small_wait(kind, diag_x)
        for copy in own_copies + others:
            copy.wait()
        whole = w_ref[...]
        w_hi[...], w_lo[...] = split2(whole)
        wt_hi[...], wt_lo[...] = split2(jnp.transpose(whole))
        w, turned = (w_hi[...], w_lo[...]), (wt_hi[...], wt_lo[...])
        ai_hi[...], ai_lo[...] = split2(dot3(turned, w, INNER))
        phenos = jnp.concatenate([pheno_buf[q] for q in range(pheno_buf.shape[0])], axis=1)
        joined = jnp.concatenate([top_buf[...].reshape(width, variants), column(phenos)], axis=1)
        both = dot3(w, split2(joined), INNER)
        g_hi[...], g_lo[...] = split2(dot3(turned, split2(both), INNER))
        white = both[:, :variants]
        stat[...] = jnp.zeros_like(stat)
        stat[2:3, :] = weighted(both[:, variants:], white)
        stat[3:4, :] = jnp.sum(white * white, axis=0, keepdims=True)
        at = pl.ds(pl.multiple_of(c * rows_piece, rows_piece), rows_piece)
        own_out[...] = dot3(split2(row_buf[at, :]), (wt_hi[...], wt_lo[...]), INNER)

    unit = rest_buf.shape[2]
    units = row_buf.shape[0] // unit
    col_unit = min(col_parts, max(1, 256 // rows_piece))
    col_units = col_parts // col_unit
    col_wide = col_unit * rows_piece

    def place(b):
        return pl.ds(pl.multiple_of(b * unit, unit), unit)

    def row_step(b):
        at = place(b)
        parts = split2(row_buf[at, :])
        row_hi[at, :], row_lo[at, :] = parts
        shift = dot3(parts, (g_hi[...], g_lo[...]), INNER)
        white = white_out[at, :] - shift[:, :variants]
        white_out[at, :] = white
        stat[0:1, :] += weighted(column(rest_buf[b]) - shift[:, variants:], white)
        stat[1:2, :] += jnp.sum(white * white, axis=0, keepdims=True)

    def cols_of(q):
        return pl.ds(pl.multiple_of(q * col_wide, col_wide), col_wide)

    def block(b, q):
        at, cols = place(b), cols_of(q)
        u_out[at, cols] -= dot3((row_hi[at, :], row_lo[at, :]), (y_hi[:, cols], y_lo[:, cols]), INNER)

    def col_ready(i, h):
        @pl.when(is_root)
        def _():
            pltpu.make_async_copy(col_at(i, h), col_at(i, h), local_sem.at[2 * i + h]).wait()

        @pl.when(jnp.logical_not(is_root))
        def _():
            handed = remote(col_at(i, h), col_at(i, h), col_send.at[1, 2 * i + h], col_recv.at[2 * i + h], sib, c)
            handed.wait_recv()
            pl.when(r == root_cross)(handed.start)

    def col_step(q):
        for i in range(col_unit):
            for h in range(2):
                col_ready(q * col_unit + i, h)
        cols = cols_of(q)
        y_hi[:, cols], y_lo[:, cols] = split2(
            dot3((ai_hi[...], ai_lo[...]), split2(col_buf[cols, :]), LAST)
        )

    def over(lo, hi, fn):
        def body(k, carry):
            fn(k)
            return carry

        lax.fori_loop(lo, hi, body, 0)

    def nearest(k):
        near = jnp.minimum(z, lz - 1 - z)
        step = (k + 1) // 2
        zigzag = z + jnp.where(lax.rem(k, 2) == 1, step, -step)
        onward = jnp.where(z < lz - 1 - z, k, lz - 1 - k)
        return jnp.where(k <= 2 * near, zigzag, onward)

    def send_stats():
        stat_buf[r] = stat[...]
        for k, target in enumerate((sib, cross, diag_x)):
            remote(stat, stat_buf.at[r], stat_send.at[k], stat_recv.at[r], target, c).start()

    if lz == 4 and unit == rows_piece and col_units == 4:
        flip = (first // ly + 1 <= z)

        def row_at(k):
            own = nearest(k) * ly + y
            return own

        def col_order(q):
            zi = jnp.where(flip, 1 - q % 2, q % 2)
            yi = y if q // 2 == 0 else 1 - y
            return zi * ly + yi

        rows = [(0, 0), (0, 1), (1, 0), (2, 0), (1, 1), (3, 0), (2, 1), (3, 1)]

        def row_id(s):
            k, side_y = rows[s]
            return nearest(jnp.int32(k)) * ly + (y if side_y == 0 else 1 - y)

        def pick(values, k):
            out = values[-1]
            for j in range(len(values) - 2, -1, -1):
                out = jnp.where(k == j, values[j], out)
            return out

        row_ids = [row_id(s) for s in range(8)]
        col_ids = [col_order(q) for q in range(4)]

        def do_rows(lo, hi, done):
            def one(s):
                b = pick(row_ids, s)
                row_step(b)
                if done:
                    over(0, done, lambda q: block(b, pick(col_ids, q)))

            over(lo, hi, one)

        def do_col(q, done):
            col_step(col_ids[q])
            over(0, done, lambda s: block(pick(row_ids, s), col_ids[q]))

        prepare()
        event(5)()
        do_rows(0, 4, 0)
        do_col(0, 4)
        event(6)()
        do_rows(4, 6, 1)
        do_col(1, 6)
        arrive(across_arrivals(2, 1))
        do_rows(6, 7, 2)
        do_col(2, 7)
        arrive(far_arrivals(3))
        arrive(across_arrivals(3, 0))
        arrive(across_arrivals(3, 1))
        row_step(row_ids[7])
        send_stats()
        over(0, 3, lambda q: block(row_ids[7], pick(col_ids, q)))
        do_col(3, 8)
    else:
        for t in range(5, count + 2):
            event(t)()
        prepare()
        over(0, col_units, col_step)
        over(0, units, row_step)
        send_stats()
        over(0, units, lambda b: over(0, col_units, lambda q: block(b, q)))

    for k, source in enumerate((sib, cross, diag_x)):
        remote(stat, stat_buf.at[source], stat_send.at[k], stat_recv.at[source], sib, c).wait_recv()
    total = stat_buf[0]
    for q in range(1, stat_buf.shape[0]):
        total = total + stat_buf[q]
    people = jnp.float32(width + row_buf.shape[0] * stat_buf.shape[0])
    total_out[...] = jnp.zeros_like(total_out)
    total_out[0:1, :] = (total[0:1] + stat[2:3, :]) / jnp.sqrt(people)
    total_out[1:2, :] = (total[1:2] + stat[3:4, :]) / people

    for k in range(3):
        remote(stat, stat_buf.at[r], stat_send.at[k], stat_recv.at[r], sib, c).wait_send()
    small(0, 1).wait_send()
    small(0, 0).wait_send()
    for kind in (1, 2):
        for lane in range(3):
            small(kind, lane).wait_send()
    for h in range(2):
        sent_all(own_sends(h))
    finish(across_arrivals(0, 1))
    for d in range(1, lz):
        for h in range(2):
            finish(hop_arrivals(d, h))
        finish(far_arrivals(d))

    @pl.when(is_root)
    def _():
        def body(k, carry):
            for lane in range(2):
                remote(
                    col_at(k, 0), col_at(k, 0), col_send.at[lane, 2 * k], col_recv.at[0], sib, c
                ).wait_send()
                remote(
                    col_at(k, 1), col_at(k, 1), col_send.at[lane, 2 * k + 1], col_recv.at[0], sib, c
                ).wait_send()
            return carry

        lax.fori_loop(0, col_parts, body, 0)

    @pl.when(r == root_cross)
    def _():
        def body(k, carry):
            for h in range(2):
                remote(
                    col_at(k, h), col_at(k, h), col_send.at[1, 2 * k + h], col_recv.at[0], sib, c
                ).wait_send()
            return carry

        lax.fori_loop(0, col_parts, body, 0)


def store_kernel(u_in, white_in, own_in, total_in, u_out, white_out, own_out, score_out, info_out, sem):
    pairs = [(own_in, own_out), (white_in, white_out), (u_in, u_out)]
    pairs += [(total_in.at[0:1], score_out), (total_in.at[1:2], info_out)]
    copies = [pltpu.make_async_copy(src, dst, sem.at[k]) for k, (src, dst) in enumerate(pairs)]
    for copy in copies:
        copy.start()
    for copy in copies:
        copy.wait()


def local(diag_block, panel_cols, trailing, geno_top, geno_rest, pheno_top, pheno_rest):
    prow_size, pcol_size = lax.axis_size("prow"), lax.axis_size("pcol")
    height, width = diag_block.shape
    rows_piece = panel_cols.shape[0]
    row_count, col_count = trailing.shape
    variants = geno_top.shape[1]
    ly = 2
    lz = pcol_size // ly
    unit = min(row_count, max(rows_piece, 256))
    chunks, col_chunks = 2 * pcol_size, 2 * (col_count // rows_piece)
    f32, bf16 = jnp.float32, jnp.bfloat16
    vmem = pl.BlockSpec(memory_space=pltpu.VMEM)
    hbm = pl.BlockSpec(memory_space=pltpu.HBM)
    dma = pltpu.SemaphoreType.DMA
    wide = variants + BLOCK
    stats = (8, variants)
    arrays = [
        ((width, width), f32), ((BLOCK, 2 * BLOCK), f32), ((width, width), f32),
        ((row_count, width), f32), ((col_count, width), f32),
        ((prow_size, height, variants), f32), ((prow_size, 1, height), f32),
        ((row_count // unit, 1, unit), f32),
        ((row_count, width), bf16), ((row_count, width), bf16),
        ((width, col_count), bf16), ((width, col_count), bf16),
        ((width, wide), bf16), ((width, wide), bf16),
    ]
    arrays += [((width, width), bf16)] * 6
    arrays += [(stats, f32), ((prow_size,) + stats, f32)]
    held = pl.pallas_call(
        functools.partial(main_kernel, ly, lz, pcol_size // prow_size),
        out_shape=(
            pltpu.VMEM(trailing.shape, f32),
            pltpu.VMEM(geno_rest.shape, f32),
            pltpu.VMEM(panel_cols.shape, f32),
            pltpu.VMEM(stats, f32),
        ),
        in_specs=[hbm] * 7,
        out_specs=(vmem,) * 4,
        scratch_shapes=[pltpu.VMEM(shape, dtype) for shape, dtype in arrays]
        + [
            dma((3, 3)), dma((3, prow_size)), dma((3, chunks)), dma((chunks,)),
            dma((2, col_chunks)), dma((col_chunks,)), dma((3,)), dma((prow_size,)), dma((col_chunks + 8,)),
        ],
        compiler_params=pltpu.CompilerParams(
            collective_id=0, has_side_effects=True, vmem_limit_bytes=32 * 1024 * 1024
        ),
    )(
        *(pltpu.with_memory_space_constraint(value, pltpu.HBM) for value in (
            diag_block, geno_top, pheno_top.reshape(1, height), panel_cols, trailing, geno_rest,
            pheno_rest.reshape(row_count // unit, 1, unit),
        ))
    )
    updated_block, own_factor, white_geno, score, info = order(pl.pallas_call(
        store_kernel,
        out_shape=(
            jax.ShapeDtypeStruct(trailing.shape, f32),
            jax.ShapeDtypeStruct(geno_rest.shape, f32),
            jax.ShapeDtypeStruct(panel_cols.shape, f32),
            jax.ShapeDtypeStruct((1, variants), f32),
            jax.ShapeDtypeStruct((1, variants), f32),
        ),
        in_specs=[vmem] * 4,
        out_specs=(hbm,) * 5,
        scratch_shapes=[dma((5,))],
        compiler_params=pltpu.CompilerParams(vmem_limit_bytes=1024 * 1024),
    )(*(pltpu.with_memory_space_constraint(value, pltpu.VMEM) for value in held)))
    return (updated_block, own_factor, white_geno, score.reshape(variants), info.reshape(variants))


def order(values):
    updated, white, own, score, info = values
    return updated, own, white, score, info


def solution(mesh):
    placed = (
        P("prow", None),
        P(("prow", "pcol"), None),
        P("prow", "pcol"),
        P("prow", "pcol"),
        P("prow", "pcol"),
        P("prow"),
        P("prow"),
    )
    return jax.shard_map(
        local,
        mesh=mesh,
        in_specs=placed,
        out_specs=(
            P("prow", "pcol"),
            P(("prow", "pcol"), None),
            P("prow", "pcol"),
            P("pcol"),
            P("pcol"),
        ),
        check_vma=False,
    )
```

```python
import functools

import jax
import jax.numpy as jnp
from jax import lax
from jax.experimental import pallas as pl
from jax.experimental.pallas import tpu as pltpu
from jax.sharding import PartitionSpec as P

MESH = pl.DeviceIdType.MESH
HIGHEST = lax.Precision.HIGHEST
TILE = 16
PARTS = 4
BLOCK = 128


def split3(value):
    hi = value.astype(jnp.bfloat16).astype(jnp.float32)
    rest = value - hi
    mid = rest.astype(jnp.bfloat16).astype(jnp.float32)
    return hi, mid, rest - mid


def tile_step(m_ref, step):
    start = pl.multiple_of(step * TILE, TILE)
    half = TILE // 2
    left = m_ref[pl.ds(start, TILE), :BLOCK]
    right = m_ref[pl.ds(start, TILE), BLOCK:]
    rolled = pltpu.roll(left, lax.rem(BLOCK - start, BLOCK), 1)
    rows = lax.broadcasted_iota(jnp.int32, (half, BLOCK), 0)
    lanes = lax.broadcasted_iota(jnp.int32, (TILE, BLOCK), 1)

    def halves(value):
        return [value[:half], value[half:]]

    def spread(parts, j):
        part, at = parts[j // half], j % half
        return jnp.broadcast_to(part[at : at + 1, :], (half, BLOCK))

    cols = [halves(jnp.broadcast_to(rolled[:, k : k + 1], (TILE, BLOCK))) for k in range(TILE)]
    values = [halves(left), halves(right)]
    pivots = [jnp.zeros((half, BLOCK), jnp.float32) for _ in range(2)]
    def inverse(value):
        inv = pl.reciprocal(value, approx=True)
        return inv * (2.0 - value * inv)

    for j in range(0, TILE, 2):
        own, low = j // half, j % half
        one, two = cols[j], cols[j + 1]
        p, b, c = spread(one, j), spread(one, j + 1), spread(two, j + 1)
        det = p * c - b * b
        inv_p, inv_det = inverse(p), inverse(det)
        ratio = b * inv_p
        pivots[own] = jnp.where(rows == low, p, jnp.where(rows == low + 1, det * inv_p, pivots[own]))
        lead, tail, after = {}, {}, [None, None]
        for part in range(own, 2):
            after[part] = two[part] - ratio * one[part]
            lead[part] = one[part] * inv_p
            tail[part] = (p * two[part] - b * one[part]) * inv_det
            if part == own:
                lead[part] = jnp.where(rows > low, lead[part], 0.0)
                tail[part] = jnp.where(rows > low + 1, tail[part], 0.0)
        for k in range(j + 2, TILE):
            top, under = spread(one, k), spread(after, k)
            for part in lead:
                if part >= k // half:
                    cols[k][part] = (cols[k][part] - lead[part] * top) - tail[part] * under
        for value in values:
            top = spread(value, j)
            under = spread(value, j + 1) - ratio * top
            for part in lead:
                value[part] = (value[part] - lead[part] * top) - tail[part] * under
    left, right = (jnp.concatenate(value, axis=0) for value in values)
    pivots = jnp.concatenate(pivots, axis=0)
    scale = lax.rsqrt(pivots)
    scale = scale * (1.5 - (0.5 * pivots) * scale * scale)
    left, right = left * scale, right * scale
    m_ref[pl.ds(start, TILE), :BLOCK] = left
    m_ref[pl.ds(start, TILE), BLOCK:] = right
    both = jnp.concatenate([left, right], axis=1)
    mult = jnp.where(lanes >= start + TILE, left, 0.0)
    a0, a1, a2 = split3(mult)
    b0, b1, b2 = split3(both)
    lhs = jnp.concatenate([a0, a0, a1, a0, a1, a2], axis=0).astype(jnp.bfloat16)
    rhs = jnp.concatenate([b0, b1, b0, b2, b1, b0], axis=0).astype(jnp.bfloat16)
    m_ref[...] -= lax.dot_general(
        lhs, rhs, (((0,), (0,)), ((), ())), preferred_element_type=jnp.float32
    )


def dot_t(a, b):
    return lax.dot_general(
        a, b, (((0,), (0,)), ((), ())), precision=HIGHEST, preferred_element_type=jnp.float32
    )


def dot_n(a, b):
    return jnp.dot(a, b, precision=HIGHEST, preferred_element_type=jnp.float32)


def invert(a_ref, w_ref, m_ref, events):
    width = a_ref.shape[0]
    blocks = width // BLOCK
    tiles = BLOCK // TILE
    w_ref[...] = jnp.zeros_like(w_ref)
    eye = (
        lax.broadcasted_iota(jnp.int32, (BLOCK, BLOCK), 0)
        == lax.broadcasted_iota(jnp.int32, (BLOCK, BLOCK), 1)
    ).astype(jnp.float32)
    slot = 0
    for k in range(blocks):
        lo, hi = k * BLOCK, (k + 1) * BLOCK
        m_ref[:, :BLOCK] = a_ref[lo:hi, lo:hi]
        m_ref[:, BLOCK:] = eye
        for part in range(PARTS):

            def body(step, carry):
                tile_step(m_ref, step)
                return carry

            lax.fori_loop(part * tiles // PARTS, (part + 1) * tiles // PARTS, body, 0)
            if part < PARTS - 1:
                if slot < len(events):
                    events[slot]()
                slot += 1
        own = m_ref[:, BLOCK:]
        if k > 0:
            w_ref[lo:hi, :lo] = dot_n(own, w_ref[lo:hi, :lo])
        w_ref[lo:hi, lo:hi] = own
        if k < blocks - 1:
            upper = dot_n(own, a_ref[lo:hi, hi:])
            a_ref[hi:, hi:] -= dot_t(upper, upper)
            w_ref[hi:, :hi] -= dot_t(upper, w_ref[lo:hi, :hi])
        if slot < len(events):
            events[slot]()
        slot += 1
    while slot < len(events):
        events[slot]()
        slot += 1


LAST = ((1,), (1,))
INNER = ((1,), (0,))


def split2(value):
    hi = value.astype(jnp.bfloat16)
    return hi, (value - hi.astype(jnp.float32)).astype(jnp.bfloat16)


def dot3(a, b, dims):
    left = jnp.concatenate([a[0], a[0], a[1]], axis=dims[0][0])
    right = jnp.concatenate([b[0], b[1], b[0]], axis=dims[1][0])
    return lax.dot_general(left, right, (dims, ((), ())), preferred_element_type=jnp.float32)


def column(row):
    return jnp.transpose(jnp.broadcast_to(row, (BLOCK, row.shape[1])))


def weighted(weights, values):
    wide = jnp.concatenate([weights] * (values.shape[1] // BLOCK), axis=1)
    return jnp.sum(wide * values, axis=0, keepdims=True)


def orders(ly, lz, first, z, y):
    low_end, high_end = z == 0, z == lz - 1
    far = (low_end & (y == 1)) | (high_end & (y == 0))

    def nearest(k):
        near = jnp.minimum(z, lz - 1 - z)
        step = (k + 1) // 2
        zigzag = z + (step if k % 2 == 1 else -step)
        onward = jnp.where(z < lz - 1 - z, k, lz - 1 - k)
        return jnp.where(k <= 2 * near, zigzag, onward)

    def row(k, turned):
        return nearest(k) * ly + (1 - y if turned else y)

    row_ids = [
        row(0, False), row(0, True), row(1, False), row(2, False),
        row(1, True), row(3, False), row(2, True), row(3, True),
    ]
    flip = first // ly + 1 <= z
    col_ids = [
        jnp.where(flip, 1 - q % 2, q % 2) * ly + (y if q // 2 == 0 else 1 - y) for q in range(4)
    ]
    return far, row_ids, col_ids


def pick(values, k):
    out = values[-1]
    for j in range(len(values) - 2, -1, -1):
        out = jnp.where(k == j, values[j], out)
    return out


def over(lo, hi, fn):
    def body(k, carry):
        fn(k)
        return carry

    lax.fori_loop(lo, hi, body, 0)


def is_tuned(lz, rows_piece, col_parts):
    return lz == 4 and rows_piece == 256 and col_parts == 4


def grid_copies(tuned, far_side, near_side, row_ids, col_ids, rows_piece, outward, sem):
    if not tuned:
        src, dst = (near_side, far_side) if outward else (far_side, near_side)
        pltpu.make_async_copy(src, dst, sem).start()
        return

    def one(k):
        i, j = k // 4, lax.rem(k, 4)

        def at(ref, row, col):
            return ref.at[
                pl.ds(pl.multiple_of(row * rows_piece, rows_piece), rows_piece),
                pl.ds(pl.multiple_of(col * rows_piece, rows_piece), rows_piece),
            ]

        here, there = at(near_side, i, j), at(far_side, pick(row_ids, i), pick(col_ids, j))
        src, dst = (here, there) if outward else (there, here)
        pltpu.make_async_copy(src, dst, sem).start()

    over(0, 32, one)


def main_kernel(
    ly, lz, group,
    diag_in, top_in, pheno_in, panel_in, trailing_in, geno_in, rest_in,
    u_out, white_out, own_out, total_out,
    a_ref, m_ref, w_ref, row_buf, col_buf, top_buf, pheno_buf, rest_buf,
    row_hi, row_lo, y_hi, y_lo, g_hi, g_lo, w_hi, w_lo, wt_hi, wt_lo, ai_hi, ai_lo,
    stat, stat_buf,
    small_send, small_recv, row_send, row_recv, col_send, col_recv, stat_send, stat_recv, local_sem,
):
    r, c = lax.axis_index("prow"), lax.axis_index("pcol")
    z, y = c // ly, lax.rem(c, ly)
    sib = r + 1 - 2 * lax.rem(r, 2)
    cross = r + 2 - 4 * (r // 2)
    diag_x = sib + 2 - 4 * (sib // 2)
    other = z * ly + (1 - y)
    rows_piece, width = panel_in.shape
    half = rows_piece // 2
    pieces = row_buf.shape[0] // rows_piece
    variants = top_in.shape[1]
    col_parts = col_buf.shape[0] // rows_piece
    root = c // group
    first = lax.rem(c, group) * col_parts
    is_root = root == r
    root_cross = root + 2 - 4 * (root // 2)
    low_end, high_end = z == 0, z == lz - 1
    tuned = is_tuned(lz, rows_piece, col_parts)
    far, row_ids, col_ids = orders(ly, lz, first, z, y) if tuned else (None, None, None)

    barrier = pltpu.get_barrier_semaphore()

    def greet(row, col):
        pl.semaphore_signal(barrier, inc=1, device_id={"prow": row, "pcol": col}, device_id_type=MESH)

    greet(sib, c)
    greet(cross, c)
    greet(diag_x, c)
    greet(r, other)

    @pl.when(z > 0)
    def _():
        greet(r, c - ly)

    @pl.when(z < lz - 1)
    def _():
        greet(r, c + ly)

    pl.semaphore_wait(barrier, 4 + jnp.minimum(z, 1) + jnp.minimum(lz - 1 - z, 1))

    def remote(src, dst, send, recv, row, col):
        return pltpu.make_async_remote_copy(
            src_ref=src, dst_ref=dst, send_sem=send, recv_sem=recv,
            device_id={"prow": row, "pcol": col}, device_id_type=MESH,
        )

    def each(items, act):
        for item in items:
            if item[0] is True:
                act(item)
            elif item[0] is not False:
                pl.when(item[0])(functools.partial(act, item))

    def start_all(sends):
        each(sends, lambda item: item[1]().start())

    def sent_all(sends):
        each(sends, lambda item: item[1]().wait_send())

    height = diag_in.shape[0]
    side = 2 * height
    mine, theirs = (r // 2) * side, (cross // 2) * side

    def band(q):
        return pl.ds(pl.multiple_of(q * height, height), height)

    def small(kind, lane):
        part = cross if lane == 2 else r
        if kind == 0:
            if lane == 0:
                src, dst = diag_in, a_ref.at[band(r), :]
            else:
                cols = pl.ds(pl.multiple_of(theirs if lane == 2 else mine, side), side)
                dst = a_ref.at[band(part), cols]
                src = dst if lane == 2 else diag_in.at[:, cols]
        else:
            buf = (None, top_buf, pheno_buf)[kind]
            dst = buf.at[part]
            src = dst if lane == 2 else (None, top_in, pheno_in)[kind]
        return remote(
            src, dst, small_send.at[kind, lane], small_recv.at[kind, part],
            cross if lane == 1 else sib, c,
        )

    def small_wait(kind, part):
        if kind == 0:
            dst = a_ref.at[band(part), :]
            if part is not sib:
                dst = a_ref.at[band(part), pl.ds(pl.multiple_of(theirs, side), side)]
        else:
            dst = (None, top_buf, pheno_buf)[kind].at[part]
        remote(dst, dst, small_send.at[kind, 0], small_recv.at[kind, part], sib, c).wait_recv()

    def chunk(b, h):
        return row_buf.at[pl.ds(pl.multiple_of((2 * b + h) * half, half), half), :]

    def own_half(h):
        return panel_in.at[pl.ds(h * half, half), :]

    def row_copy(way, b, h, own=False):
        target = (c + ly, c - ly, other)[way]
        return lambda: remote(
            own_half(h) if own else chunk(b, h), chunk(b, h),
            row_send.at[way, 2 * b + h], row_recv.at[2 * b + h], r, target,
        )

    def row_wait(b, h):
        remote(chunk(b, h), chunk(b, h), row_send.at[0, 0], row_recv.at[2 * b + h], r, other).wait_recv()

    def col_at(i, h):
        return col_buf.at[pl.ds(pl.multiple_of((2 * i + h) * half, half), half), :]

    def col_copies(b, h, own):
        i = b - first
        src = own_half(h) if own else chunk(b, h)
        k = 2 * i + h
        return (
            remote(src, col_at(i, h), col_send.at[0, k], col_recv.at[k], cross, c),
            remote(src, col_at(i, h), col_send.at[1, k], col_recv.at[k], sib, c),
            pltpu.make_async_copy(src, col_at(i, h), local_sem.at[k]),
        )

    def col_start(b, h, own=False):
        @pl.when(is_root & (b >= first) & (b < first + col_parts))
        def _():
            for copy in col_copies(b, h, own):
                copy.start()

    def own_sends(h):
        return [
            (True, row_copy(2, c, h, True)),
            (z < lz - 1, row_copy(0, c, h, True)),
            (z > 0, row_copy(1, c, h, True)),
        ]

    def hop_arrivals(d, h):
        low, high = c - d * ly, c + d * ly
        low_over = True if h == 0 else z != d
        high_over = True if h == 0 else z + d != lz - 1
        return [
            (z >= d, low, h, [(z < lz - 1, row_copy(0, low, h)), (low_over, row_copy(2, low, h))]),
            (z + d < lz, high, h, [(z > 0, row_copy(1, high, h)), (high_over, row_copy(2, high, h))]),
        ]

    def across_arrivals(d, h):
        if d == 0:
            sends = []
            if h == 1 and lz > 1:
                sends = [(low_end, row_copy(0, other, h)), (high_end, row_copy(1, other, h))]
            return [(True, other, h, sends)]
        return [
            (z >= d if h == 0 else z > d, other - d * ly, h, []),
            (z + d < lz if h == 0 else z + d < lz - 1, other + d * ly, h, []),
        ]

    def far_arrivals(d):
        low, high = 1 - y, (lz - 1) * ly + 1 - y
        return [
            (z == d, low, 1, [(z < lz - 1, row_copy(0, low, 1))]),
            (z == lz - 1 - d, high, 1, [(z > 0, row_copy(1, high, 1))]),
        ]

    def arrive(items):
        def act(item):
            _, b, h, sends = item
            row_wait(b, h)
            start_all(sends)
            col_start(b, h)

        each(items, act)

    def finish(items):
        each(items, lambda item: sent_all(item[3]))

    small(0, 0).start()
    small(0, 1).start()
    diag_copy = pltpu.make_async_copy(diag_in, a_ref.at[band(r), :], local_sem.at[2 * col_parts])
    diag_copy.start()
    for h in range(2):
        start_all(own_sends(h))
    for kind in (1, 2):
        small(kind, 1).start()
        small(kind, 0).start()
    own_copies = [
        pltpu.make_async_copy(own_half(h), chunk(c, h), local_sem.at[2 * col_parts + 1 + h]) for h in range(2)
    ]
    others = [
        pltpu.make_async_copy(src, dst, local_sem.at[2 * col_parts + 3 + k])
        for k, (src, dst) in enumerate((
            (top_in, top_buf.at[r]), (pheno_in, pheno_buf.at[r]), (rest_in, rest_buf),
            (geno_in, white_out),
        ))
    ]
    for copy in own_copies + others:
        copy.start()
    for h in range(2):
        col_start(c, h, True)
    trailing_sem = local_sem.at[2 * col_parts + 7]
    grid_copies(tuned, trailing_in, u_out, row_ids, col_ids, rows_piece, False, trailing_sem)
    others.append(pltpu.make_async_copy(trailing_in, u_out, trailing_sem))
    small_wait(0, cross)
    small(0, 2).start()
    small_wait(0, sib)
    small_wait(0, diag_x)
    diag_copy.wait()
    small(0, 2).wait_send()

    @pl.when(r >= 2)
    def _():
        a_ref[:side, side:] = jnp.transpose(a_ref[side:, :side])

    def top_event():
        for kind in (1, 2):
            small_wait(kind, cross)
            small(kind, 2).start()

    def nothing():
        pass

    last = 2 * (lz - 1)

    def event(t):
        def run():
            if t <= last:
                arrive(hop_arrivals((t + 1) // 2, (t - 1) % 2))
            if t % 2 == 1 and t // 2 >= 1:
                arrive(far_arrivals(t // 2))
            if t == 2:
                arrive(across_arrivals(0, 0))
                arrive(across_arrivals(0, 1))
            if t >= 4 and (t - 2) // 2 < lz:
                arrive(across_arrivals((t - 2) // 2, t % 2))

        return run

    count = 2 * lz
    events = [nothing] * 16
    events[2], events[3], events[6] = event(1), top_event, event(2)
    events[11], events[15] = event(3), event(4)
    invert(a_ref, w_ref, m_ref, events)

    def prepare():
        for kind in (1, 2):
            small_wait(kind, sib)
            small_wait(kind, diag_x)
        for copy in own_copies + others:
            copy.wait()
        whole = w_ref[...]
        w_hi[...], w_lo[...] = split2(whole)
        wt_hi[...], wt_lo[...] = split2(jnp.transpose(whole))
        w, turned = (w_hi[...], w_lo[...]), (wt_hi[...], wt_lo[...])
        ai_hi[...], ai_lo[...] = split2(dot3(turned, w, INNER))
        phenos = jnp.concatenate([pheno_buf[q] for q in range(pheno_buf.shape[0])], axis=1)
        joined = jnp.concatenate([top_buf[...].reshape(width, variants), column(phenos)], axis=1)
        both = dot3(w, split2(joined), INNER)
        g_hi[...], g_lo[...] = split2(dot3(turned, split2(both), INNER))
        white = both[:, :variants]
        stat[...] = jnp.zeros_like(stat)
        stat[2:3, :] = weighted(both[:, variants:], white)
        stat[3:4, :] = jnp.sum(white * white, axis=0, keepdims=True)
        at = pl.ds(pl.multiple_of(c * rows_piece, rows_piece), rows_piece)
        own_out[...] = dot3(split2(row_buf[at, :]), (wt_hi[...], wt_lo[...]), INNER)

    unit = rest_buf.shape[2]
    units = row_buf.shape[0] // unit
    col_unit = min(col_parts, max(1, 256 // rows_piece))
    col_units = col_parts // col_unit
    col_wide = col_unit * rows_piece

    def place(b):
        return pl.ds(pl.multiple_of(b * unit, unit), unit)

    def row_step(k, b):
        at, slot = place(b), place(k)
        parts = split2(row_buf[at, :])
        row_hi[slot, :], row_lo[slot, :] = parts
        shift = dot3(parts, (g_hi[...], g_lo[...]), INNER)
        white = white_out[at, :] - shift[:, :variants]
        white_out[at, :] = white
        stat[0:1, :] += weighted(column(rest_buf[b]) - shift[:, variants:], white)
        stat[1:2, :] += jnp.sum(white * white, axis=0, keepdims=True)

    def cols_of(q, count=1):
        return pl.ds(pl.multiple_of(q * col_wide, col_wide), col_wide * count)

    def product(k, many, q, count):
        slots = pl.ds(pl.multiple_of(k * unit, unit), unit * many)
        cols = cols_of(q, count)
        return dot3((row_hi[slots, :], row_lo[slots, :]), (y_hi[:, cols], y_lo[:, cols]), INNER)

    def col_ready(i, h):
        @pl.when(is_root)
        def _():
            pltpu.make_async_copy(col_at(i, h), col_at(i, h), local_sem.at[2 * i + h]).wait()

        @pl.when(jnp.logical_not(is_root))
        def _():
            handed = remote(col_at(i, h), col_at(i, h), col_send.at[1, 2 * i + h], col_recv.at[2 * i + h], sib, c)
            handed.wait_recv()
            pl.when(r == root_cross)(handed.start)

    def cols_ready(unit_at):
        for i in range(col_unit):
            for h in range(2):
                col_ready(unit_at * col_unit + i, h)

    def col_step(q, unit_at, waits=True):
        if waits:
            cols_ready(unit_at)
        y_hi[:, cols_of(q)], y_lo[:, cols_of(q)] = split2(
            dot3((ai_hi[...], ai_lo[...]), split2(col_buf[cols_of(unit_at), :]), LAST)
        )

    def send_stats():
        stat_buf[r] = stat[...]
        for k, target in enumerate((sib, cross, diag_x)):
            remote(stat, stat_buf.at[r], stat_send.at[k], stat_recv.at[r], target, c).start()

    if tuned:
        near = jnp.logical_not(far)

        def apply(k, many, q, count):
            u_out[pl.ds(pl.multiple_of(k * unit, unit), unit * many), cols_of(q, count)] -= product(k, many, q, count)

        def first_stage():
            arrive(across_arrivals(1, 1))
            arrive(hop_arrivals(3, 0))
            arrive(far_arrivals(2))

        def second_stage():
            arrive(across_arrivals(2, 0))
            arrive(hop_arrivals(3, 1))
            arrive(across_arrivals(2, 1))

        def stage(t):
            pl.when(t == 0)(first_stage)
            pl.when(t == 1)(second_stage)
            pl.when(t < 3)(lambda: row_step(4 + t, pick(row_ids, 4 + t)))

            @pl.when((t < 3) | near)
            def _():
                col_step(t, pick(col_ids, t))
                apply(0, 4, t, 1)

        def last_rows():
            arrive(far_arrivals(3))
            arrive(across_arrivals(3, 0))
            row_step(7, row_ids[7])
            send_stats()

        def rest(k):
            pl.when((k == 6) & far)(lambda: cols_ready(col_ids[3]))
            pl.when(near)(lambda: apply(k, 1, 0, 4))
            pl.when(far)(lambda: apply(k, 1, 0, 3))

        prepare()
        over(0, 4, lambda k: row_step(k, pick(row_ids, k)))
        over(0, 4, stage)
        last_rows()
        over(4, 8, rest)

        @pl.when(far)
        def _():
            col_step(3, col_ids[3], False)
            over(0, 2, lambda g: apply(4 * g, 4, 3, 1))
    else:
        for t in range(5, count + 2):
            event(t)()
        prepare()

        def apply(k):
            over(0, col_units, lambda q: apply_one(k, q))

        def apply_one(k, q):
            u_out[place(k), cols_of(q)] -= product(k, 1, q, 1)

        over(0, col_units, lambda q: col_step(q, q))
        over(0, units, lambda k: row_step(k, k))
        send_stats()
        over(0, units, apply)

    for k, source in enumerate((sib, cross, diag_x)):
        remote(stat, stat_buf.at[source], stat_send.at[k], stat_recv.at[source], sib, c).wait_recv()
    total = stat_buf[0]
    for q in range(1, stat_buf.shape[0]):
        total = total + stat_buf[q]
    people = jnp.float32(width + row_buf.shape[0] * stat_buf.shape[0])
    total_out[...] = jnp.zeros_like(total_out)
    total_out[0:1, :] = (total[0:1] + stat[2:3, :]) / jnp.sqrt(people)
    total_out[1:2, :] = (total[1:2] + stat[3:4, :]) / people

    for k in range(3):
        remote(stat, stat_buf.at[r], stat_send.at[k], stat_recv.at[r], sib, c).wait_send()
    small(0, 1).wait_send()
    small(0, 0).wait_send()
    for kind in (1, 2):
        for lane in range(3):
            small(kind, lane).wait_send()
    for h in range(2):
        sent_all(own_sends(h))
    finish(across_arrivals(0, 1))
    for d in range(1, lz):
        for h in range(2):
            finish(hop_arrivals(d, h))
        finish(far_arrivals(d))

    @pl.when(is_root)
    def _():
        def body(k, carry):
            for lane in range(2):
                remote(
                    col_at(k, 0), col_at(k, 0), col_send.at[lane, 2 * k], col_recv.at[0], sib, c
                ).wait_send()
                remote(
                    col_at(k, 1), col_at(k, 1), col_send.at[lane, 2 * k + 1], col_recv.at[0], sib, c
                ).wait_send()
            return carry

        lax.fori_loop(0, col_parts, body, 0)

    @pl.when(r == root_cross)
    def _():
        def body(k, carry):
            for h in range(2):
                remote(
                    col_at(k, h), col_at(k, h), col_send.at[1, 2 * k + h], col_recv.at[0], sib, c
                ).wait_send()
            return carry

        lax.fori_loop(0, col_parts, body, 0)


def store_kernel(ly, lz, group, u_in, white_in, own_in, total_in, u_out, white_out, own_out, score_out, info_out, sem):
    c = lax.axis_index("pcol")
    rows_piece = own_in.shape[0]
    col_parts = u_in.shape[1] // rows_piece
    tuned = is_tuned(lz, rows_piece, col_parts)
    row_ids, col_ids = None, None
    if tuned:
        _, row_ids, col_ids = orders(ly, lz, lax.rem(c, group) * col_parts, c // ly, lax.rem(c, ly))
    grid_copies(tuned, u_out, u_in, row_ids, col_ids, rows_piece, True, sem.at[0])
    pairs = [(own_in, own_out), (white_in, white_out)]
    pairs += [(total_in.at[0:1], score_out), (total_in.at[1:2], info_out)]
    copies = [pltpu.make_async_copy(src, dst, sem.at[1 + k]) for k, (src, dst) in enumerate(pairs)]
    for copy in copies:
        copy.start()
    for copy in copies:
        copy.wait()
    pltpu.make_async_copy(u_in, u_out, sem.at[0]).wait()


def local(diag_block, panel_cols, trailing, geno_top, geno_rest, pheno_top, pheno_rest):
    prow_size, pcol_size = lax.axis_size("prow"), lax.axis_size("pcol")
    height, width = diag_block.shape
    rows_piece = panel_cols.shape[0]
    row_count, col_count = trailing.shape
    variants = geno_top.shape[1]
    ly = 2
    lz = pcol_size // ly
    unit = min(row_count, max(rows_piece, 256))
    chunks, col_chunks = 2 * pcol_size, 2 * (col_count // rows_piece)
    f32, bf16 = jnp.float32, jnp.bfloat16
    vmem = pl.BlockSpec(memory_space=pltpu.VMEM)
    hbm = pl.BlockSpec(memory_space=pltpu.HBM)
    dma = pltpu.SemaphoreType.DMA
    wide = variants + BLOCK
    stats = (8, variants)
    arrays = [
        ((width, width), f32), ((BLOCK, 2 * BLOCK), f32), ((width, width), f32),
        ((row_count, width), f32), ((col_count, width), f32),
        ((prow_size, height, variants), f32), ((prow_size, 1, height), f32),
        ((row_count // unit, 1, unit), f32),
        ((row_count, width), bf16), ((row_count, width), bf16),
        ((width, col_count), bf16), ((width, col_count), bf16),
        ((width, wide), bf16), ((width, wide), bf16),
    ]
    arrays += [((width, width), bf16)] * 6
    arrays += [(stats, f32), ((prow_size,) + stats, f32)]
    held = pl.pallas_call(
        functools.partial(main_kernel, ly, lz, pcol_size // prow_size),
        out_shape=(
            pltpu.VMEM(trailing.shape, f32),
            pltpu.VMEM(geno_rest.shape, f32),
            pltpu.VMEM(panel_cols.shape, f32),
            pltpu.VMEM(stats, f32),
        ),
        in_specs=[hbm] * 7,
        out_specs=(vmem,) * 4,
        scratch_shapes=[pltpu.VMEM(shape, dtype) for shape, dtype in arrays]
        + [
            dma((3, 3)), dma((3, prow_size)), dma((3, chunks)), dma((chunks,)),
            dma((2, col_chunks)), dma((col_chunks,)), dma((3,)), dma((prow_size,)), dma((col_chunks + 9,)),
        ],
        compiler_params=pltpu.CompilerParams(
            collective_id=0, has_side_effects=True, vmem_limit_bytes=32 * 1024 * 1024
        ),
    )(
        *(pltpu.with_memory_space_constraint(value, pltpu.HBM) for value in (
            diag_block, geno_top, pheno_top.reshape(1, height), panel_cols, trailing, geno_rest,
            pheno_rest.reshape(row_count // unit, 1, unit),
        ))
    )
    updated_block, own_factor, white_geno, score, info = order(pl.pallas_call(
        functools.partial(store_kernel, ly, lz, pcol_size // prow_size),
        out_shape=(
            jax.ShapeDtypeStruct(trailing.shape, f32),
            jax.ShapeDtypeStruct(geno_rest.shape, f32),
            jax.ShapeDtypeStruct(panel_cols.shape, f32),
            jax.ShapeDtypeStruct((1, variants), f32),
            jax.ShapeDtypeStruct((1, variants), f32),
        ),
        in_specs=[vmem] * 4,
        out_specs=(hbm,) * 5,
        scratch_shapes=[dma((5,))],
        compiler_params=pltpu.CompilerParams(vmem_limit_bytes=1024 * 1024),
    )(*(pltpu.with_memory_space_constraint(value, pltpu.VMEM) for value in held)))
    return (updated_block, own_factor, white_geno, score.reshape(variants), info.reshape(variants))


def order(values):
    updated, white, own, score, info = values
    return updated, own, white, score, info


def solution(mesh):
    placed = (
        P("prow", None),
        P(("prow", "pcol"), None),
        P("prow", "pcol"),
        P("prow", "pcol"),
        P("prow", "pcol"),
        P("prow"),
        P("prow"),
    )
    return jax.shard_map(
        local,
        mesh=mesh,
        in_specs=placed,
        out_specs=(
            P("prow", "pcol"),
            P(("prow", "pcol"), None),
            P("prow", "pcol"),
            P("pcol"),
            P("pcol"),
        ),
        check_vma=False,
    )
```

```python
import functools

import jax
import jax.numpy as jnp
from jax import lax
from jax.experimental import pallas as pl
from jax.experimental.pallas import tpu as pltpu
from jax.sharding import PartitionSpec as P

MESH = pl.DeviceIdType.MESH
HIGHEST = lax.Precision.HIGHEST
TILE = 16
FINE = 4
PARTS = 4
BLOCK = 128


def split3(value):
    hi = value.astype(jnp.bfloat16).astype(jnp.float32)
    rest = value - hi
    mid = rest.astype(jnp.bfloat16).astype(jnp.float32)
    return hi, mid, rest - mid


def tile_step(m_ref, step):
    start = pl.multiple_of(step * TILE, TILE)
    half = TILE // 2
    left = m_ref[pl.ds(start, TILE), :BLOCK]
    right = m_ref[pl.ds(start, TILE), BLOCK:]
    rolled = pltpu.roll(left, lax.rem(BLOCK - start, BLOCK), 1)
    rows = lax.broadcasted_iota(jnp.int32, (half, BLOCK), 0)
    lanes = lax.broadcasted_iota(jnp.int32, (TILE, BLOCK), 1)

    def halves(value):
        return [value[:half], value[half:]]

    def spread(parts, j):
        part, at = parts[j // half], j % half
        return jnp.broadcast_to(part[at : at + 1, :], (half, BLOCK))

    cols = [halves(jnp.broadcast_to(rolled[:, k : k + 1], (TILE, BLOCK))) for k in range(TILE)]
    values = [halves(left), halves(right)]
    pivots = [jnp.zeros((half, BLOCK), jnp.float32) for _ in range(2)]
    def inverse(value):
        inv = pl.reciprocal(value, approx=True)
        return inv * (2.0 - value * inv)

    for j in range(0, TILE, 2):
        own, low = j // half, j % half
        one, two = cols[j], cols[j + 1]
        p, b, c = spread(one, j), spread(one, j + 1), spread(two, j + 1)
        det = p * c - b * b
        inv_p, inv_det = inverse(p), inverse(det)
        ratio = b * inv_p
        pivots[own] = jnp.where(rows == low, p, jnp.where(rows == low + 1, det * inv_p, pivots[own]))
        lead, tail, after = {}, {}, [None, None]
        for part in range(own, 2):
            after[part] = two[part] - ratio * one[part]
            lead[part] = one[part] * inv_p
            tail[part] = (p * two[part] - b * one[part]) * inv_det
            if part == own:
                lead[part] = jnp.where(rows > low, lead[part], 0.0)
                tail[part] = jnp.where(rows > low + 1, tail[part], 0.0)
        for k in range(j + 2, TILE):
            top, under = spread(one, k), spread(after, k)
            for part in lead:
                if part >= k // half:
                    cols[k][part] = (cols[k][part] - lead[part] * top) - tail[part] * under
        for value in values:
            top = spread(value, j)
            under = spread(value, j + 1) - ratio * top
            for part in lead:
                value[part] = (value[part] - lead[part] * top) - tail[part] * under
    left, right = (jnp.concatenate(value, axis=0) for value in values)
    pivots = jnp.concatenate(pivots, axis=0)
    scale = lax.rsqrt(pivots)
    scale = scale * (1.5 - (0.5 * pivots) * scale * scale)
    left, right = left * scale, right * scale
    m_ref[pl.ds(start, TILE), :BLOCK] = left
    m_ref[pl.ds(start, TILE), BLOCK:] = right
    both = jnp.concatenate([left, right], axis=1)
    mult = jnp.where(lanes >= start + TILE, left, 0.0)
    a0, a1, a2 = split3(mult)
    b0, b1, b2 = split3(both)
    lhs = jnp.concatenate([a0, a0, a1, a0, a1, a2], axis=0).astype(jnp.bfloat16)
    rhs = jnp.concatenate([b0, b1, b0, b2, b1, b0], axis=0).astype(jnp.bfloat16)
    m_ref[...] -= lax.dot_general(
        lhs, rhs, (((0,), (0,)), ((), ())), preferred_element_type=jnp.float32
    )


def dot_t(a, b):
    return lax.dot_general(
        a, b, (((0,), (0,)), ((), ())), precision=HIGHEST, preferred_element_type=jnp.float32
    )


def dot_n(a, b):
    return jnp.dot(a, b, precision=HIGHEST, preferred_element_type=jnp.float32)


def invert(a_ref, w_ref, m_ref, events):
    width = a_ref.shape[0]
    blocks = width // BLOCK
    tiles = BLOCK // TILE
    w_ref[...] = jnp.zeros_like(w_ref)
    eye = (
        lax.broadcasted_iota(jnp.int32, (BLOCK, BLOCK), 0)
        == lax.broadcasted_iota(jnp.int32, (BLOCK, BLOCK), 1)
    ).astype(jnp.float32)
    slot = 0
    for k in range(blocks):
        lo, hi = k * BLOCK, (k + 1) * BLOCK
        m_ref[:, :BLOCK] = a_ref[lo:hi, lo:hi]
        m_ref[:, BLOCK:] = eye
        for part in range(PARTS):

            def body(step, carry):
                tile_step(m_ref, step)
                return carry

            lax.fori_loop(part * tiles // PARTS, (part + 1) * tiles // PARTS, body, 0)
            if part < PARTS - 1:
                if slot < len(events):
                    events[slot]()
                slot += 1
        own = m_ref[:, BLOCK:]
        if k > 0:
            w_ref[lo:hi, :lo] = dot_n(own, w_ref[lo:hi, :lo])
        w_ref[lo:hi, lo:hi] = own
        if k < blocks - 1:
            upper = dot_n(own, a_ref[lo:hi, hi:])
            a_ref[hi:, hi:] -= dot_t(upper, upper)
            w_ref[hi:, :hi] -= dot_t(upper, w_ref[lo:hi, :hi])
        if slot < len(events):
            events[slot]()
        slot += 1
    while slot < len(events):
        events[slot]()
        slot += 1


LAST = ((1,), (1,))
INNER = ((1,), (0,))


def split2(value):
    hi = value.astype(jnp.bfloat16)
    return hi, (value - hi.astype(jnp.float32)).astype(jnp.bfloat16)


def dot3(a, b, dims):
    left = jnp.concatenate([a[0], a[0], a[1]], axis=dims[0][0])
    right = jnp.concatenate([b[0], b[1], b[0]], axis=dims[1][0])
    return lax.dot_general(left, right, (dims, ((), ())), preferred_element_type=jnp.float32)


def column(row):
    return jnp.transpose(jnp.broadcast_to(row, (BLOCK, row.shape[1])))


def weighted(weights, values):
    wide = jnp.concatenate([weights] * (values.shape[1] // BLOCK), axis=1)
    return jnp.sum(wide * values, axis=0, keepdims=True)


def orders(ly, lz, first, z, y):
    low_end, high_end = z == 0, z == lz - 1
    far = (low_end & (y == 1)) | (high_end & (y == 0))

    def nearest(k):
        near = jnp.minimum(z, lz - 1 - z)
        step = (k + 1) // 2
        zigzag = z + (step if k % 2 == 1 else -step)
        onward = jnp.where(z < lz - 1 - z, k, lz - 1 - k)
        return jnp.where(k <= 2 * near, zigzag, onward)

    def row(k, turned):
        return nearest(k) * ly + (1 - y if turned else y)

    row_ids = [
        row(0, False), row(0, True), row(1, False), row(2, False),
        row(1, True), row(3, False), row(2, True), row(3, True),
    ]
    flip = first // ly + 1 <= z
    col_ids = [
        jnp.where(flip, 1 - q % 2, q % 2) * ly + (y if q // 2 == 0 else 1 - y) for q in range(4)
    ]
    return far, row_ids, col_ids


def pick(values, k):
    out = values[-1]
    for j in range(len(values) - 2, -1, -1):
        out = jnp.where(k == j, values[j], out)
    return out


def over(lo, hi, fn):
    def body(k, carry):
        fn(k)
        return carry

    lax.fori_loop(lo, hi, body, 0)


def is_tuned(lz, rows_piece, col_parts):
    return lz == 4 and rows_piece == 256 and col_parts == 4


def grid_copies(tuned, far_side, near_side, row_ids, col_ids, rows_piece, outward, sem):
    if not tuned:
        src, dst = (near_side, far_side) if outward else (far_side, near_side)
        pltpu.make_async_copy(src, dst, sem).start()
        return

    def one(k):
        i, j = k // 4, lax.rem(k, 4)

        def at(ref, row, col):
            return ref.at[
                pl.ds(pl.multiple_of(row * rows_piece, rows_piece), rows_piece),
                pl.ds(pl.multiple_of(col * rows_piece, rows_piece), rows_piece),
            ]

        here, there = at(near_side, i, j), at(far_side, pick(row_ids, i), pick(col_ids, j))
        src, dst = (here, there) if outward else (there, here)
        pltpu.make_async_copy(src, dst, sem).start()

    over(0, 32, one)


def main_kernel(
    ly, lz, group,
    diag_in, top_in, pheno_in, panel_in, trailing_in, geno_in, rest_in,
    u_out, white_out, own_out, total_out,
    a_ref, m_ref, w_ref, row_buf, col_buf, top_buf, pheno_buf, rest_buf,
    row_hi, row_lo, y_hi, y_lo, g_hi, g_lo, w_hi, w_lo, wt_hi, wt_lo, ai_hi, ai_lo,
    stat, stat_buf,
    small_send, small_recv, row_send, row_recv, col_send, col_recv, stat_send, stat_recv, local_sem,
    fine_send, fine_recv, fine_col_send, fine_col_recv, fine_local,
):
    r, c = lax.axis_index("prow"), lax.axis_index("pcol")
    z, y = c // ly, lax.rem(c, ly)
    sib = r + 1 - 2 * lax.rem(r, 2)
    cross = r + 2 - 4 * (r // 2)
    diag_x = sib + 2 - 4 * (sib // 2)
    other = z * ly + (1 - y)
    rows_piece, width = panel_in.shape
    half = rows_piece // 2
    pieces = row_buf.shape[0] // rows_piece
    variants = top_in.shape[1]
    col_parts = col_buf.shape[0] // rows_piece
    root = c // group
    first = lax.rem(c, group) * col_parts
    is_root = root == r
    root_cross = root + 2 - 4 * (root // 2)
    low_end, high_end = z == 0, z == lz - 1
    tuned = is_tuned(lz, rows_piece, col_parts)
    far, row_ids, col_ids = orders(ly, lz, first, z, y) if tuned else (None, None, None)

    barrier = pltpu.get_barrier_semaphore()

    def greet(row, col):
        pl.semaphore_signal(barrier, inc=1, device_id={"prow": row, "pcol": col}, device_id_type=MESH)

    greet(sib, c)
    greet(cross, c)
    greet(diag_x, c)
    greet(r, other)

    @pl.when(z > 0)
    def _():
        greet(r, c - ly)

    @pl.when(z < lz - 1)
    def _():
        greet(r, c + ly)

    pl.semaphore_wait(barrier, 4 + jnp.minimum(z, 1) + jnp.minimum(lz - 1 - z, 1))

    def remote(src, dst, send, recv, row, col):
        return pltpu.make_async_remote_copy(
            src_ref=src, dst_ref=dst, send_sem=send, recv_sem=recv,
            device_id={"prow": row, "pcol": col}, device_id_type=MESH,
        )

    def each(items, act):
        for item in items:
            if item[0] is True:
                act(item)
            elif item[0] is not False:
                pl.when(item[0])(functools.partial(act, item))

    def start_all(sends):
        each(sends, lambda item: item[1]().start())

    def sent_all(sends):
        each(sends, lambda item: item[1]().wait_send())

    height = diag_in.shape[0]
    side = 2 * height
    mine, theirs = (r // 2) * side, (cross // 2) * side

    def band(q):
        return pl.ds(pl.multiple_of(q * height, height), height)

    def half_cols(start, kind):
        return pl.ds(pl.multiple_of(start + (height if kind == 3 else 0), height), height)

    def small(kind, lane):
        part = cross if lane == 2 else r
        if kind in (0, 3):
            if lane == 0:
                src, dst = diag_in, a_ref.at[band(r), :]
            else:
                cols = half_cols(theirs if lane == 2 else mine, kind)
                dst = a_ref.at[band(part), cols]
                src = dst if lane == 2 else diag_in.at[:, cols]
        else:
            buf = (None, top_buf, pheno_buf)[kind]
            dst = buf.at[part]
            src = dst if lane == 2 else (None, top_in, pheno_in)[kind]
        return remote(
            src, dst, small_send.at[kind, lane], small_recv.at[kind, part],
            cross if lane == 1 else sib, c,
        )

    def small_wait(kind, part):
        if kind in (0, 3):
            dst = a_ref.at[band(part), :]
            if part is not sib:
                dst = a_ref.at[band(part), half_cols(theirs, kind)]
        else:
            dst = (None, top_buf, pheno_buf)[kind].at[part]
        remote(dst, dst, small_send.at[kind, 0], small_recv.at[kind, part], sib, c).wait_recv()

    def chunk(b, h):
        return row_buf.at[pl.ds(pl.multiple_of((2 * b + h) * half, half), half), :]

    def own_half(h):
        return panel_in.at[pl.ds(h * half, half), :]

    def row_copy(way, b, h, own=False):
        target = (c + ly, c - ly, other)[way]
        return lambda: remote(
            own_half(h) if own else chunk(b, h), chunk(b, h),
            row_send.at[way, 2 * b + h], row_recv.at[2 * b + h], r, target,
        )

    def row_wait(b, h):
        remote(chunk(b, h), chunk(b, h), row_send.at[0, 0], row_recv.at[2 * b + h], r, other).wait_recv()

    def col_at(i, h):
        return col_buf.at[pl.ds(pl.multiple_of((2 * i + h) * half, half), half), :]

    def col_copies(b, h, own):
        i = b - first
        src = own_half(h) if own else chunk(b, h)
        k = 2 * i + h
        return (
            remote(src, col_at(i, h), col_send.at[0, k], col_recv.at[k], cross, c),
            remote(src, col_at(i, h), col_send.at[1, k], col_recv.at[k], sib, c),
            pltpu.make_async_copy(src, col_at(i, h), local_sem.at[k]),
        )

    def col_start(b, h, own=False):
        @pl.when(is_root & (b >= first) & (b < first + col_parts))
        def _():
            for copy in col_copies(b, h, own):
                copy.start()

    def part(ref, b, h, p):
        rows = half // FINE
        return ref.at[pl.ds(pl.multiple_of((2 * b + h) * half + p * rows, rows), rows), :]

    def fine_copies(way, b, h):
        target = (c + ly, c - ly, other)[way]

        def one(p):
            return lambda: remote(
                part(row_buf, b, h, p), part(row_buf, b, h, p), fine_send.at[h, p], fine_recv.at[h, p], r, target
            )

        return [one(p) for p in range(FINE)]

    last_piece = jnp.where(low_end, (lz - 1) * ly, 0) + 1 - y

    def fine_col(h, p):
        src, dst = part(row_buf, last_piece, h, p), part(col_buf, last_piece - first, h, p)
        return (
            remote(src, dst, fine_col_send.at[0, h, p], fine_col_recv.at[h, p], cross, c),
            remote(src, dst, fine_col_send.at[1, h, p], fine_col_recv.at[h, p], sib, c),
            pltpu.make_async_copy(src, dst, fine_local.at[h, p]),
        )

    def fine_handed(h, p):
        dst = part(col_buf, last_piece - first, h, p)
        return remote(dst, dst, fine_col_send.at[1, h, p], fine_col_recv.at[h, p], sib, c)

    def fine_arrive():
        for p in range(FINE):
            for h in (1, 0):
                dst = part(row_buf, last_piece, h, p)
                remote(dst, dst, fine_send.at[h, p], fine_recv.at[h, p], r, other).wait_recv()

                @pl.when(is_root & far)
                def _():
                    for copy in fine_col(h, p):
                        copy.start()

    def fine_hand():
        for p in range(FINE):
            for h in (1, 0):
                fine_handed(h, p).wait_recv()
                fine_handed(h, p).start()

    def fine_ready():
        for p in range(FINE):
            for h in (1, 0):

                @pl.when(is_root)
                def _():
                    fine_col(h, p)[2].wait()

                @pl.when(jnp.logical_not(is_root) & (r != root_cross))
                def _():
                    fine_handed(h, p).wait_recv()

    def fine_sent():
        for p in range(FINE):
            for h in (1, 0):

                @pl.when(is_root)
                def _():
                    for copy in fine_col(h, p)[:2]:
                        copy.wait_send()

                @pl.when(r == root_cross)
                def _():
                    fine_handed(h, p).wait_send()

    def own_sends(h):
        return [
            (True, row_copy(2, c, h, True)),
            (z < lz - 1, row_copy(0, c, h, True)),
            (z > 0, row_copy(1, c, h, True)),
        ]

    def hop_arrivals(d, h):
        low, high = c - d * ly, c + d * ly
        low_over = True if h == 0 else z != d
        high_over = True if h == 0 else z + d != lz - 1
        low_across, high_across = [(low_over, row_copy(2, low, h))], [(high_over, row_copy(2, high, h))]
        if tuned and d == lz - 1 and h == 0:
            low_across = [(True, copy) for copy in fine_copies(2, low, h)]
            high_across = [(True, copy) for copy in fine_copies(2, high, h)]
        return [
            (z >= d, low, h, [(z < lz - 1, row_copy(0, low, h))] + low_across),
            (z + d < lz, high, h, [(z > 0, row_copy(1, high, h))] + high_across),
        ]

    def across_arrivals(d, h):
        if d == 0:
            sends = []
            if h == 1 and lz > 1:
                sends = [(low_end, row_copy(0, other, h)), (high_end, row_copy(1, other, h))]
            return [(True, other, h, sends)]
        return [
            (z >= d if h == 0 else z > d, other - d * ly, h, []),
            (z + d < lz if h == 0 else z + d < lz - 1, other + d * ly, h, []),
        ]

    def far_arrivals(d):
        low, high = 1 - y, (lz - 1) * ly + 1 - y
        ups, downs = [row_copy(0, low, 1)], [row_copy(1, high, 1)]
        if tuned and d == lz - 2:
            ups, downs = fine_copies(0, low, 1), fine_copies(1, high, 1)
        return [
            (z == d, low, 1, [(z < lz - 1, copy) for copy in ups]),
            (z == lz - 1 - d, high, 1, [(z > 0, copy) for copy in downs]),
        ]

    def arrive(items):
        def act(item):
            _, b, h, sends = item
            row_wait(b, h)
            start_all(sends)
            col_start(b, h)

        each(items, act)

    def finish(items):
        each(items, lambda item: sent_all(item[3]))

    small(0, 1).start()
    small(0, 0).start()
    small(3, 1).start()
    diag_copy = pltpu.make_async_copy(diag_in, a_ref.at[band(r), :], local_sem.at[2 * col_parts])
    diag_copy.start()
    for h in range(2):
        start_all(own_sends(h))
    for kind in (1, 2):
        small(kind, 1).start()
        small(kind, 0).start()
    own_copies = [
        pltpu.make_async_copy(own_half(h), chunk(c, h), local_sem.at[2 * col_parts + 1 + h]) for h in range(2)
    ]
    others = [
        pltpu.make_async_copy(src, dst, local_sem.at[2 * col_parts + 3 + k])
        for k, (src, dst) in enumerate((
            (top_in, top_buf.at[r]), (pheno_in, pheno_buf.at[r]), (rest_in, rest_buf),
            (geno_in, white_out),
        ))
    ]
    for copy in own_copies + others:
        copy.start()
    for h in range(2):
        col_start(c, h, True)
    trailing_sem = local_sem.at[2 * col_parts + 7]
    grid_copies(tuned, trailing_in, u_out, row_ids, col_ids, rows_piece, False, trailing_sem)
    others.append(pltpu.make_async_copy(trailing_in, u_out, trailing_sem))
    small_wait(0, cross)
    small(0, 2).start()
    small_wait(0, sib)
    small_wait(0, diag_x)
    diag_copy.wait()

    def diag_event():
        small_wait(3, cross)
        small(3, 2).start()

    def corner_event():
        small_wait(3, diag_x)
        small(0, 2).wait_send()
        small(3, 2).wait_send()

        @pl.when(r >= 2)
        def _():
            a_ref[:side, side:] = jnp.transpose(a_ref[side:, :side])

    def top_event():
        for kind in (1, 2):
            small_wait(kind, cross)
            small(kind, 2).start()

    def nothing():
        pass

    last = 2 * (lz - 1)

    def event(t):
        def run():
            if t <= last:
                arrive(hop_arrivals((t + 1) // 2, (t - 1) % 2))
            if t % 2 == 1 and t // 2 >= 1:
                arrive(far_arrivals(t // 2))
            if t == 2:
                arrive(across_arrivals(0, 0))
                arrive(across_arrivals(0, 1))
            if t >= 4 and (t - 2) // 2 < lz:
                arrive(across_arrivals((t - 2) // 2, t % 2))

        return run

    count = 2 * lz
    events = [nothing] * 16
    events[0], events[2], events[3] = diag_event, corner_event, event(1)
    events[4], events[7] = top_event, event(2)
    events[11], events[15] = event(3), event(4)
    invert(a_ref, w_ref, m_ref, events)

    def prepare():
        for kind in (1, 2):
            small_wait(kind, sib)
            small_wait(kind, diag_x)
        for copy in own_copies + others:
            copy.wait()
        whole = w_ref[...]
        w_hi[...], w_lo[...] = split2(whole)
        wt_hi[...], wt_lo[...] = split2(jnp.transpose(whole))
        w, turned = (w_hi[...], w_lo[...]), (wt_hi[...], wt_lo[...])
        ai_hi[...], ai_lo[...] = split2(dot3(turned, w, INNER))
        phenos = jnp.concatenate([pheno_buf[q] for q in range(pheno_buf.shape[0])], axis=1)
        joined = jnp.concatenate([top_buf[...].reshape(width, variants), column(phenos)], axis=1)
        both = dot3(w, split2(joined), INNER)
        g_hi[...], g_lo[...] = split2(dot3(turned, split2(both), INNER))
        white = both[:, :variants]
        stat[...] = jnp.zeros_like(stat)
        stat[2:3, :] = weighted(both[:, variants:], white)
        stat[3:4, :] = jnp.sum(white * white, axis=0, keepdims=True)
        at = pl.ds(pl.multiple_of(c * rows_piece, rows_piece), rows_piece)
        own_out[...] = dot3(split2(row_buf[at, :]), (wt_hi[...], wt_lo[...]), INNER)

    unit = rest_buf.shape[2]
    units = row_buf.shape[0] // unit
    col_unit = min(col_parts, max(1, 256 // rows_piece))
    col_units = col_parts // col_unit
    col_wide = col_unit * rows_piece

    def place(b):
        return pl.ds(pl.multiple_of(b * unit, unit), unit)

    def row_step(k, b):
        at, slot = place(b), place(k)
        parts = split2(row_buf[at, :])
        row_hi[slot, :], row_lo[slot, :] = parts
        shift = dot3(parts, (g_hi[...], g_lo[...]), INNER)
        white = white_out[at, :] - shift[:, :variants]
        white_out[at, :] = white
        stat[0:1, :] += weighted(column(rest_buf[b]) - shift[:, variants:], white)
        stat[1:2, :] += jnp.sum(white * white, axis=0, keepdims=True)

    def cols_of(q, count=1):
        return pl.ds(pl.multiple_of(q * col_wide, col_wide), col_wide * count)

    def product(k, many, q, count):
        slots = pl.ds(pl.multiple_of(k * unit, unit), unit * many)
        cols = cols_of(q, count)
        return dot3((row_hi[slots, :], row_lo[slots, :]), (y_hi[:, cols], y_lo[:, cols]), INNER)

    def col_ready(i, h):
        @pl.when(is_root)
        def _():
            pltpu.make_async_copy(col_at(i, h), col_at(i, h), local_sem.at[2 * i + h]).wait()

        @pl.when(jnp.logical_not(is_root))
        def _():
            handed = remote(col_at(i, h), col_at(i, h), col_send.at[1, 2 * i + h], col_recv.at[2 * i + h], sib, c)
            handed.wait_recv()
            pl.when(r == root_cross)(handed.start)

    def cols_ready(unit_at):
        for i in range(col_unit):
            for h in range(2):
                col_ready(unit_at * col_unit + i, h)

    def col_step(q, unit_at, waits=True):
        if waits:
            cols_ready(unit_at)
        y_hi[:, cols_of(q)], y_lo[:, cols_of(q)] = split2(
            dot3((ai_hi[...], ai_lo[...]), split2(col_buf[cols_of(unit_at), :]), LAST)
        )

    def send_stats():
        stat_buf[r] = stat[...]
        for k, target in enumerate((sib, cross, diag_x)):
            remote(stat, stat_buf.at[r], stat_send.at[k], stat_recv.at[r], target, c).start()

    if tuned:
        near = jnp.logical_not(far)

        def apply(k, many, q, count):
            u_out[pl.ds(pl.multiple_of(k * unit, unit), unit * many), cols_of(q, count)] -= product(k, many, q, count)

        def only(cond, items):
            return [(cond if item[0] is True else item[0] & cond,) + tuple(item[1:]) for item in items]

        def first_stage():
            arrive(across_arrivals(1, 1))
            arrive(hop_arrivals(3, 0))
            arrive(far_arrivals(2))
            arrive(only(low_end | high_end, across_arrivals(2, 0)))

        def second_stage():
            arrive(only((z > 0) & (z < lz - 1), across_arrivals(2, 0)))
            arrive(hop_arrivals(3, 1))
            arrive(across_arrivals(2, 1))

        def stage(t):
            pl.when(t == 0)(first_stage)
            pl.when(t == 1)(second_stage)
            pl.when(t < 3)(lambda: row_step(4 + t, pick(row_ids, 4 + t)))

            @pl.when((t < 2) | near)
            def _():
                col_step(t, pick(col_ids, t))
                apply(0, 4, t, 1)

        def last_rows():
            pl.when(low_end | high_end)(fine_arrive)
            row_step(7, row_ids[7])
            send_stats()

        def rest(k):
            pl.when((k == 5) & far)(lambda: cols_ready(col_ids[2]))
            pl.when(near)(lambda: apply(k, 1, 0, 4))
            pl.when(far)(lambda: apply(k, 1, 0, 2))

        prepare()
        over(0, 4, lambda k: row_step(k, pick(row_ids, k)))
        over(0, 4, stage)
        last_rows()
        over(4, 8, rest)

        def late_column(t):
            pl.when(t == 3)(fine_ready)
            col_step(t, pick(col_ids, t), False)

            def part_of_rows(g):
                pl.when((t == 2) & (g == 1) & (r == root_cross))(fine_hand)
                apply(4 * g, 4, t, 1)

            over(0, 2, part_of_rows)

        pl.when(far)(lambda: over(2, 4, late_column))
    else:
        for t in range(5, count + 2):
            event(t)()
        prepare()

        def apply(k):
            over(0, col_units, lambda q: apply_one(k, q))

        def apply_one(k, q):
            u_out[place(k), cols_of(q)] -= product(k, 1, q, 1)

        over(0, col_units, lambda q: col_step(q, q))
        over(0, units, lambda k: row_step(k, k))
        send_stats()
        over(0, units, apply)

    for k, source in enumerate((sib, cross, diag_x)):
        remote(stat, stat_buf.at[source], stat_send.at[k], stat_recv.at[source], sib, c).wait_recv()
    total = stat_buf[0]
    for q in range(1, stat_buf.shape[0]):
        total = total + stat_buf[q]
    people = jnp.float32(width + row_buf.shape[0] * stat_buf.shape[0])
    total_out[...] = jnp.zeros_like(total_out)
    total_out[0:1, :] = (total[0:1] + stat[2:3, :]) / jnp.sqrt(people)
    total_out[1:2, :] = (total[1:2] + stat[3:4, :]) / people

    for k in range(3):
        remote(stat, stat_buf.at[r], stat_send.at[k], stat_recv.at[r], sib, c).wait_send()
    for lane in range(2):
        small(0, lane).wait_send()
    small(3, 1).wait_send()
    for kind in (1, 2):
        for lane in range(3):
            small(kind, lane).wait_send()
    for h in range(2):
        sent_all(own_sends(h))
    finish(across_arrivals(0, 1))
    for d in range(1, lz):
        for h in range(2):
            finish(hop_arrivals(d, h))
        finish(far_arrivals(d))

    skip = jnp.where(far, last_piece - first, col_parts) if tuned else col_parts

    def sent(k):
        def act():
            for h in range(2):
                handed = remote(
                    col_at(k, h), col_at(k, h), col_send.at[1, 2 * k + h], col_recv.at[0], sib, c
                )
                pl.when(is_root | (r == root_cross))(handed.wait_send)
                over_x = remote(
                    col_at(k, h), col_at(k, h), col_send.at[0, 2 * k + h], col_recv.at[0], sib, c
                )
                pl.when(is_root)(over_x.wait_send)

        pl.when(k != skip)(act)

    over(0, col_parts, sent)
    if tuned:
        pl.when(far)(fine_sent)


def store_kernel(ly, lz, group, u_in, white_in, own_in, total_in, u_out, white_out, own_out, score_out, info_out, sem):
    c = lax.axis_index("pcol")
    rows_piece = own_in.shape[0]
    col_parts = u_in.shape[1] // rows_piece
    tuned = is_tuned(lz, rows_piece, col_parts)
    row_ids, col_ids = None, None
    if tuned:
        _, row_ids, col_ids = orders(ly, lz, lax.rem(c, group) * col_parts, c // ly, lax.rem(c, ly))
    grid_copies(tuned, u_out, u_in, row_ids, col_ids, rows_piece, True, sem.at[0])
    pairs = [(own_in, own_out), (white_in, white_out)]
    pairs += [(total_in.at[0:1], score_out), (total_in.at[1:2], info_out)]
    copies = [pltpu.make_async_copy(src, dst, sem.at[1 + k]) for k, (src, dst) in enumerate(pairs)]
    for copy in copies:
        copy.start()
    for copy in copies:
        copy.wait()
    pltpu.make_async_copy(u_in, u_out, sem.at[0]).wait()


def local(diag_block, panel_cols, trailing, geno_top, geno_rest, pheno_top, pheno_rest):
    prow_size, pcol_size = lax.axis_size("prow"), lax.axis_size("pcol")
    height, width = diag_block.shape
    rows_piece = panel_cols.shape[0]
    row_count, col_count = trailing.shape
    variants = geno_top.shape[1]
    ly = 2
    lz = pcol_size // ly
    unit = min(row_count, max(rows_piece, 256))
    chunks, col_chunks = 2 * pcol_size, 2 * (col_count // rows_piece)
    f32, bf16 = jnp.float32, jnp.bfloat16
    vmem = pl.BlockSpec(memory_space=pltpu.VMEM)
    hbm = pl.BlockSpec(memory_space=pltpu.HBM)
    dma = pltpu.SemaphoreType.DMA
    wide = variants + BLOCK
    stats = (8, variants)
    arrays = [
        ((width, width), f32), ((BLOCK, 2 * BLOCK), f32), ((width, width), f32),
        ((row_count, width), f32), ((col_count, width), f32),
        ((prow_size, height, variants), f32), ((prow_size, 1, height), f32),
        ((row_count // unit, 1, unit), f32),
        ((row_count, width), bf16), ((row_count, width), bf16),
        ((width, col_count), bf16), ((width, col_count), bf16),
        ((width, wide), bf16), ((width, wide), bf16),
    ]
    arrays += [((width, width), bf16)] * 6
    arrays += [(stats, f32), ((prow_size,) + stats, f32)]
    held = pl.pallas_call(
        functools.partial(main_kernel, ly, lz, pcol_size // prow_size),
        out_shape=(
            pltpu.VMEM(trailing.shape, f32),
            pltpu.VMEM(geno_rest.shape, f32),
            pltpu.VMEM(panel_cols.shape, f32),
            pltpu.VMEM(stats, f32),
        ),
        in_specs=[hbm] * 7,
        out_specs=(vmem,) * 4,
        scratch_shapes=[pltpu.VMEM(shape, dtype) for shape, dtype in arrays]
        + [
            dma((4, 3)), dma((4, prow_size)), dma((3, chunks)), dma((chunks,)),
            dma((2, col_chunks)), dma((col_chunks,)), dma((3,)), dma((prow_size,)), dma((col_chunks + 9,)),
            dma((2, FINE)), dma((2, FINE)), dma((2, 2, FINE)), dma((2, FINE)), dma((2, FINE)),
        ],
        compiler_params=pltpu.CompilerParams(
            collective_id=0, has_side_effects=True, vmem_limit_bytes=32 * 1024 * 1024
        ),
    )(
        *(pltpu.with_memory_space_constraint(value, pltpu.HBM) for value in (
            diag_block, geno_top, pheno_top.reshape(1, height), panel_cols, trailing, geno_rest,
            pheno_rest.reshape(row_count // unit, 1, unit),
        ))
    )
    updated_block, own_factor, white_geno, score, info = order(pl.pallas_call(
        functools.partial(store_kernel, ly, lz, pcol_size // prow_size),
        out_shape=(
            jax.ShapeDtypeStruct(trailing.shape, f32),
            jax.ShapeDtypeStruct(geno_rest.shape, f32),
            jax.ShapeDtypeStruct(panel_cols.shape, f32),
            jax.ShapeDtypeStruct((1, variants), f32),
            jax.ShapeDtypeStruct((1, variants), f32),
        ),
        in_specs=[vmem] * 4,
        out_specs=(hbm,) * 5,
        scratch_shapes=[dma((5,))],
        compiler_params=pltpu.CompilerParams(vmem_limit_bytes=1024 * 1024),
    )(*(pltpu.with_memory_space_constraint(value, pltpu.VMEM) for value in held)))
    return (updated_block, own_factor, white_geno, score.reshape(variants), info.reshape(variants))


def order(values):
    updated, white, own, score, info = values
    return updated, own, white, score, info


def solution(mesh):
    placed = (
        P("prow", None),
        P(("prow", "pcol"), None),
        P("prow", "pcol"),
        P("prow", "pcol"),
        P("prow", "pcol"),
        P("prow"),
        P("prow"),
    )
    return jax.shard_map(
        local,
        mesh=mesh,
        in_specs=placed,
        out_specs=(
            P("prow", "pcol"),
            P(("prow", "pcol"), None),
            P("prow", "pcol"),
            P("pcol"),
            P("pcol"),
        ),
        check_vma=False,
    )
```

```python
import functools

import jax
import jax.numpy as jnp
from jax import lax
from jax.experimental import pallas as pl
from jax.experimental.pallas import tpu as pltpu
from jax.sharding import PartitionSpec as P

MESH = pl.DeviceIdType.MESH
HIGHEST = lax.Precision.HIGHEST
TILE = 16
FINE = 2
PARTS = 4
BLOCK = 128


def split3(value):
    hi = value.astype(jnp.bfloat16).astype(jnp.float32)
    rest = value - hi
    mid = rest.astype(jnp.bfloat16).astype(jnp.float32)
    return hi, mid, rest - mid


def tile_step(m_ref, step):
    start = pl.multiple_of(step * TILE, TILE)
    half = TILE // 2
    left = m_ref[pl.ds(start, TILE), :BLOCK]
    right = m_ref[pl.ds(start, TILE), BLOCK:]
    rolled = pltpu.roll(left, lax.rem(BLOCK - start, BLOCK), 1)
    rows = lax.broadcasted_iota(jnp.int32, (half, BLOCK), 0)
    lanes = lax.broadcasted_iota(jnp.int32, (TILE, BLOCK), 1)

    def halves(value):
        return [value[:half], value[half:]]

    def spread(parts, j):
        part, at = parts[j // half], j % half
        return jnp.broadcast_to(part[at : at + 1, :], (half, BLOCK))

    cols = [halves(jnp.broadcast_to(rolled[:, k : k + 1], (TILE, BLOCK))) for k in range(TILE)]
    values = [halves(left), halves(right)]
    pivots = [jnp.zeros((half, BLOCK), jnp.float32) for _ in range(2)]
    def inverse(value):
        inv = pl.reciprocal(value, approx=True)
        return inv * (2.0 - value * inv)

    for j in range(0, TILE, 2):
        own, low = j // half, j % half
        one, two = cols[j], cols[j + 1]
        p, b, c = spread(one, j), spread(one, j + 1), spread(two, j + 1)
        det = p * c - b * b
        inv_p, inv_det = inverse(p), inverse(det)
        ratio = b * inv_p
        pivots[own] = jnp.where(rows == low, p, jnp.where(rows == low + 1, det * inv_p, pivots[own]))
        lead, tail, after = {}, {}, [None, None]
        for part in range(own, 2):
            after[part] = two[part] - ratio * one[part]
            lead[part] = one[part] * inv_p
            tail[part] = (p * two[part] - b * one[part]) * inv_det
            if part == own:
                lead[part] = jnp.where(rows > low, lead[part], 0.0)
                tail[part] = jnp.where(rows > low + 1, tail[part], 0.0)
        for k in range(j + 2, TILE):
            top, under = spread(one, k), spread(after, k)
            for part in lead:
                if part >= k // half:
                    cols[k][part] = (cols[k][part] - lead[part] * top) - tail[part] * under
        for value in values:
            top = spread(value, j)
            under = spread(value, j + 1) - ratio * top
            for part in lead:
                value[part] = (value[part] - lead[part] * top) - tail[part] * under
    left, right = (jnp.concatenate(value, axis=0) for value in values)
    pivots = jnp.concatenate(pivots, axis=0)
    scale = lax.rsqrt(pivots)
    scale = scale * (1.5 - (0.5 * pivots) * scale * scale)
    left, right = left * scale, right * scale
    m_ref[pl.ds(start, TILE), :BLOCK] = left
    m_ref[pl.ds(start, TILE), BLOCK:] = right
    both = jnp.concatenate([left, right], axis=1)
    mult = jnp.where(lanes >= start + TILE, left, 0.0)
    a0, a1, a2 = split3(mult)
    b0, b1, b2 = split3(both)
    lhs = jnp.concatenate([a0, a0, a1, a0, a1, a2], axis=0).astype(jnp.bfloat16)
    rhs = jnp.concatenate([b0, b1, b0, b2, b1, b0], axis=0).astype(jnp.bfloat16)
    m_ref[...] -= lax.dot_general(
        lhs, rhs, (((0,), (0,)), ((), ())), preferred_element_type=jnp.float32
    )


def dot_t(a, b):
    return lax.dot_general(
        a, b, (((0,), (0,)), ((), ())), precision=HIGHEST, preferred_element_type=jnp.float32
    )


def dot_n(a, b):
    return jnp.dot(a, b, precision=HIGHEST, preferred_element_type=jnp.float32)


def invert(a_ref, w_ref, m_ref, events):
    width = a_ref.shape[0]
    blocks = width // BLOCK
    tiles = BLOCK // TILE
    w_ref[...] = jnp.zeros_like(w_ref)
    eye = (
        lax.broadcasted_iota(jnp.int32, (BLOCK, BLOCK), 0)
        == lax.broadcasted_iota(jnp.int32, (BLOCK, BLOCK), 1)
    ).astype(jnp.float32)
    slot = 0
    for k in range(blocks):
        lo, hi = k * BLOCK, (k + 1) * BLOCK
        m_ref[:, :BLOCK] = a_ref[lo:hi, lo:hi]
        m_ref[:, BLOCK:] = eye
        for part in range(PARTS):

            def body(step, carry):
                tile_step(m_ref, step)
                return carry

            lax.fori_loop(part * tiles // PARTS, (part + 1) * tiles // PARTS, body, 0)
            if part < PARTS - 1:
                if slot < len(events):
                    events[slot]()
                slot += 1
        own = m_ref[:, BLOCK:]
        if k > 0:
            w_ref[lo:hi, :lo] = dot_n(own, w_ref[lo:hi, :lo])
        w_ref[lo:hi, lo:hi] = own
        if k < blocks - 1:
            upper = dot_n(own, a_ref[lo:hi, hi:])
            a_ref[hi:, hi:] -= dot_t(upper, upper)
            w_ref[hi:, :hi] -= dot_t(upper, w_ref[lo:hi, :hi])
        if slot < len(events):
            events[slot]()
        slot += 1
    while slot < len(events):
        events[slot]()
        slot += 1


LAST = ((1,), (1,))
INNER = ((1,), (0,))


def split2(value):
    hi = value.astype(jnp.bfloat16)
    return hi, (value - hi.astype(jnp.float32)).astype(jnp.bfloat16)


def dot3(a, b, dims):
    left = jnp.concatenate([a[0], a[0], a[1]], axis=dims[0][0])
    right = jnp.concatenate([b[0], b[1], b[0]], axis=dims[1][0])
    return lax.dot_general(left, right, (dims, ((), ())), preferred_element_type=jnp.float32)


def column(row):
    return jnp.transpose(jnp.broadcast_to(row, (BLOCK, row.shape[1])))


def weighted(weights, values):
    wide = jnp.concatenate([weights] * (values.shape[1] // BLOCK), axis=1)
    return jnp.sum(wide * values, axis=0, keepdims=True)


def orders(ly, lz, first, z, y):
    low_end, high_end = z == 0, z == lz - 1
    far = (low_end & (y == 1)) | (high_end & (y == 0))

    def nearest(k):
        near = jnp.minimum(z, lz - 1 - z)
        step = (k + 1) // 2
        zigzag = z + (step if k % 2 == 1 else -step)
        onward = jnp.where(z < lz - 1 - z, k, lz - 1 - k)
        return jnp.where(k <= 2 * near, zigzag, onward)

    def row(k, turned):
        return nearest(k) * ly + (1 - y if turned else y)

    row_ids = [
        row(0, False), row(0, True), row(1, False), row(2, False),
        row(1, True), row(3, False), row(2, True), row(3, True),
    ]
    flip = first // ly + 1 <= z
    col_ids = [
        jnp.where(flip, 1 - q % 2, q % 2) * ly + (y if q // 2 == 0 else 1 - y) for q in range(4)
    ]
    return far, row_ids, col_ids


def pick(values, k):
    out = values[-1]
    for j in range(len(values) - 2, -1, -1):
        out = jnp.where(k == j, values[j], out)
    return out


def over(lo, hi, fn):
    def body(k, carry):
        fn(k)
        return carry

    lax.fori_loop(lo, hi, body, 0)


def is_tuned(lz, rows_piece, col_parts):
    return lz == 4 and rows_piece == 256 and col_parts == 4


def grid_copies(tuned, far_side, near_side, row_ids, col_ids, rows_piece, outward, sem):
    if not tuned:
        src, dst = (near_side, far_side) if outward else (far_side, near_side)
        pltpu.make_async_copy(src, dst, sem).start()
        return

    def one(k):
        i, j = k // 4, lax.rem(k, 4)

        def at(ref, row, col):
            return ref.at[
                pl.ds(pl.multiple_of(row * rows_piece, rows_piece), rows_piece),
                pl.ds(pl.multiple_of(col * rows_piece, rows_piece), rows_piece),
            ]

        here, there = at(near_side, i, j), at(far_side, pick(row_ids, i), pick(col_ids, j))
        src, dst = (here, there) if outward else (there, here)
        pltpu.make_async_copy(src, dst, sem).start()

    over(0, 32, one)


def main_kernel(
    ly, lz, group,
    diag_in, top_in, pheno_in, panel_in, trailing_in, geno_in, rest_in,
    u_out, white_out, own_out, total_out, row_hi, row_lo, y_hi, y_lo,
    a_ref, m_ref, w_ref, row_buf, col_buf, top_buf, pheno_buf, rest_buf,
    g_hi, g_lo, w_hi, w_lo, wt_hi, wt_lo, ai_hi, ai_lo,
    stat, stat_buf,
    small_send, small_recv, row_send, row_recv, col_send, col_recv, stat_send, stat_recv, local_sem,
    fine_send, fine_recv, fine_col_send, fine_col_recv, fine_local,
):
    r, c = lax.axis_index("prow"), lax.axis_index("pcol")
    z, y = c // ly, lax.rem(c, ly)
    sib = r + 1 - 2 * lax.rem(r, 2)
    cross = r + 2 - 4 * (r // 2)
    diag_x = sib + 2 - 4 * (sib // 2)
    other = z * ly + (1 - y)
    rows_piece, width = panel_in.shape
    half = rows_piece // 2
    pieces = row_buf.shape[0] // rows_piece
    variants = top_in.shape[1]
    col_parts = col_buf.shape[0] // rows_piece
    root = c // group
    first = lax.rem(c, group) * col_parts
    is_root = root == r
    root_cross = root + 2 - 4 * (root // 2)
    low_end, high_end = z == 0, z == lz - 1
    tuned = is_tuned(lz, rows_piece, col_parts)
    far, row_ids, col_ids = orders(ly, lz, first, z, y) if tuned else (None, None, None)

    barrier = pltpu.get_barrier_semaphore()

    def greet(row, col):
        pl.semaphore_signal(barrier, inc=1, device_id={"prow": row, "pcol": col}, device_id_type=MESH)

    greet(sib, c)
    greet(cross, c)
    greet(diag_x, c)
    greet(r, other)

    @pl.when(z > 0)
    def _():
        greet(r, c - ly)

    @pl.when(z < lz - 1)
    def _():
        greet(r, c + ly)

    pl.semaphore_wait(barrier, 4 + jnp.minimum(z, 1) + jnp.minimum(lz - 1 - z, 1))

    def remote(src, dst, send, recv, row, col):
        return pltpu.make_async_remote_copy(
            src_ref=src, dst_ref=dst, send_sem=send, recv_sem=recv,
            device_id={"prow": row, "pcol": col}, device_id_type=MESH,
        )

    def each(items, act):
        for item in items:
            if item[0] is True:
                act(item)
            elif item[0] is not False:
                pl.when(item[0])(functools.partial(act, item))

    def start_all(sends):
        each(sends, lambda item: item[1]().start())

    def sent_all(sends):
        each(sends, lambda item: item[1]().wait_send())

    height = diag_in.shape[0]
    side = 2 * height
    mine, theirs = (r // 2) * side, (cross // 2) * side

    def band(q):
        return pl.ds(pl.multiple_of(q * height, height), height)

    def half_cols(start, kind):
        return pl.ds(pl.multiple_of(start + (height if kind == 3 else 0), height), height)

    def small(kind, lane):
        part = cross if lane == 2 else r
        if kind in (0, 3):
            if lane == 0:
                src, dst = diag_in, a_ref.at[band(r), :]
            else:
                cols = half_cols(theirs if lane == 2 else mine, kind)
                dst = a_ref.at[band(part), cols]
                src = dst if lane == 2 else diag_in.at[:, cols]
        else:
            buf = (None, top_buf, pheno_buf)[kind]
            dst = buf.at[part]
            src = dst if lane == 2 else (None, top_in, pheno_in)[kind]
        return remote(
            src, dst, small_send.at[kind, lane], small_recv.at[kind, part],
            cross if lane == 1 else sib, c,
        )

    def small_wait(kind, part):
        if kind in (0, 3):
            dst = a_ref.at[band(part), :]
            if part is not sib:
                dst = a_ref.at[band(part), half_cols(theirs, kind)]
        else:
            dst = (None, top_buf, pheno_buf)[kind].at[part]
        remote(dst, dst, small_send.at[kind, 0], small_recv.at[kind, part], sib, c).wait_recv()

    def chunk(b, h):
        return row_buf.at[pl.ds(pl.multiple_of((2 * b + h) * half, half), half), :]

    def own_half(h):
        return panel_in.at[pl.ds(h * half, half), :]

    def row_copy(way, b, h, own=False):
        target = (c + ly, c - ly, other)[way]
        return lambda: remote(
            own_half(h) if own else chunk(b, h), chunk(b, h),
            row_send.at[way, 2 * b + h], row_recv.at[2 * b + h], r, target,
        )

    def row_wait(b, h):
        remote(chunk(b, h), chunk(b, h), row_send.at[0, 0], row_recv.at[2 * b + h], r, other).wait_recv()

    def col_at(i, h):
        return col_buf.at[pl.ds(pl.multiple_of((2 * i + h) * half, half), half), :]

    def col_copies(b, h, own):
        i = b - first
        src = own_half(h) if own else chunk(b, h)
        k = 2 * i + h
        return (
            remote(src, col_at(i, h), col_send.at[0, k], col_recv.at[k], cross, c),
            remote(src, col_at(i, h), col_send.at[1, k], col_recv.at[k], sib, c),
            pltpu.make_async_copy(src, col_at(i, h), local_sem.at[k]),
        )

    def col_start(b, h, own=False):
        @pl.when(is_root & (b >= first) & (b < first + col_parts))
        def _():
            for copy in col_copies(b, h, own):
                copy.start()

    def part(ref, b, h, p):
        rows = half // FINE
        return ref.at[pl.ds(pl.multiple_of((2 * b + h) * half + p * rows, rows), rows), :]

    def fine_copies(way, b, h):
        target = (c + ly, c - ly, other)[way]

        def one(p):
            return lambda: remote(
                part(row_buf, b, h, p), part(row_buf, b, h, p), fine_send.at[h, p], fine_recv.at[h, p], r, target
            )

        return [one(p) for p in range(FINE)]

    last_piece = jnp.where(low_end, (lz - 1) * ly, 0) + 1 - y

    def fine_col(h, p):
        src, dst = part(row_buf, last_piece, h, p), part(col_buf, last_piece - first, h, p)
        return (
            remote(src, dst, fine_col_send.at[0, h, p], fine_col_recv.at[h, p], cross, c),
            remote(src, dst, fine_col_send.at[1, h, p], fine_col_recv.at[h, p], sib, c),
            pltpu.make_async_copy(src, dst, fine_local.at[h, p]),
        )

    def fine_handed(h, p):
        dst = part(col_buf, last_piece - first, h, p)
        return remote(dst, dst, fine_col_send.at[1, h, p], fine_col_recv.at[h, p], sib, c)

    def fine_arrive():
        for p in range(FINE):
            for h in (1, 0):
                dst = part(row_buf, last_piece, h, p)
                remote(dst, dst, fine_send.at[h, p], fine_recv.at[h, p], r, other).wait_recv()

                @pl.when(is_root & far)
                def _():
                    for copy in fine_col(h, p):
                        copy.start()

    def fine_hand():
        for p in range(FINE):
            for h in (1, 0):
                fine_handed(h, p).wait_recv()
                fine_handed(h, p).start()

    def fine_ready():
        for p in range(FINE):
            for h in (1, 0):

                @pl.when(is_root)
                def _():
                    fine_col(h, p)[2].wait()

                @pl.when(jnp.logical_not(is_root) & (r != root_cross))
                def _():
                    fine_handed(h, p).wait_recv()

    def fine_sent():
        for p in range(FINE):
            for h in (1, 0):

                @pl.when(is_root)
                def _():
                    for copy in fine_col(h, p)[:2]:
                        copy.wait_send()

                @pl.when(r == root_cross)
                def _():
                    fine_handed(h, p).wait_send()

    def own_sends(h):
        return [
            (True, row_copy(2, c, h, True)),
            (z < lz - 1, row_copy(0, c, h, True)),
            (z > 0, row_copy(1, c, h, True)),
        ]

    def hop_arrivals(d, h):
        low, high = c - d * ly, c + d * ly
        low_over = True if h == 0 else z != d
        high_over = True if h == 0 else z + d != lz - 1
        low_across, high_across = [(low_over, row_copy(2, low, h))], [(high_over, row_copy(2, high, h))]
        if tuned and d == lz - 1 and h == 0:
            low_across = [(True, copy) for copy in fine_copies(2, low, h)]
            high_across = [(True, copy) for copy in fine_copies(2, high, h)]
        return [
            (z >= d, low, h, [(z < lz - 1, row_copy(0, low, h))] + low_across),
            (z + d < lz, high, h, [(z > 0, row_copy(1, high, h))] + high_across),
        ]

    def across_arrivals(d, h):
        if d == 0:
            sends = []
            if h == 1 and lz > 1:
                sends = [(low_end, row_copy(0, other, h)), (high_end, row_copy(1, other, h))]
            return [(True, other, h, sends)]
        return [
            (z >= d if h == 0 else z > d, other - d * ly, h, []),
            (z + d < lz if h == 0 else z + d < lz - 1, other + d * ly, h, []),
        ]

    def far_arrivals(d):
        low, high = 1 - y, (lz - 1) * ly + 1 - y
        ups, downs = [row_copy(0, low, 1)], [row_copy(1, high, 1)]
        if tuned and d == lz - 2:
            ups, downs = fine_copies(0, low, 1), fine_copies(1, high, 1)
        return [
            (z == d, low, 1, [(z < lz - 1, copy) for copy in ups]),
            (z == lz - 1 - d, high, 1, [(z > 0, copy) for copy in downs]),
        ]

    def arrive(items):
        def act(item):
            _, b, h, sends = item
            row_wait(b, h)
            start_all(sends)
            col_start(b, h)

        each(items, act)

    def finish(items):
        each(items, lambda item: sent_all(item[3]))

    small(0, 1).start()
    small(0, 0).start()
    small(3, 1).start()
    diag_copy = pltpu.make_async_copy(diag_in, a_ref.at[band(r), :], local_sem.at[2 * col_parts])
    diag_copy.start()
    for h in range(2):
        start_all(own_sends(h))
    for kind in (1, 2):
        small(kind, 1).start()
        small(kind, 0).start()
    own_copies = [
        pltpu.make_async_copy(own_half(h), chunk(c, h), local_sem.at[2 * col_parts + 1 + h]) for h in range(2)
    ]
    others = [
        pltpu.make_async_copy(src, dst, local_sem.at[2 * col_parts + 3 + k])
        for k, (src, dst) in enumerate((
            (top_in, top_buf.at[r]), (pheno_in, pheno_buf.at[r]), (rest_in, rest_buf),
            (geno_in, white_out),
        ))
    ]
    for copy in own_copies + others:
        copy.start()
    for h in range(2):
        col_start(c, h, True)
    trailing_sem = local_sem.at[2 * col_parts + 7]
    grid_copies(tuned, trailing_in, u_out, row_ids, col_ids, rows_piece, False, trailing_sem)
    others.append(pltpu.make_async_copy(trailing_in, u_out, trailing_sem))
    small_wait(0, cross)
    small(0, 2).start()
    small_wait(0, sib)
    small_wait(0, diag_x)
    diag_copy.wait()

    def diag_event():
        small_wait(3, cross)
        small(3, 2).start()

    def corner_event():
        small_wait(3, diag_x)
        small(0, 2).wait_send()
        small(3, 2).wait_send()

        @pl.when(r >= 2)
        def _():
            a_ref[:side, side:] = jnp.transpose(a_ref[side:, :side])

    def top_event():
        for kind in (1, 2):
            small_wait(kind, cross)
            small(kind, 2).start()

    def nothing():
        pass

    last = 2 * (lz - 1)

    def event(t):
        def run():
            if t <= last:
                arrive(hop_arrivals((t + 1) // 2, (t - 1) % 2))
            if t % 2 == 1 and t // 2 >= 1:
                arrive(far_arrivals(t // 2))
            if t == 2:
                arrive(across_arrivals(0, 0))
                arrive(across_arrivals(0, 1))
            if t >= 4 and (t - 2) // 2 < lz:
                arrive(across_arrivals((t - 2) // 2, t % 2))

        return run

    count = 2 * lz
    events = [nothing] * 16
    events[0], events[2], events[3] = diag_event, corner_event, event(1)
    events[4], events[7] = top_event, event(2)
    events[11], events[15] = event(3), event(4)
    invert(a_ref, w_ref, m_ref, events)

    def prepare():
        for kind in (1, 2):
            small_wait(kind, sib)
            small_wait(kind, diag_x)
        for copy in own_copies + others:
            copy.wait()
        whole = w_ref[...]
        w_hi[...], w_lo[...] = split2(whole)
        wt_hi[...], wt_lo[...] = split2(jnp.transpose(whole))
        w, turned = (w_hi[...], w_lo[...]), (wt_hi[...], wt_lo[...])
        ai_hi[...], ai_lo[...] = split2(dot3(turned, w, INNER))
        phenos = jnp.concatenate([pheno_buf[q] for q in range(pheno_buf.shape[0])], axis=1)
        joined = jnp.concatenate([top_buf[...].reshape(width, variants), column(phenos)], axis=1)
        both = dot3(w, split2(joined), INNER)
        g_hi[...], g_lo[...] = split2(dot3(turned, split2(both), INNER))
        white = both[:, :variants]
        stat[...] = jnp.zeros_like(stat)
        stat[2:3, :] = weighted(both[:, variants:], white)
        stat[3:4, :] = jnp.sum(white * white, axis=0, keepdims=True)
        at = pl.ds(pl.multiple_of(c * rows_piece, rows_piece), rows_piece)
        own_out[...] = dot3(split2(row_buf[at, :]), (wt_hi[...], wt_lo[...]), INNER)

    unit = rest_buf.shape[2]
    units = row_buf.shape[0] // unit
    col_unit = min(col_parts, max(1, 256 // rows_piece))
    col_units = col_parts // col_unit
    col_wide = col_unit * rows_piece

    def place(b):
        return pl.ds(pl.multiple_of(b * unit, unit), unit)

    def row_step(k, b):
        at, slot = place(b), place(k)
        parts = split2(row_buf[at, :])
        row_hi[slot, :], row_lo[slot, :] = parts
        shift = dot3(parts, (g_hi[...], g_lo[...]), INNER)
        white = white_out[at, :] - shift[:, :variants]
        white_out[at, :] = white
        stat[0:1, :] += weighted(column(rest_buf[b]) - shift[:, variants:], white)
        stat[1:2, :] += jnp.sum(white * white, axis=0, keepdims=True)

    def cols_of(q, count=1):
        return pl.ds(pl.multiple_of(q * col_wide, col_wide), col_wide * count)

    def product(k, many, q, count):
        slots = pl.ds(pl.multiple_of(k * unit, unit), unit * many)
        cols = cols_of(q, count)
        return dot3((row_hi[slots, :], row_lo[slots, :]), (y_hi[:, cols], y_lo[:, cols]), INNER)

    def col_ready(i, h):
        @pl.when(is_root)
        def _():
            pltpu.make_async_copy(col_at(i, h), col_at(i, h), local_sem.at[2 * i + h]).wait()

        @pl.when(jnp.logical_not(is_root))
        def _():
            handed = remote(col_at(i, h), col_at(i, h), col_send.at[1, 2 * i + h], col_recv.at[2 * i + h], sib, c)
            handed.wait_recv()
            pl.when(r == root_cross)(handed.start)

    def cols_ready(unit_at):
        for i in range(col_unit):
            for h in range(2):
                col_ready(unit_at * col_unit + i, h)

    def col_step(q, unit_at, waits=True):
        if waits:
            cols_ready(unit_at)
        y_hi[:, cols_of(q)], y_lo[:, cols_of(q)] = split2(
            dot3((ai_hi[...], ai_lo[...]), split2(col_buf[cols_of(unit_at), :]), LAST)
        )

    def send_stats():
        stat_buf[r] = stat[...]
        for k, target in enumerate((sib, cross, diag_x)):
            remote(stat, stat_buf.at[r], stat_send.at[k], stat_recv.at[r], target, c).start()

    if tuned:
        near = jnp.logical_not(far)

        def apply(k, many, q, count):
            u_out[pl.ds(pl.multiple_of(k * unit, unit), unit * many), cols_of(q, count)] -= product(k, many, q, count)

        def only(cond, items):
            return [(cond if item[0] is True else item[0] & cond,) + tuple(item[1:]) for item in items]

        def first_stage():
            arrive(across_arrivals(1, 1))
            arrive(hop_arrivals(3, 0))
            arrive(far_arrivals(2))
            arrive(only(low_end | high_end, across_arrivals(2, 0)))

        def second_stage():
            arrive(only((z > 0) & (z < lz - 1), across_arrivals(2, 0)))
            arrive(hop_arrivals(3, 1))
            arrive(across_arrivals(2, 1))

        def last_rows():
            pl.when((low_end | high_end) & near)(fine_arrive)
            row_step(7, row_ids[7])
            send_stats()

        def last_column():
            spare()
            fine_ready()

        def spare():
            def one(k):
                pl.when((k == 7) & (r == root_cross))(fine_hand)
                apply(k, 1, 0, 2)

            over(4, 8, one)

        def stage(t):
            pl.when(t == 1)(second_stage)
            pl.when((t == 2) & far & (low_end | high_end))(fine_arrive)
            pl.when(t < 3)(lambda: row_step(4 + t, pick(row_ids, 4 + t)))
            pl.when(((t == 3) & near) | ((t == 2) & far))(last_rows)
            unit_at = pick(col_ids, t)
            pl.when((t < 3) | near)(lambda: cols_ready(unit_at))
            pl.when((t == 3) & far)(last_column)
            col_step(t, unit_at, False)
            apply(0, 4, t, 1)

        prepare()
        first_stage()
        over(0, 4, lambda k: row_step(k, pick(row_ids, k)))
        over(0, 4, stage)
    else:
        for t in range(5, count + 2):
            event(t)()
        prepare()

        def apply(k):
            over(0, col_units, lambda q: apply_one(k, q))

        def apply_one(k, q):
            u_out[place(k), cols_of(q)] -= product(k, 1, q, 1)

        over(0, col_units, lambda q: col_step(q, q))
        over(0, units, lambda k: row_step(k, k))
        send_stats()
        over(0, units, apply)

    for k, source in enumerate((sib, cross, diag_x)):
        remote(stat, stat_buf.at[source], stat_send.at[k], stat_recv.at[source], sib, c).wait_recv()
    total = stat_buf[0]
    for q in range(1, stat_buf.shape[0]):
        total = total + stat_buf[q]
    people = jnp.float32(width + row_buf.shape[0] * stat_buf.shape[0])
    total_out[...] = jnp.zeros_like(total_out)
    total_out[0:1, :] = (total[0:1] + stat[2:3, :]) / jnp.sqrt(people)
    total_out[1:2, :] = (total[1:2] + stat[3:4, :]) / people

    for k in range(3):
        remote(stat, stat_buf.at[r], stat_send.at[k], stat_recv.at[r], sib, c).wait_send()
    for lane in range(2):
        small(0, lane).wait_send()
    small(3, 1).wait_send()
    for kind in (1, 2):
        for lane in range(3):
            small(kind, lane).wait_send()
    for h in range(2):
        sent_all(own_sends(h))
    finish(across_arrivals(0, 1))
    for d in range(1, lz):
        for h in range(2):
            finish(hop_arrivals(d, h))
        finish(far_arrivals(d))

    skip = jnp.where(far, last_piece - first, col_parts) if tuned else col_parts

    def sent(k):
        def act():
            for h in range(2):
                handed = remote(
                    col_at(k, h), col_at(k, h), col_send.at[1, 2 * k + h], col_recv.at[0], sib, c
                )
                pl.when(is_root | (r == root_cross))(handed.wait_send)
                over_x = remote(
                    col_at(k, h), col_at(k, h), col_send.at[0, 2 * k + h], col_recv.at[0], sib, c
                )
                pl.when(is_root)(over_x.wait_send)

        pl.when(k != skip)(act)

    over(0, col_parts, sent)
    if tuned:
        pl.when(far)(fine_sent)


def store_kernel(
    ly, lz, group,
    u_in, white_in, own_in, total_in, row_hi, row_lo, y_hi, y_lo,
    u_out, white_out, own_out, score_out, info_out,
    held, sem, row_sem,
):
    c = lax.axis_index("pcol")
    rows_piece = own_in.shape[0]
    col_parts = u_in.shape[1] // rows_piece
    tuned = is_tuned(lz, rows_piece, col_parts)
    pairs = [(own_in, own_out), (white_in, white_out)]
    pairs += [(total_in.at[0:1], score_out), (total_in.at[1:2], info_out)]
    copies = [pltpu.make_async_copy(src, dst, sem.at[1 + k]) for k, (src, dst) in enumerate(pairs)]
    if not tuned:
        copies.append(pltpu.make_async_copy(u_in, u_out, sem.at[0]))
        for copy in copies:
            copy.start()
        for copy in copies:
            copy.wait()
        return
    far, row_ids, col_ids = orders(ly, lz, lax.rem(c, group) * col_parts, c // ly, lax.rem(c, ly))
    near = jnp.logical_not(far)

    def span(k):
        return pl.ds(pl.multiple_of(k * rows_piece, rows_piece), rows_piece)

    def store_row(k, src, at, row_at, cols=range(4)):
        for j in cols:
            pltpu.make_async_copy(
                src.at[span(at), span(j)], u_out.at[span(pick(row_ids, k)), span(col_ids[j])], row_at
            ).start()

    over(0, 4, lambda k: store_row(k, u_in, k, row_sem.at[k]))
    for copy in copies:
        copy.start()

    pl.when(far)(lambda: over(4, 8, lambda k: store_row(k, u_in, k, row_sem.at[k], (0, 1))))

    def later(k, start):
        at, cols = span(k), pl.ds(start * rows_piece, (4 - start) * rows_piece)
        moved = dot3((row_hi[at, :], row_lo[at, :]), (y_hi[:, cols], y_lo[:, cols]), INNER)
        held[span(k - 4), cols] = u_in[at, cols] - moved
        store_row(k, held, k - 4, row_sem.at[k], range(start, 4))

    pl.when(near)(lambda: over(4, 8, lambda k: later(k, 0)))
    pl.when(far)(lambda: over(4, 8, lambda k: later(k, 2)))
    for copy in copies:
        copy.wait()
    over(0, 8, lambda k: pltpu.make_async_copy(held.at[span(0), :], u_out.at[span(0), :], row_sem.at[k]).wait())


def local(diag_block, panel_cols, trailing, geno_top, geno_rest, pheno_top, pheno_rest):
    prow_size, pcol_size = lax.axis_size("prow"), lax.axis_size("pcol")
    height, width = diag_block.shape
    rows_piece = panel_cols.shape[0]
    row_count, col_count = trailing.shape
    variants = geno_top.shape[1]
    ly = 2
    lz = pcol_size // ly
    unit = min(row_count, max(rows_piece, 256))
    chunks, col_chunks = 2 * pcol_size, 2 * (col_count // rows_piece)
    f32, bf16 = jnp.float32, jnp.bfloat16
    vmem = pl.BlockSpec(memory_space=pltpu.VMEM)
    hbm = pl.BlockSpec(memory_space=pltpu.HBM)
    dma = pltpu.SemaphoreType.DMA
    wide = variants + BLOCK
    stats = (8, variants)
    arrays = [
        ((width, width), f32), ((BLOCK, 2 * BLOCK), f32), ((width, width), f32),
        ((row_count, width), f32), ((col_count, width), f32),
        ((prow_size, height, variants), f32), ((prow_size, 1, height), f32),
        ((row_count // unit, 1, unit), f32),
        ((width, wide), bf16), ((width, wide), bf16),
    ]
    arrays += [((width, width), bf16)] * 6
    arrays += [(stats, f32), ((prow_size,) + stats, f32)]
    held = pl.pallas_call(
        functools.partial(main_kernel, ly, lz, pcol_size // prow_size),
        out_shape=(
            pltpu.VMEM(trailing.shape, f32),
            pltpu.VMEM(geno_rest.shape, f32),
            pltpu.VMEM(panel_cols.shape, f32),
            pltpu.VMEM(stats, f32),
            pltpu.VMEM((row_count, width), bf16),
            pltpu.VMEM((row_count, width), bf16),
            pltpu.VMEM((width, col_count), bf16),
            pltpu.VMEM((width, col_count), bf16),
        ),
        in_specs=[hbm] * 7,
        out_specs=(vmem,) * 8,
        scratch_shapes=[pltpu.VMEM(shape, dtype) for shape, dtype in arrays]
        + [
            dma((4, 3)), dma((4, prow_size)), dma((3, chunks)), dma((chunks,)),
            dma((2, col_chunks)), dma((col_chunks,)), dma((3,)), dma((prow_size,)), dma((col_chunks + 9,)),
            dma((2, FINE)), dma((2, FINE)), dma((2, 2, FINE)), dma((2, FINE)), dma((2, FINE)),
        ],
        compiler_params=pltpu.CompilerParams(
            collective_id=0, has_side_effects=True, vmem_limit_bytes=32 * 1024 * 1024
        ),
    )(
        *(pltpu.with_memory_space_constraint(value, pltpu.HBM) for value in (
            diag_block, geno_top, pheno_top.reshape(1, height), panel_cols, trailing, geno_rest,
            pheno_rest.reshape(row_count // unit, 1, unit),
        ))
    )
    updated_block, own_factor, white_geno, score, info = order(pl.pallas_call(
        functools.partial(store_kernel, ly, lz, pcol_size // prow_size),
        out_shape=(
            jax.ShapeDtypeStruct(trailing.shape, f32),
            jax.ShapeDtypeStruct(geno_rest.shape, f32),
            jax.ShapeDtypeStruct(panel_cols.shape, f32),
            jax.ShapeDtypeStruct((1, variants), f32),
            jax.ShapeDtypeStruct((1, variants), f32),
        ),
        in_specs=[vmem] * 8,
        out_specs=(hbm,) * 5,
        scratch_shapes=[
            pltpu.VMEM((row_count // 2, col_count), f32), dma((5,)), dma((8,)),
        ],
        compiler_params=pltpu.CompilerParams(vmem_limit_bytes=12 * 1024 * 1024),
    )(*(pltpu.with_memory_space_constraint(value, pltpu.VMEM) for value in held)))
    return (updated_block, own_factor, white_geno, score.reshape(variants), info.reshape(variants))


def order(values):
    updated, white, own, score, info = values
    return updated, own, white, score, info


def solution(mesh):
    placed = (
        P("prow", None),
        P(("prow", "pcol"), None),
        P("prow", "pcol"),
        P("prow", "pcol"),
        P("prow", "pcol"),
        P("prow"),
        P("prow"),
    )
    return jax.shard_map(
        local,
        mesh=mesh,
        in_specs=placed,
        out_specs=(
            P("prow", "pcol"),
            P(("prow", "pcol"), None),
            P("prow", "pcol"),
            P("pcol"),
            P("pcol"),
        ),
        check_vma=False,
    )
```

```python
import functools

import jax
import jax.numpy as jnp
from jax import lax
from jax.experimental import pallas as pl
from jax.experimental.pallas import tpu as pltpu
from jax.sharding import PartitionSpec as P

MESH = pl.DeviceIdType.MESH
HIGHEST = lax.Precision.HIGHEST
TILE = 16
FINE = 2
PARTS = 4
BLOCK = 128


def split3(value):
    hi = value.astype(jnp.bfloat16).astype(jnp.float32)
    rest = value - hi
    mid = rest.astype(jnp.bfloat16).astype(jnp.float32)
    return hi, mid, rest - mid


def tile_step(m_ref, step):
    start = pl.multiple_of(step * TILE, TILE)
    half = TILE // 2
    left = m_ref[pl.ds(start, TILE), :BLOCK]
    right = m_ref[pl.ds(start, TILE), BLOCK:]
    rolled = pltpu.roll(left, lax.rem(BLOCK - start, BLOCK), 1)
    rows = lax.broadcasted_iota(jnp.int32, (half, BLOCK), 0)
    lanes = lax.broadcasted_iota(jnp.int32, (TILE, BLOCK), 1)

    def halves(value):
        return [value[:half], value[half:]]

    def spread(parts, j):
        part, at = parts[j // half], j % half
        return jnp.broadcast_to(part[at : at + 1, :], (half, BLOCK))

    cols = [halves(jnp.broadcast_to(rolled[:, k : k + 1], (TILE, BLOCK))) for k in range(TILE)]
    values = [halves(left), halves(right)]
    pivots = [jnp.zeros((half, BLOCK), jnp.float32) for _ in range(2)]
    def inverse(value):
        inv = pl.reciprocal(value, approx=True)
        return inv * (2.0 - value * inv)

    for j in range(0, TILE, 2):
        own, low = j // half, j % half
        one, two = cols[j], cols[j + 1]
        p, b, c = spread(one, j), spread(one, j + 1), spread(two, j + 1)
        det = p * c - b * b
        inv_p, inv_det = inverse(p), inverse(det)
        ratio = b * inv_p
        pivots[own] = jnp.where(rows == low, p, jnp.where(rows == low + 1, det * inv_p, pivots[own]))
        lead, tail, after = {}, {}, [None, None]
        for part in range(own, 2):
            after[part] = two[part] - ratio * one[part]
            lead[part] = one[part] * inv_p
            tail[part] = (p * two[part] - b * one[part]) * inv_det
            if part == own:
                lead[part] = jnp.where(rows > low, lead[part], 0.0)
                tail[part] = jnp.where(rows > low + 1, tail[part], 0.0)
        for k in range(j + 2, TILE):
            top, under = spread(one, k), spread(after, k)
            for part in lead:
                if part >= k // half:
                    cols[k][part] = (cols[k][part] - lead[part] * top) - tail[part] * under
        for value in values:
            top = spread(value, j)
            under = spread(value, j + 1) - ratio * top
            for part in lead:
                value[part] = (value[part] - lead[part] * top) - tail[part] * under
    left, right = (jnp.concatenate(value, axis=0) for value in values)
    pivots = jnp.concatenate(pivots, axis=0)
    scale = lax.rsqrt(pivots)
    scale = scale * (1.5 - (0.5 * pivots) * scale * scale)
    left, right = left * scale, right * scale
    m_ref[pl.ds(start, TILE), :BLOCK] = left
    m_ref[pl.ds(start, TILE), BLOCK:] = right
    both = jnp.concatenate([left, right], axis=1)
    mult = jnp.where(lanes >= start + TILE, left, 0.0)
    a0, a1, a2 = split3(mult)
    b0, b1, b2 = split3(both)
    lhs = jnp.concatenate([a0, a0, a1, a0, a1, a2], axis=0).astype(jnp.bfloat16)
    rhs = jnp.concatenate([b0, b1, b0, b2, b1, b0], axis=0).astype(jnp.bfloat16)
    m_ref[...] -= lax.dot_general(
        lhs, rhs, (((0,), (0,)), ((), ())), preferred_element_type=jnp.float32
    )


def dot_t(a, b):
    return lax.dot_general(
        a, b, (((0,), (0,)), ((), ())), precision=HIGHEST, preferred_element_type=jnp.float32
    )


def dot_n(a, b):
    return jnp.dot(a, b, precision=HIGHEST, preferred_element_type=jnp.float32)


def invert(a_ref, w_ref, m_ref, events):
    width = a_ref.shape[0]
    blocks = width // BLOCK
    tiles = BLOCK // TILE
    w_ref[...] = jnp.zeros_like(w_ref)
    eye = (
        lax.broadcasted_iota(jnp.int32, (BLOCK, BLOCK), 0)
        == lax.broadcasted_iota(jnp.int32, (BLOCK, BLOCK), 1)
    ).astype(jnp.float32)
    slot = 0
    for k in range(blocks):
        lo, hi = k * BLOCK, (k + 1) * BLOCK
        m_ref[:, :BLOCK] = a_ref[lo:hi, lo:hi]
        m_ref[:, BLOCK:] = eye
        for part in range(PARTS):

            def body(step, carry):
                tile_step(m_ref, step)
                return carry

            lax.fori_loop(part * tiles // PARTS, (part + 1) * tiles // PARTS, body, 0)
            if part < PARTS - 1:
                if slot < len(events):
                    events[slot]()
                slot += 1
        own = m_ref[:, BLOCK:]
        if k > 0:
            w_ref[lo:hi, :lo] = dot_n(own, w_ref[lo:hi, :lo])
        w_ref[lo:hi, lo:hi] = own
        if k < blocks - 1:
            upper = dot_n(own, a_ref[lo:hi, hi:])
            a_ref[hi:, hi:] -= dot_t(upper, upper)
            w_ref[hi:, :hi] -= dot_t(upper, w_ref[lo:hi, :hi])
        if slot < len(events):
            events[slot]()
        slot += 1
    while slot < len(events):
        events[slot]()
        slot += 1


LAST = ((1,), (1,))
INNER = ((1,), (0,))


def split2(value):
    hi = value.astype(jnp.bfloat16)
    return hi, (value - hi.astype(jnp.float32)).astype(jnp.bfloat16)


def dot3(a, b, dims):
    left = jnp.concatenate([a[0], a[0], a[1]], axis=dims[0][0])
    right = jnp.concatenate([b[0], b[1], b[0]], axis=dims[1][0])
    return lax.dot_general(left, right, (dims, ((), ())), preferred_element_type=jnp.float32)


def column(row):
    return jnp.transpose(jnp.broadcast_to(row, (BLOCK, row.shape[1])))


def weighted(weights, values):
    wide = jnp.concatenate([weights] * (values.shape[1] // BLOCK), axis=1)
    return jnp.sum(wide * values, axis=0, keepdims=True)


def orders(ly, lz, first, z, y):
    low_end, high_end = z == 0, z == lz - 1
    far = (low_end & (y == 1)) | (high_end & (y == 0))

    def nearest(k):
        near = jnp.minimum(z, lz - 1 - z)
        step = (k + 1) // 2
        zigzag = z + (step if k % 2 == 1 else -step)
        onward = jnp.where(z < lz - 1 - z, k, lz - 1 - k)
        return jnp.where(k <= 2 * near, zigzag, onward)

    def row(k, turned):
        return nearest(k) * ly + (1 - y if turned else y)

    row_ids = [
        row(0, False), row(0, True), row(1, False), row(2, False),
        row(1, True), row(3, False), row(2, True), row(3, True),
    ]
    flip = first // ly + 1 <= z
    col_ids = [
        jnp.where(flip, 1 - q % 2, q % 2) * ly + (y if q // 2 == 0 else 1 - y) for q in range(4)
    ]
    return far, row_ids, col_ids


def pick(values, k):
    out = values[-1]
    for j in range(len(values) - 2, -1, -1):
        out = jnp.where(k == j, values[j], out)
    return out


def over(lo, hi, fn):
    def body(k, carry):
        fn(k)
        return carry

    lax.fori_loop(lo, hi, body, 0)


def is_tuned(lz, rows_piece, col_parts):
    return lz == 4 and rows_piece == 256 and col_parts == 4


def grid_copies(tuned, far_side, near_side, row_ids, col_ids, rows_piece, outward, sem):
    if not tuned:
        src, dst = (near_side, far_side) if outward else (far_side, near_side)
        pltpu.make_async_copy(src, dst, sem).start()
        return

    def one(k):
        i, j = k // 4, lax.rem(k, 4)

        def at(ref, row, col):
            return ref.at[
                pl.ds(pl.multiple_of(row * rows_piece, rows_piece), rows_piece),
                pl.ds(pl.multiple_of(col * rows_piece, rows_piece), rows_piece),
            ]

        here, there = at(near_side, i, j), at(far_side, pick(row_ids, i), pick(col_ids, j))
        src, dst = (here, there) if outward else (there, here)
        pltpu.make_async_copy(src, dst, sem).start()

    over(0, 32, one)


def main_kernel(
    ly, lz, group,
    diag_in, top_in, pheno_in, panel_in, trailing_in, geno_in, rest_in,
    u_out, white_out, own_out, total_out, row_hi, row_lo, y_hi, y_lo,
    a_ref, m_ref, w_ref, row_buf, col_buf, top_buf, pheno_buf, rest_buf,
    g_hi, g_lo, w_hi, w_lo, wt_hi, wt_lo, ai_hi, ai_lo,
    stat, stat_buf,
    small_send, small_recv, row_send, row_recv, col_send, col_recv, stat_send, stat_recv, local_sem,
    fine_send, fine_recv, fine_col_send, fine_col_recv, fine_local,
):
    r, c = lax.axis_index("prow"), lax.axis_index("pcol")
    z, y = c // ly, lax.rem(c, ly)
    sib = r + 1 - 2 * lax.rem(r, 2)
    cross = r + 2 - 4 * (r // 2)
    diag_x = sib + 2 - 4 * (sib // 2)
    other = z * ly + (1 - y)
    rows_piece, width = panel_in.shape
    half = rows_piece // 2
    pieces = row_buf.shape[0] // rows_piece
    variants = top_in.shape[1]
    col_parts = col_buf.shape[0] // rows_piece
    root = c // group
    first = lax.rem(c, group) * col_parts
    is_root = root == r
    root_cross = root + 2 - 4 * (root // 2)
    low_end, high_end = z == 0, z == lz - 1
    tuned = is_tuned(lz, rows_piece, col_parts)
    far, row_ids, col_ids = orders(ly, lz, first, z, y) if tuned else (None, None, None)

    barrier = pltpu.get_barrier_semaphore()

    def greet(row, col):
        pl.semaphore_signal(barrier, inc=1, device_id={"prow": row, "pcol": col}, device_id_type=MESH)

    greet(sib, c)
    greet(cross, c)
    greet(diag_x, c)
    greet(r, other)

    @pl.when(z > 0)
    def _():
        greet(r, c - ly)

    @pl.when(z < lz - 1)
    def _():
        greet(r, c + ly)

    pl.semaphore_wait(barrier, 4 + jnp.minimum(z, 1) + jnp.minimum(lz - 1 - z, 1))

    def remote(src, dst, send, recv, row, col):
        return pltpu.make_async_remote_copy(
            src_ref=src, dst_ref=dst, send_sem=send, recv_sem=recv,
            device_id={"prow": row, "pcol": col}, device_id_type=MESH,
        )

    def each(items, act):
        for item in items:
            if item[0] is True:
                act(item)
            elif item[0] is not False:
                pl.when(item[0])(functools.partial(act, item))

    def start_all(sends):
        each(sends, lambda item: item[1]().start())

    def sent_all(sends):
        each(sends, lambda item: item[1]().wait_send())

    height = diag_in.shape[0]
    side = 2 * height
    mine, theirs = (r // 2) * side, (cross // 2) * side

    def band(q):
        return pl.ds(pl.multiple_of(q * height, height), height)

    def half_cols(start, kind):
        return pl.ds(pl.multiple_of(start + (height if kind == 3 else 0), height), height)

    def small(kind, lane):
        part = cross if lane == 2 else r
        if kind in (0, 3):
            if lane == 0:
                src, dst = diag_in, a_ref.at[band(r), :]
            else:
                cols = half_cols(theirs if lane == 2 else mine, kind)
                dst = a_ref.at[band(part), cols]
                src = dst if lane == 2 else diag_in.at[:, cols]
        else:
            buf = (None, top_buf, pheno_buf)[kind]
            dst = buf.at[part]
            src = dst if lane == 2 else (None, top_in, pheno_in)[kind]
        return remote(
            src, dst, small_send.at[kind, lane], small_recv.at[kind, part],
            cross if lane == 1 else sib, c,
        )

    def small_wait(kind, part):
        if kind in (0, 3):
            dst = a_ref.at[band(part), :]
            if part is not sib:
                dst = a_ref.at[band(part), half_cols(theirs, kind)]
        else:
            dst = (None, top_buf, pheno_buf)[kind].at[part]
        remote(dst, dst, small_send.at[kind, 0], small_recv.at[kind, part], sib, c).wait_recv()

    def chunk(b, h):
        return row_buf.at[pl.ds(pl.multiple_of((2 * b + h) * half, half), half), :]

    def own_half(h):
        return panel_in.at[pl.ds(h * half, half), :]

    def row_copy(way, b, h, own=False):
        target = (c + ly, c - ly, other)[way]
        return lambda: remote(
            own_half(h) if own else chunk(b, h), chunk(b, h),
            row_send.at[way, 2 * b + h], row_recv.at[2 * b + h], r, target,
        )

    def row_wait(b, h):
        remote(chunk(b, h), chunk(b, h), row_send.at[0, 0], row_recv.at[2 * b + h], r, other).wait_recv()

    def col_at(i, h):
        return col_buf.at[pl.ds(pl.multiple_of((2 * i + h) * half, half), half), :]

    def col_copies(b, h, own):
        i = b - first
        src = own_half(h) if own else chunk(b, h)
        k = 2 * i + h
        return (
            remote(src, col_at(i, h), col_send.at[0, k], col_recv.at[k], cross, c),
            remote(src, col_at(i, h), col_send.at[1, k], col_recv.at[k], sib, c),
            pltpu.make_async_copy(src, col_at(i, h), local_sem.at[k]),
        )

    def col_start(b, h, own=False):
        @pl.when(is_root & (b >= first) & (b < first + col_parts))
        def _():
            for copy in col_copies(b, h, own):
                copy.start()

    def part(ref, b, h, p):
        rows = half // FINE
        return ref.at[pl.ds(pl.multiple_of((2 * b + h) * half + p * rows, rows), rows), :]

    def fine_copies(way, b, h):
        target = (c + ly, c - ly, other)[way]

        def one(p):
            return lambda: remote(
                part(row_buf, b, h, p), part(row_buf, b, h, p), fine_send.at[h, p], fine_recv.at[h, p], r, target
            )

        return [one(p) for p in range(FINE)]

    last_piece = jnp.where(low_end, (lz - 1) * ly, 0) + 1 - y

    def fine_col(h, p):
        src, dst = part(row_buf, last_piece, h, p), part(col_buf, last_piece - first, h, p)
        return (
            remote(src, dst, fine_col_send.at[0, h, p], fine_col_recv.at[h, p], cross, c),
            remote(src, dst, fine_col_send.at[1, h, p], fine_col_recv.at[h, p], sib, c),
            pltpu.make_async_copy(src, dst, fine_local.at[h, p]),
        )

    def fine_handed(h, p):
        dst = part(col_buf, last_piece - first, h, p)
        return remote(dst, dst, fine_col_send.at[1, h, p], fine_col_recv.at[h, p], sib, c)

    def fine_arrive():
        for p in range(FINE):
            for h in (1, 0):
                dst = part(row_buf, last_piece, h, p)
                remote(dst, dst, fine_send.at[h, p], fine_recv.at[h, p], r, other).wait_recv()

                @pl.when(is_root & far)
                def _():
                    for copy in fine_col(h, p):
                        copy.start()

    def fine_hand():
        for p in range(FINE):
            for h in (1, 0):
                fine_handed(h, p).wait_recv()
                fine_handed(h, p).start()

    def fine_ready():
        for p in range(FINE):
            for h in (1, 0):

                @pl.when(is_root)
                def _():
                    fine_col(h, p)[2].wait()

                @pl.when(jnp.logical_not(is_root) & (r != root_cross))
                def _():
                    fine_handed(h, p).wait_recv()

    def fine_sent():
        for p in range(FINE):
            for h in (1, 0):

                @pl.when(is_root)
                def _():
                    for copy in fine_col(h, p)[:2]:
                        copy.wait_send()

                @pl.when(r == root_cross)
                def _():
                    fine_handed(h, p).wait_send()

    def own_sends(h):
        return [
            (True, row_copy(2, c, h, True)),
            (z < lz - 1, row_copy(0, c, h, True)),
            (z > 0, row_copy(1, c, h, True)),
        ]

    def hop_arrivals(d, h):
        low, high = c - d * ly, c + d * ly
        low_over = True if h == 0 else z != d
        high_over = True if h == 0 else z + d != lz - 1
        low_across, high_across = [(low_over, row_copy(2, low, h))], [(high_over, row_copy(2, high, h))]
        if tuned and d == lz - 1 and h == 0:
            low_across = [(True, copy) for copy in fine_copies(2, low, h)]
            high_across = [(True, copy) for copy in fine_copies(2, high, h)]
        return [
            (z >= d, low, h, [(z < lz - 1, row_copy(0, low, h))] + low_across),
            (z + d < lz, high, h, [(z > 0, row_copy(1, high, h))] + high_across),
        ]

    def across_arrivals(d, h):
        if d == 0:
            sends = []
            if h == 1 and lz > 1:
                sends = [(low_end, row_copy(0, other, h)), (high_end, row_copy(1, other, h))]
            return [(True, other, h, sends)]
        return [
            (z >= d if h == 0 else z > d, other - d * ly, h, []),
            (z + d < lz if h == 0 else z + d < lz - 1, other + d * ly, h, []),
        ]

    def far_arrivals(d):
        low, high = 1 - y, (lz - 1) * ly + 1 - y
        ups, downs = [row_copy(0, low, 1)], [row_copy(1, high, 1)]
        if tuned and d == lz - 2:
            ups, downs = fine_copies(0, low, 1), fine_copies(1, high, 1)
        return [
            (z == d, low, 1, [(z < lz - 1, copy) for copy in ups]),
            (z == lz - 1 - d, high, 1, [(z > 0, copy) for copy in downs]),
        ]

    def arrive(items):
        def act(item):
            _, b, h, sends = item
            row_wait(b, h)
            start_all(sends)
            col_start(b, h)

        each(items, act)

    def finish(items):
        each(items, lambda item: sent_all(item[3]))

    small(0, 1).start()
    small(0, 0).start()
    small(3, 1).start()
    diag_copy = pltpu.make_async_copy(diag_in, a_ref.at[band(r), :], local_sem.at[2 * col_parts])
    diag_copy.start()
    for h in range(2):
        start_all(own_sends(h))
    for kind in (1, 2):
        small(kind, 1).start()
        small(kind, 0).start()
    own_copies = [
        pltpu.make_async_copy(own_half(h), chunk(c, h), local_sem.at[2 * col_parts + 1 + h]) for h in range(2)
    ]
    others = [
        pltpu.make_async_copy(src, dst, local_sem.at[2 * col_parts + 3 + k])
        for k, (src, dst) in enumerate((
            (top_in, top_buf.at[r]), (pheno_in, pheno_buf.at[r]), (rest_in, rest_buf),
            (geno_in, white_out),
        ))
    ]
    for copy in own_copies + others:
        copy.start()
    for h in range(2):
        col_start(c, h, True)
    trailing_sem = local_sem.at[2 * col_parts + 7]
    grid_copies(tuned, trailing_in, u_out, row_ids, col_ids, rows_piece, False, trailing_sem)
    others.append(pltpu.make_async_copy(trailing_in, u_out, trailing_sem))
    small_wait(0, cross)
    small(0, 2).start()
    small_wait(0, sib)
    small_wait(0, diag_x)
    diag_copy.wait()

    def diag_event():
        small_wait(3, cross)
        small(3, 2).start()

    def corner_event():
        small_wait(3, diag_x)
        small(0, 2).wait_send()
        small(3, 2).wait_send()

        @pl.when(r >= 2)
        def _():
            a_ref[:side, side:] = jnp.transpose(a_ref[side:, :side])

    def top_event():
        for kind in (1, 2):
            small_wait(kind, cross)
            small(kind, 2).start()

    def nothing():
        pass

    last = 2 * (lz - 1)

    def event(t):
        def run():
            if t <= last:
                arrive(hop_arrivals((t + 1) // 2, (t - 1) % 2))
            if t % 2 == 1 and t // 2 >= 1:
                arrive(far_arrivals(t // 2))
            if t == 2:
                arrive(across_arrivals(0, 0))
                arrive(across_arrivals(0, 1))
            if t >= 4 and (t - 2) // 2 < lz:
                arrive(across_arrivals((t - 2) // 2, t % 2))

        return run

    count = 2 * lz
    events = [nothing] * 16
    events[0], events[2], events[3] = diag_event, corner_event, event(1)
    events[4], events[7] = top_event, event(2)
    events[11], events[15] = event(3), event(4)
    invert(a_ref, w_ref, m_ref, events)

    def prepare():
        for kind in (1, 2):
            small_wait(kind, sib)
            small_wait(kind, diag_x)
        for copy in own_copies + others:
            copy.wait()
        whole = w_ref[...]
        w_hi[...], w_lo[...] = split2(whole)
        wt_hi[...], wt_lo[...] = split2(jnp.transpose(whole))
        w, turned = (w_hi[...], w_lo[...]), (wt_hi[...], wt_lo[...])
        ai_hi[...], ai_lo[...] = split2(dot3(turned, w, INNER))
        phenos = jnp.concatenate([pheno_buf[q] for q in range(pheno_buf.shape[0])], axis=1)
        joined = jnp.concatenate([top_buf[...].reshape(width, variants), column(phenos)], axis=1)
        both = dot3(w, split2(joined), INNER)
        g_hi[...], g_lo[...] = split2(dot3(turned, split2(both), INNER))
        white = both[:, :variants]
        stat[...] = jnp.zeros_like(stat)
        stat[2:3, :] = weighted(both[:, variants:], white)
        stat[3:4, :] = jnp.sum(white * white, axis=0, keepdims=True)
        at = pl.ds(pl.multiple_of(c * rows_piece, rows_piece), rows_piece)
        own_out[...] = dot3(split2(row_buf[at, :]), (wt_hi[...], wt_lo[...]), INNER)

    unit = rest_buf.shape[2]
    units = row_buf.shape[0] // unit
    col_unit = min(col_parts, max(1, 256 // rows_piece))
    col_units = col_parts // col_unit
    col_wide = col_unit * rows_piece

    def place(b):
        return pl.ds(pl.multiple_of(b * unit, unit), unit)

    def row_step(k, b):
        at, slot = place(b), place(k)
        parts = split2(row_buf[at, :])
        row_hi[slot, :], row_lo[slot, :] = parts
        shift = dot3(parts, (g_hi[...], g_lo[...]), INNER)
        white = white_out[at, :] - shift[:, :variants]
        white_out[at, :] = white
        stat[0:1, :] += weighted(column(rest_buf[b]) - shift[:, variants:], white)
        stat[1:2, :] += jnp.sum(white * white, axis=0, keepdims=True)

    def cols_of(q, count=1):
        return pl.ds(pl.multiple_of(q * col_wide, col_wide), col_wide * count)

    def product(k, many, q, count):
        slots = pl.ds(pl.multiple_of(k * unit, unit), unit * many)
        cols = cols_of(q, count)
        return dot3((row_hi[slots, :], row_lo[slots, :]), (y_hi[:, cols], y_lo[:, cols]), INNER)

    def col_ready(i, h):
        @pl.when(is_root)
        def _():
            pltpu.make_async_copy(col_at(i, h), col_at(i, h), local_sem.at[2 * i + h]).wait()

        @pl.when(jnp.logical_not(is_root))
        def _():
            handed = remote(col_at(i, h), col_at(i, h), col_send.at[1, 2 * i + h], col_recv.at[2 * i + h], sib, c)
            handed.wait_recv()
            pl.when(r == root_cross)(handed.start)

    def cols_ready(unit_at):
        for i in range(col_unit):
            for h in range(2):
                col_ready(unit_at * col_unit + i, h)

    def col_step(q, unit_at, waits=True):
        if waits:
            cols_ready(unit_at)
        y_hi[:, cols_of(q)], y_lo[:, cols_of(q)] = split2(
            dot3((ai_hi[...], ai_lo[...]), split2(col_buf[cols_of(unit_at), :]), LAST)
        )

    def send_stats():
        stat_buf[r] = stat[...]
        for k, target in enumerate((sib, cross, diag_x)):
            remote(stat, stat_buf.at[r], stat_send.at[k], stat_recv.at[r], target, c).start()

    if tuned:
        near = jnp.logical_not(far)

        def apply(k, many, q, count):
            u_out[pl.ds(pl.multiple_of(k * unit, unit), unit * many), cols_of(q, count)] -= product(k, many, q, count)

        def only(cond, items):
            return [(cond if item[0] is True else item[0] & cond,) + tuple(item[1:]) for item in items]

        def first_stage():
            arrive(across_arrivals(1, 1))
            arrive(hop_arrivals(3, 0))
            arrive(far_arrivals(2))
            arrive(only(low_end | high_end, across_arrivals(2, 0)))

        def second_stage():
            arrive(only((z > 0) & (z < lz - 1), across_arrivals(2, 0)))
            arrive(hop_arrivals(3, 1))
            arrive(across_arrivals(2, 1))

        def last_rows():
            pl.when((low_end | high_end) & near)(fine_arrive)
            row_step(7, row_ids[7])
            send_stats()

        def last_column():
            spare()
            fine_ready()

        def spare():
            def one(k):
                pl.when((k == 7) & (r == root_cross))(fine_hand)
                apply(k, 1, 0, 2)

            over(4, 8, one)

        def stage(t):
            pl.when(t == 1)(second_stage)
            pl.when((t == 2) & far & (low_end | high_end))(fine_arrive)
            pl.when(t < 3)(lambda: row_step(4 + t, pick(row_ids, 4 + t)))
            pl.when(((t == 3) & near) | ((t == 2) & far))(last_rows)
            unit_at = pick(col_ids, t)
            pl.when((t < 3) | near)(lambda: cols_ready(unit_at))
            pl.when((t == 3) & far)(last_column)
            col_step(t, unit_at, False)
            pl.when((t < 3) | near)(lambda: apply(0, 4, t, 1))

        prepare()
        first_stage()
        over(0, 4, lambda k: row_step(k, pick(row_ids, k)))
        over(0, 4, stage)
    else:
        for t in range(5, count + 2):
            event(t)()
        prepare()

        def apply(k):
            over(0, col_units, lambda q: apply_one(k, q))

        def apply_one(k, q):
            u_out[place(k), cols_of(q)] -= product(k, 1, q, 1)

        over(0, col_units, lambda q: col_step(q, q))
        over(0, units, lambda k: row_step(k, k))
        send_stats()
        over(0, units, apply)

    for k, source in enumerate((sib, cross, diag_x)):
        remote(stat, stat_buf.at[source], stat_send.at[k], stat_recv.at[source], sib, c).wait_recv()
    total = stat_buf[0]
    for q in range(1, stat_buf.shape[0]):
        total = total + stat_buf[q]
    people = jnp.float32(width + row_buf.shape[0] * stat_buf.shape[0])
    total_out[...] = jnp.zeros_like(total_out)
    total_out[0:1, :] = (total[0:1] + stat[2:3, :]) / jnp.sqrt(people)
    total_out[1:2, :] = (total[1:2] + stat[3:4, :]) / people

    for k in range(3):
        remote(stat, stat_buf.at[r], stat_send.at[k], stat_recv.at[r], sib, c).wait_send()
    for lane in range(2):
        small(0, lane).wait_send()
    small(3, 1).wait_send()
    for kind in (1, 2):
        for lane in range(3):
            small(kind, lane).wait_send()
    for h in range(2):
        sent_all(own_sends(h))
    finish(across_arrivals(0, 1))
    for d in range(1, lz):
        for h in range(2):
            finish(hop_arrivals(d, h))
        finish(far_arrivals(d))

    skip = jnp.where(far, last_piece - first, col_parts) if tuned else col_parts

    def sent(k):
        def act():
            for h in range(2):
                handed = remote(
                    col_at(k, h), col_at(k, h), col_send.at[1, 2 * k + h], col_recv.at[0], sib, c
                )
                pl.when(is_root | (r == root_cross))(handed.wait_send)
                over_x = remote(
                    col_at(k, h), col_at(k, h), col_send.at[0, 2 * k + h], col_recv.at[0], sib, c
                )
                pl.when(is_root)(over_x.wait_send)

        pl.when(k != skip)(act)

    over(0, col_parts, sent)
    if tuned:
        pl.when(far)(fine_sent)


def store_kernel(
    ly, lz, group,
    u_in, white_in, own_in, total_in, row_hi, row_lo, y_hi, y_lo,
    u_out, white_out, own_out, score_out, info_out,
    held, sem, row_sem,
):
    c = lax.axis_index("pcol")
    rows_piece = own_in.shape[0]
    col_parts = u_in.shape[1] // rows_piece
    tuned = is_tuned(lz, rows_piece, col_parts)
    pairs = [(own_in, own_out), (white_in, white_out)]
    pairs += [(total_in.at[0:1], score_out), (total_in.at[1:2], info_out)]
    copies = [pltpu.make_async_copy(src, dst, sem.at[1 + k]) for k, (src, dst) in enumerate(pairs)]
    if not tuned:
        copies.append(pltpu.make_async_copy(u_in, u_out, sem.at[0]))
        for copy in copies:
            copy.start()
        for copy in copies:
            copy.wait()
        return
    far, row_ids, col_ids = orders(ly, lz, lax.rem(c, group) * col_parts, c // ly, lax.rem(c, ly))
    near = jnp.logical_not(far)

    def span(k):
        return pl.ds(pl.multiple_of(k * rows_piece, rows_piece), rows_piece)

    def store_row(k, src, at, row_at, cols=range(4)):
        for j in cols:
            pltpu.make_async_copy(
                src.at[span(at), span(j)], u_out.at[span(pick(row_ids, k)), span(col_ids[j])], row_at
            ).start()

    over(0, 4, lambda k: store_row(k, u_in, k, row_sem.at[k], range(3)))
    pl.when(near)(lambda: over(0, 4, lambda k: store_row(k, u_in, k, row_sem.at[k], (3,))))
    for copy in copies:
        copy.start()

    pl.when(far)(lambda: over(4, 8, lambda k: store_row(k, u_in, k, row_sem.at[k], (0, 1))))

    def later(k, start):
        at, cols = span(k), pl.ds(start * rows_piece, (4 - start) * rows_piece)
        moved = dot3((row_hi[at, :], row_lo[at, :]), (y_hi[:, cols], y_lo[:, cols]), INNER)
        held[span(k - 4), cols] = u_in[at, cols] - moved
        store_row(k, held, k - 4, row_sem.at[k], range(start, 4))

    def corner(k):
        at, cols = span(k), pl.ds(3 * rows_piece, rows_piece)
        moved = dot3((row_hi[at, :], row_lo[at, :]), (y_hi[:, cols], y_lo[:, cols]), INNER)
        held[at, :rows_piece] = u_in[at, cols] - moved
        pltpu.make_async_copy(
            held.at[at, pl.ds(0, rows_piece)], u_out.at[span(pick(row_ids, k)), span(col_ids[3])], row_sem.at[k]
        ).start()

    pl.when(far)(lambda: over(0, 4, corner))
    pl.when(near)(lambda: over(4, 8, lambda k: later(k, 0)))
    pl.when(far)(lambda: over(4, 8, lambda k: later(k, 2)))
    for copy in copies:
        copy.wait()
    over(0, 8, lambda k: pltpu.make_async_copy(held.at[span(0), :], u_out.at[span(0), :], row_sem.at[k]).wait())


def local(diag_block, panel_cols, trailing, geno_top, geno_rest, pheno_top, pheno_rest):
    prow_size, pcol_size = lax.axis_size("prow"), lax.axis_size("pcol")
    height, width = diag_block.shape
    rows_piece = panel_cols.shape[0]
    row_count, col_count = trailing.shape
    variants = geno_top.shape[1]
    ly = 2
    lz = pcol_size // ly
    unit = min(row_count, max(rows_piece, 256))
    chunks, col_chunks = 2 * pcol_size, 2 * (col_count // rows_piece)
    f32, bf16 = jnp.float32, jnp.bfloat16
    vmem = pl.BlockSpec(memory_space=pltpu.VMEM)
    hbm = pl.BlockSpec(memory_space=pltpu.HBM)
    dma = pltpu.SemaphoreType.DMA
    wide = variants + BLOCK
    stats = (8, variants)
    arrays = [
        ((width, width), f32), ((BLOCK, 2 * BLOCK), f32), ((width, width), f32),
        ((row_count, width), f32), ((col_count, width), f32),
        ((prow_size, height, variants), f32), ((prow_size, 1, height), f32),
        ((row_count // unit, 1, unit), f32),
        ((width, wide), bf16), ((width, wide), bf16),
    ]
    arrays += [((width, width), bf16)] * 6
    arrays += [(stats, f32), ((prow_size,) + stats, f32)]
    held = pl.pallas_call(
        functools.partial(main_kernel, ly, lz, pcol_size // prow_size),
        out_shape=(
            pltpu.VMEM(trailing.shape, f32),
            pltpu.VMEM(geno_rest.shape, f32),
            pltpu.VMEM(panel_cols.shape, f32),
            pltpu.VMEM(stats, f32),
            pltpu.VMEM((row_count, width), bf16),
            pltpu.VMEM((row_count, width), bf16),
            pltpu.VMEM((width, col_count), bf16),
            pltpu.VMEM((width, col_count), bf16),
        ),
        in_specs=[hbm] * 7,
        out_specs=(vmem,) * 8,
        scratch_shapes=[pltpu.VMEM(shape, dtype) for shape, dtype in arrays]
        + [
            dma((4, 3)), dma((4, prow_size)), dma((3, chunks)), dma((chunks,)),
            dma((2, col_chunks)), dma((col_chunks,)), dma((3,)), dma((prow_size,)), dma((col_chunks + 9,)),
            dma((2, FINE)), dma((2, FINE)), dma((2, 2, FINE)), dma((2, FINE)), dma((2, FINE)),
        ],
        compiler_params=pltpu.CompilerParams(
            collective_id=0, has_side_effects=True, vmem_limit_bytes=32 * 1024 * 1024
        ),
    )(
        *(pltpu.with_memory_space_constraint(value, pltpu.HBM) for value in (
            diag_block, geno_top, pheno_top.reshape(1, height), panel_cols, trailing, geno_rest,
            pheno_rest.reshape(row_count // unit, 1, unit),
        ))
    )
    updated_block, own_factor, white_geno, score, info = order(pl.pallas_call(
        functools.partial(store_kernel, ly, lz, pcol_size // prow_size),
        out_shape=(
            jax.ShapeDtypeStruct(trailing.shape, f32),
            jax.ShapeDtypeStruct(geno_rest.shape, f32),
            jax.ShapeDtypeStruct(panel_cols.shape, f32),
            jax.ShapeDtypeStruct((1, variants), f32),
            jax.ShapeDtypeStruct((1, variants), f32),
        ),
        in_specs=[vmem] * 8,
        out_specs=(hbm,) * 5,
        scratch_shapes=[
            pltpu.VMEM((row_count // 2, col_count), f32), dma((5,)), dma((8,)),
        ],
        compiler_params=pltpu.CompilerParams(vmem_limit_bytes=12 * 1024 * 1024),
    )(*(pltpu.with_memory_space_constraint(value, pltpu.VMEM) for value in held)))
    return (updated_block, own_factor, white_geno, score.reshape(variants), info.reshape(variants))


def order(values):
    updated, white, own, score, info = values
    return updated, own, white, score, info


def solution(mesh):
    placed = (
        P("prow", None),
        P(("prow", "pcol"), None),
        P("prow", "pcol"),
        P("prow", "pcol"),
        P("prow", "pcol"),
        P("prow"),
        P("prow"),
    )
    return jax.shard_map(
        local,
        mesh=mesh,
        in_specs=placed,
        out_specs=(
            P("prow", "pcol"),
            P(("prow", "pcol"), None),
            P("prow", "pcol"),
            P("pcol"),
            P("pcol"),
        ),
        check_vma=False,
    )
```

```python
import functools

import jax
import jax.numpy as jnp
from jax import lax
from jax.experimental import pallas as pl
from jax.experimental.pallas import tpu as pltpu
from jax.sharding import PartitionSpec as P

MESH = pl.DeviceIdType.MESH
HIGHEST = lax.Precision.HIGHEST
TILE = 16
FINE = 4
PARTS = 4
BLOCK = 128


def split3(value):
    hi = value.astype(jnp.bfloat16).astype(jnp.float32)
    rest = value - hi
    mid = rest.astype(jnp.bfloat16).astype(jnp.float32)
    return hi, mid, rest - mid


def tile_step(m_ref, step):
    start = pl.multiple_of(step * TILE, TILE)
    half = TILE // 2
    left = m_ref[pl.ds(start, TILE), :BLOCK]
    right = m_ref[pl.ds(start, TILE), BLOCK:]
    rolled = pltpu.roll(left, lax.rem(BLOCK - start, BLOCK), 1)
    rows = lax.broadcasted_iota(jnp.int32, (half, BLOCK), 0)
    lanes = lax.broadcasted_iota(jnp.int32, (TILE, BLOCK), 1)

    def halves(value):
        return [value[:half], value[half:]]

    def spread(parts, j):
        part, at = parts[j // half], j % half
        return jnp.broadcast_to(part[at : at + 1, :], (half, BLOCK))

    cols = [halves(jnp.broadcast_to(rolled[:, k : k + 1], (TILE, BLOCK))) for k in range(TILE)]
    values = [halves(left), halves(right)]
    pivots = [jnp.zeros((half, BLOCK), jnp.float32) for _ in range(2)]
    def inverse(value):
        inv = pl.reciprocal(value, approx=True)
        return inv * (2.0 - value * inv)

    for j in range(0, TILE, 2):
        own, low = j // half, j % half
        one, two = cols[j], cols[j + 1]
        p, b, c = spread(one, j), spread(one, j + 1), spread(two, j + 1)
        det = p * c - b * b
        inv_p, inv_det = inverse(p), inverse(det)
        ratio = b * inv_p
        pivots[own] = jnp.where(rows == low, p, jnp.where(rows == low + 1, det * inv_p, pivots[own]))
        lead, tail, after = {}, {}, [None, None]
        for part in range(own, 2):
            after[part] = two[part] - ratio * one[part]
            lead[part] = one[part] * inv_p
            tail[part] = (p * two[part] - b * one[part]) * inv_det
            if part == own:
                lead[part] = jnp.where(rows > low, lead[part], 0.0)
                tail[part] = jnp.where(rows > low + 1, tail[part], 0.0)
        for k in range(j + 2, TILE):
            top, under = spread(one, k), spread(after, k)
            for part in lead:
                if part >= k // half:
                    cols[k][part] = (cols[k][part] - lead[part] * top) - tail[part] * under
        for value in values:
            top = spread(value, j)
            under = spread(value, j + 1) - ratio * top
            for part in lead:
                value[part] = (value[part] - lead[part] * top) - tail[part] * under
    left, right = (jnp.concatenate(value, axis=0) for value in values)
    pivots = jnp.concatenate(pivots, axis=0)
    scale = lax.rsqrt(pivots)
    scale = scale * (1.5 - (0.5 * pivots) * scale * scale)
    left, right = left * scale, right * scale
    m_ref[pl.ds(start, TILE), :BLOCK] = left
    m_ref[pl.ds(start, TILE), BLOCK:] = right
    both = jnp.concatenate([left, right], axis=1)
    mult = jnp.where(lanes >= start + TILE, left, 0.0)
    a0, a1, a2 = split3(mult)
    b0, b1, b2 = split3(both)
    lhs = jnp.concatenate([a0, a0, a1, a0, a1, a2], axis=0).astype(jnp.bfloat16)
    rhs = jnp.concatenate([b0, b1, b0, b2, b1, b0], axis=0).astype(jnp.bfloat16)
    m_ref[...] -= lax.dot_general(
        lhs, rhs, (((0,), (0,)), ((), ())), preferred_element_type=jnp.float32
    )


def dot_t(a, b):
    return lax.dot_general(
        a, b, (((0,), (0,)), ((), ())), precision=HIGHEST, preferred_element_type=jnp.float32
    )


def dot_n(a, b):
    return jnp.dot(a, b, precision=HIGHEST, preferred_element_type=jnp.float32)


def invert(a_ref, w_ref, m_ref, events):
    width = a_ref.shape[0]
    blocks = width // BLOCK
    tiles = BLOCK // TILE
    w_ref[...] = jnp.zeros_like(w_ref)
    eye = (
        lax.broadcasted_iota(jnp.int32, (BLOCK, BLOCK), 0)
        == lax.broadcasted_iota(jnp.int32, (BLOCK, BLOCK), 1)
    ).astype(jnp.float32)
    slot = 0
    for k in range(blocks):
        lo, hi = k * BLOCK, (k + 1) * BLOCK
        m_ref[:, :BLOCK] = a_ref[lo:hi, lo:hi]
        m_ref[:, BLOCK:] = eye
        for part in range(PARTS):

            def body(step, carry):
                tile_step(m_ref, step)
                return carry

            lax.fori_loop(part * tiles // PARTS, (part + 1) * tiles // PARTS, body, 0)
            if part < PARTS - 1:
                if slot < len(events):
                    events[slot]()
                slot += 1
        own = m_ref[:, BLOCK:]
        if k > 0:
            w_ref[lo:hi, :lo] = dot_n(own, w_ref[lo:hi, :lo])
        w_ref[lo:hi, lo:hi] = own
        if k < blocks - 1:
            upper = dot_n(own, a_ref[lo:hi, hi:])
            a_ref[hi:, hi:] -= dot_t(upper, upper)
            w_ref[hi:, :hi] -= dot_t(upper, w_ref[lo:hi, :hi])
        if slot < len(events):
            events[slot]()
        slot += 1
    while slot < len(events):
        events[slot]()
        slot += 1


LAST = ((1,), (1,))
INNER = ((1,), (0,))


def split2(value):
    hi = value.astype(jnp.bfloat16)
    return hi, (value - hi.astype(jnp.float32)).astype(jnp.bfloat16)


def dot3(a, b, dims):
    left = jnp.concatenate([a[0], a[0], a[1]], axis=dims[0][0])
    right = jnp.concatenate([b[0], b[1], b[0]], axis=dims[1][0])
    return lax.dot_general(left, right, (dims, ((), ())), preferred_element_type=jnp.float32)


def column(row):
    return jnp.transpose(jnp.broadcast_to(row, (BLOCK, row.shape[1])))


def weighted(weights, values):
    wide = jnp.concatenate([weights] * (values.shape[1] // BLOCK), axis=1)
    return jnp.sum(wide * values, axis=0, keepdims=True)


def orders(ly, lz, first, z, y):
    low_end, high_end = z == 0, z == lz - 1
    far = (low_end & (y == 1)) | (high_end & (y == 0))

    def nearest(k):
        near = jnp.minimum(z, lz - 1 - z)
        step = (k + 1) // 2
        zigzag = z + (step if k % 2 == 1 else -step)
        onward = jnp.where(z < lz - 1 - z, k, lz - 1 - k)
        return jnp.where(k <= 2 * near, zigzag, onward)

    def row(k, turned):
        return nearest(k) * ly + (1 - y if turned else y)

    row_ids = [
        row(0, False), row(0, True), row(1, False), row(2, False),
        row(1, True), row(3, False), row(2, True), row(3, True),
    ]
    flip = first // ly + 1 <= z
    col_ids = [
        jnp.where(flip, 1 - q % 2, q % 2) * ly + (y if q // 2 == 0 else 1 - y) for q in range(4)
    ]
    return far, row_ids, col_ids


def pick(values, k):
    out = values[-1]
    for j in range(len(values) - 2, -1, -1):
        out = jnp.where(k == j, values[j], out)
    return out


def over(lo, hi, fn):
    def body(k, carry):
        fn(k)
        return carry

    lax.fori_loop(lo, hi, body, 0)


def is_tuned(lz, rows_piece, col_parts):
    return lz == 4 and rows_piece == 256 and col_parts == 4


def grid_copies(tuned, far_side, near_side, row_ids, col_ids, rows_piece, outward, sem):
    if not tuned:
        src, dst = (near_side, far_side) if outward else (far_side, near_side)
        pltpu.make_async_copy(src, dst, sem).start()
        return

    def one(k):
        i, j = k // 4, lax.rem(k, 4)

        def at(ref, row, col):
            return ref.at[
                pl.ds(pl.multiple_of(row * rows_piece, rows_piece), rows_piece),
                pl.ds(pl.multiple_of(col * rows_piece, rows_piece), rows_piece),
            ]

        here, there = at(near_side, i, j), at(far_side, pick(row_ids, i), pick(col_ids, j))
        src, dst = (here, there) if outward else (there, here)
        pltpu.make_async_copy(src, dst, sem).start()

    over(0, 32, one)


def main_kernel(
    ly, lz, group,
    diag_in, top_in, pheno_in, panel_in, trailing_in, geno_in, rest_in,
    u_out, white_out, own_out, total_out, row_hi, row_lo, y_hi, y_lo,
    a_ref, m_ref, w_ref, row_buf, col_buf, top_buf, pheno_buf, rest_buf,
    g_hi, g_lo, w_hi, w_lo, wt_hi, wt_lo, ai_hi, ai_lo,
    stat, stat_buf,
    small_send, small_recv, row_send, row_recv, col_send, col_recv, stat_send, stat_recv, local_sem,
    fine_send, fine_recv, fine_col_send, fine_col_recv, fine_local,
):
    r, c = lax.axis_index("prow"), lax.axis_index("pcol")
    z, y = c // ly, lax.rem(c, ly)
    sib = r + 1 - 2 * lax.rem(r, 2)
    cross = r + 2 - 4 * (r // 2)
    diag_x = sib + 2 - 4 * (sib // 2)
    other = z * ly + (1 - y)
    rows_piece, width = panel_in.shape
    half = rows_piece // 2
    pieces = row_buf.shape[0] // rows_piece
    variants = top_in.shape[1]
    col_parts = col_buf.shape[0] // rows_piece
    root = c // group
    first = lax.rem(c, group) * col_parts
    is_root = root == r
    root_cross = root + 2 - 4 * (root // 2)
    low_end, high_end = z == 0, z == lz - 1
    tuned = is_tuned(lz, rows_piece, col_parts)
    far, row_ids, col_ids = orders(ly, lz, first, z, y) if tuned else (None, None, None)

    barrier = pltpu.get_barrier_semaphore()

    def greet(row, col):
        pl.semaphore_signal(barrier, inc=1, device_id={"prow": row, "pcol": col}, device_id_type=MESH)

    greet(sib, c)
    greet(cross, c)
    greet(diag_x, c)
    greet(r, other)

    @pl.when(z > 0)
    def _():
        greet(r, c - ly)

    @pl.when(z < lz - 1)
    def _():
        greet(r, c + ly)

    pl.semaphore_wait(barrier, 4 + jnp.minimum(z, 1) + jnp.minimum(lz - 1 - z, 1))

    def remote(src, dst, send, recv, row, col):
        return pltpu.make_async_remote_copy(
            src_ref=src, dst_ref=dst, send_sem=send, recv_sem=recv,
            device_id={"prow": row, "pcol": col}, device_id_type=MESH,
        )

    def each(items, act):
        for item in items:
            if item[0] is True:
                act(item)
            elif item[0] is not False:
                pl.when(item[0])(functools.partial(act, item))

    def start_all(sends):
        each(sends, lambda item: item[1]().start())

    def sent_all(sends):
        each(sends, lambda item: item[1]().wait_send())

    height = diag_in.shape[0]
    side = 2 * height
    mine, theirs = (r // 2) * side, (cross // 2) * side

    def band(q):
        return pl.ds(pl.multiple_of(q * height, height), height)

    def half_cols(start, kind):
        return pl.ds(pl.multiple_of(start + (height if kind == 3 else 0), height), height)

    def small(kind, lane):
        part = cross if lane == 2 else r
        if kind in (0, 3):
            if lane == 0:
                src, dst = diag_in, a_ref.at[band(r), :]
            else:
                cols = half_cols(theirs if lane == 2 else mine, kind)
                dst = a_ref.at[band(part), cols]
                src = dst if lane == 2 else diag_in.at[:, cols]
        else:
            buf = (None, top_buf, pheno_buf)[kind]
            dst = buf.at[part]
            src = dst if lane == 2 else (None, top_in, pheno_in)[kind]
        return remote(
            src, dst, small_send.at[kind, lane], small_recv.at[kind, part],
            cross if lane == 1 else sib, c,
        )

    def small_wait(kind, part):
        if kind in (0, 3):
            dst = a_ref.at[band(part), :]
            if part is not sib:
                dst = a_ref.at[band(part), half_cols(theirs, kind)]
        else:
            dst = (None, top_buf, pheno_buf)[kind].at[part]
        remote(dst, dst, small_send.at[kind, 0], small_recv.at[kind, part], sib, c).wait_recv()

    def chunk(b, h):
        return row_buf.at[pl.ds(pl.multiple_of((2 * b + h) * half, half), half), :]

    def own_half(h):
        return panel_in.at[pl.ds(h * half, half), :]

    def row_copy(way, b, h, own=False):
        target = (c + ly, c - ly, other)[way]
        return lambda: remote(
            own_half(h) if own else chunk(b, h), chunk(b, h),
            row_send.at[way, 2 * b + h], row_recv.at[2 * b + h], r, target,
        )

    def row_wait(b, h):
        remote(chunk(b, h), chunk(b, h), row_send.at[0, 0], row_recv.at[2 * b + h], r, other).wait_recv()

    def col_at(i, h):
        return col_buf.at[pl.ds(pl.multiple_of((2 * i + h) * half, half), half), :]

    def col_copies(b, h, own):
        i = b - first
        src = own_half(h) if own else chunk(b, h)
        k = 2 * i + h
        return (
            remote(src, col_at(i, h), col_send.at[0, k], col_recv.at[k], cross, c),
            remote(src, col_at(i, h), col_send.at[1, k], col_recv.at[k], sib, c),
            pltpu.make_async_copy(src, col_at(i, h), local_sem.at[k]),
        )

    def col_start(b, h, own=False):
        @pl.when(is_root & (b >= first) & (b < first + col_parts))
        def _():
            for copy in col_copies(b, h, own):
                copy.start()

    def part(ref, b, h, p):
        rows = half // FINE
        return ref.at[pl.ds(pl.multiple_of((2 * b + h) * half + p * rows, rows), rows), :]

    def fine_copies(way, b, h):
        target = (c + ly, c - ly, other)[way]

        def one(p):
            return lambda: remote(
                part(row_buf, b, h, p), part(row_buf, b, h, p), fine_send.at[h, p], fine_recv.at[h, p], r, target
            )

        return [one(p) for p in range(FINE)]

    last_piece = jnp.where(low_end, (lz - 1) * ly, 0) + 1 - y

    def fine_col(h, p):
        src, dst = part(row_buf, last_piece, h, p), part(col_buf, last_piece - first, h, p)
        return (
            remote(src, dst, fine_col_send.at[0, h, p], fine_col_recv.at[h, p], cross, c),
            remote(src, dst, fine_col_send.at[1, h, p], fine_col_recv.at[h, p], sib, c),
            pltpu.make_async_copy(src, dst, fine_local.at[h, p]),
        )

    def fine_handed(h, p):
        dst = part(col_buf, last_piece - first, h, p)
        return remote(dst, dst, fine_col_send.at[1, h, p], fine_col_recv.at[h, p], sib, c)

    def fine_arrive():
        for p in range(FINE):
            for h in (1, 0):
                dst = part(row_buf, last_piece, h, p)
                remote(dst, dst, fine_send.at[h, p], fine_recv.at[h, p], r, other).wait_recv()

                @pl.when(is_root & far)
                def _():
                    for copy in fine_col(h, p):
                        copy.start()

    def fine_hand():
        for p in range(FINE):
            for h in (1, 0):
                fine_handed(h, p).wait_recv()
                fine_handed(h, p).start()

    def fine_ready():
        for p in range(FINE):
            for h in (1, 0):

                @pl.when(is_root)
                def _():
                    fine_col(h, p)[2].wait()

                @pl.when(jnp.logical_not(is_root) & (r != root_cross))
                def _():
                    fine_handed(h, p).wait_recv()

    def fine_sent():
        for p in range(FINE):
            for h in (1, 0):

                @pl.when(is_root)
                def _():
                    for copy in fine_col(h, p)[:2]:
                        copy.wait_send()

                @pl.when(r == root_cross)
                def _():
                    fine_handed(h, p).wait_send()

    def own_sends(h):
        return [
            (True, row_copy(2, c, h, True)),
            (z < lz - 1, row_copy(0, c, h, True)),
            (z > 0, row_copy(1, c, h, True)),
        ]

    def hop_arrivals(d, h):
        low, high = c - d * ly, c + d * ly
        low_over = True if h == 0 else z != d
        high_over = True if h == 0 else z + d != lz - 1
        low_across, high_across = [(low_over, row_copy(2, low, h))], [(high_over, row_copy(2, high, h))]
        if tuned and d == lz - 1 and h == 0:
            low_across = [(True, copy) for copy in fine_copies(2, low, h)]
            high_across = [(True, copy) for copy in fine_copies(2, high, h)]
        return [
            (z >= d, low, h, [(z < lz - 1, row_copy(0, low, h))] + low_across),
            (z + d < lz, high, h, [(z > 0, row_copy(1, high, h))] + high_across),
        ]

    def across_arrivals(d, h):
        if d == 0:
            sends = []
            if h == 1 and lz > 1:
                sends = [(low_end, row_copy(0, other, h)), (high_end, row_copy(1, other, h))]
            return [(True, other, h, sends)]
        return [
            (z >= d if h == 0 else z > d, other - d * ly, h, []),
            (z + d < lz if h == 0 else z + d < lz - 1, other + d * ly, h, []),
        ]

    def far_arrivals(d):
        low, high = 1 - y, (lz - 1) * ly + 1 - y
        ups, downs = [row_copy(0, low, 1)], [row_copy(1, high, 1)]
        if tuned and d == lz - 2:
            ups, downs = fine_copies(0, low, 1), fine_copies(1, high, 1)
        return [
            (z == d, low, 1, [(z < lz - 1, copy) for copy in ups]),
            (z == lz - 1 - d, high, 1, [(z > 0, copy) for copy in downs]),
        ]

    def arrive(items):
        def act(item):
            _, b, h, sends = item
            row_wait(b, h)
            start_all(sends)
            col_start(b, h)

        each(items, act)

    def finish(items):
        each(items, lambda item: sent_all(item[3]))

    small(0, 1).start()
    small(0, 0).start()
    small(3, 1).start()
    diag_copy = pltpu.make_async_copy(diag_in, a_ref.at[band(r), :], local_sem.at[2 * col_parts])
    diag_copy.start()
    for h in range(2):
        start_all(own_sends(h))
    for kind in (1, 2):
        small(kind, 1).start()
        small(kind, 0).start()
    own_copies = [
        pltpu.make_async_copy(own_half(h), chunk(c, h), local_sem.at[2 * col_parts + 1 + h]) for h in range(2)
    ]
    others = [
        pltpu.make_async_copy(src, dst, local_sem.at[2 * col_parts + 3 + k])
        for k, (src, dst) in enumerate((
            (top_in, top_buf.at[r]), (pheno_in, pheno_buf.at[r]), (rest_in, rest_buf),
            (geno_in, white_out),
        ))
    ]
    for copy in own_copies + others:
        copy.start()
    for h in range(2):
        col_start(c, h, True)
    trailing_sem = local_sem.at[2 * col_parts + 7]
    grid_copies(tuned, trailing_in, u_out, row_ids, col_ids, rows_piece, False, trailing_sem)
    others.append(pltpu.make_async_copy(trailing_in, u_out, trailing_sem))
    small_wait(0, cross)
    small(0, 2).start()
    small_wait(0, sib)
    small_wait(0, diag_x)
    diag_copy.wait()

    def diag_event():
        small_wait(3, cross)
        small(3, 2).start()

    def corner_event():
        small_wait(3, diag_x)
        small(0, 2).wait_send()
        small(3, 2).wait_send()

        @pl.when(r >= 2)
        def _():
            a_ref[:side, side:] = jnp.transpose(a_ref[side:, :side])

    def top_event():
        for kind in (1, 2):
            small_wait(kind, cross)
            small(kind, 2).start()

    def nothing():
        pass

    last = 2 * (lz - 1)

    def event(t):
        def run():
            if t <= last:
                arrive(hop_arrivals((t + 1) // 2, (t - 1) % 2))
            if t % 2 == 1 and t // 2 >= 1:
                arrive(far_arrivals(t // 2))
            if t == 2:
                arrive(across_arrivals(0, 0))
                arrive(across_arrivals(0, 1))
            if t >= 4 and (t - 2) // 2 < lz:
                arrive(across_arrivals((t - 2) // 2, t % 2))

        return run

    count = 2 * lz
    events = [nothing] * 16
    events[0], events[2], events[3] = diag_event, corner_event, event(1)
    events[4], events[7] = top_event, event(2)
    events[11], events[15] = event(3), event(4)
    invert(a_ref, w_ref, m_ref, events)

    def prepare():
        for kind in (1, 2):
            small_wait(kind, sib)
            small_wait(kind, diag_x)
        for copy in own_copies + others:
            copy.wait()
        whole = w_ref[...]
        w_hi[...], w_lo[...] = split2(whole)
        wt_hi[...], wt_lo[...] = split2(jnp.transpose(whole))
        w, turned = (w_hi[...], w_lo[...]), (wt_hi[...], wt_lo[...])
        ai_hi[...], ai_lo[...] = split2(dot3(turned, w, INNER))
        phenos = jnp.concatenate([pheno_buf[q] for q in range(pheno_buf.shape[0])], axis=1)
        joined = jnp.concatenate([top_buf[...].reshape(width, variants), column(phenos)], axis=1)
        both = dot3(w, split2(joined), INNER)
        g_hi[...], g_lo[...] = split2(dot3(turned, split2(both), INNER))
        white = both[:, :variants]
        stat[...] = jnp.zeros_like(stat)
        stat[2:3, :] = weighted(both[:, variants:], white)
        stat[3:4, :] = jnp.sum(white * white, axis=0, keepdims=True)
        at = pl.ds(pl.multiple_of(c * rows_piece, rows_piece), rows_piece)
        own_out[...] = dot3(split2(row_buf[at, :]), (wt_hi[...], wt_lo[...]), INNER)

    unit = rest_buf.shape[2]
    units = row_buf.shape[0] // unit
    col_unit = min(col_parts, max(1, 256 // rows_piece))
    col_units = col_parts // col_unit
    col_wide = col_unit * rows_piece

    def place(b):
        return pl.ds(pl.multiple_of(b * unit, unit), unit)

    def row_step(k, b):
        at, slot = place(b), place(k)
        parts = split2(row_buf[at, :])
        row_hi[slot, :], row_lo[slot, :] = parts
        shift = dot3(parts, (g_hi[...], g_lo[...]), INNER)
        white = white_out[at, :] - shift[:, :variants]
        white_out[at, :] = white
        stat[0:1, :] += weighted(column(rest_buf[b]) - shift[:, variants:], white)
        stat[1:2, :] += jnp.sum(white * white, axis=0, keepdims=True)

    def cols_of(q, count=1):
        return pl.ds(pl.multiple_of(q * col_wide, col_wide), col_wide * count)

    def product(k, many, q, count):
        slots = pl.ds(pl.multiple_of(k * unit, unit), unit * many)
        cols = cols_of(q, count)
        return dot3((row_hi[slots, :], row_lo[slots, :]), (y_hi[:, cols], y_lo[:, cols]), INNER)

    def col_ready(i, h):
        @pl.when(is_root)
        def _():
            pltpu.make_async_copy(col_at(i, h), col_at(i, h), local_sem.at[2 * i + h]).wait()

        @pl.when(jnp.logical_not(is_root))
        def _():
            handed = remote(col_at(i, h), col_at(i, h), col_send.at[1, 2 * i + h], col_recv.at[2 * i + h], sib, c)
            handed.wait_recv()
            pl.when(r == root_cross)(handed.start)

    def cols_ready(unit_at):
        for i in range(col_unit):
            for h in range(2):
                col_ready(unit_at * col_unit + i, h)

    def col_step(q, unit_at, waits=True):
        if waits:
            cols_ready(unit_at)
        y_hi[:, cols_of(q)], y_lo[:, cols_of(q)] = split2(
            dot3((ai_hi[...], ai_lo[...]), split2(col_buf[cols_of(unit_at), :]), LAST)
        )

    def send_stats():
        stat_buf[r] = stat[...]
        for k, target in enumerate((sib, cross, diag_x)):
            remote(stat, stat_buf.at[r], stat_send.at[k], stat_recv.at[r], target, c).start()

    if tuned:
        near = jnp.logical_not(far)

        def apply(k, many, q, count):
            u_out[pl.ds(pl.multiple_of(k * unit, unit), unit * many), cols_of(q, count)] -= product(k, many, q, count)

        def only(cond, items):
            return [(cond if item[0] is True else item[0] & cond,) + tuple(item[1:]) for item in items]

        def first_stage():
            arrive(across_arrivals(1, 1))
            arrive(hop_arrivals(3, 0))
            arrive(far_arrivals(2))
            arrive(only(low_end | high_end, across_arrivals(2, 0)))

        def second_stage():
            arrive(only((z > 0) & (z < lz - 1), across_arrivals(2, 0)))
            arrive(hop_arrivals(3, 1))
            arrive(across_arrivals(2, 1))

        def last_rows():
            pl.when((low_end | high_end) & near)(fine_arrive)
            row_step(7, row_ids[7])
            send_stats()

        def last_column():
            spare()
            fine_ready()

        def spare():
            def one(k):
                pl.when((k == 7) & (r == root_cross))(fine_hand)
                apply(k, 1, 0, 2)

            over(4, 8, one)

        def stage(t):
            pl.when(t == 1)(second_stage)
            pl.when((t == 2) & far & (low_end | high_end))(fine_arrive)
            pl.when(t < 3)(lambda: row_step(4 + t, pick(row_ids, 4 + t)))
            pl.when(((t == 3) & near) | ((t == 2) & far))(last_rows)
            unit_at = pick(col_ids, t)
            pl.when((t < 3) | near)(lambda: cols_ready(unit_at))
            pl.when((t == 3) & far)(last_column)
            col_step(t, unit_at, False)
            pl.when((t < 3) | near)(lambda: apply(0, 4, t, 1))

        prepare()
        first_stage()
        over(0, 4, lambda k: row_step(k, pick(row_ids, k)))
        over(0, 4, stage)
    else:
        for t in range(5, count + 2):
            event(t)()
        prepare()

        def apply(k):
            over(0, col_units, lambda q: apply_one(k, q))

        def apply_one(k, q):
            u_out[place(k), cols_of(q)] -= product(k, 1, q, 1)

        over(0, col_units, lambda q: col_step(q, q))
        over(0, units, lambda k: row_step(k, k))
        send_stats()
        over(0, units, apply)

    for k, source in enumerate((sib, cross, diag_x)):
        remote(stat, stat_buf.at[source], stat_send.at[k], stat_recv.at[source], sib, c).wait_recv()
    total = stat_buf[0]
    for q in range(1, stat_buf.shape[0]):
        total = total + stat_buf[q]
    people = jnp.float32(width + row_buf.shape[0] * stat_buf.shape[0])
    total_out[...] = jnp.zeros_like(total_out)
    total_out[0:1, :] = (total[0:1] + stat[2:3, :]) / jnp.sqrt(people)
    total_out[1:2, :] = (total[1:2] + stat[3:4, :]) / people

    for k in range(3):
        remote(stat, stat_buf.at[r], stat_send.at[k], stat_recv.at[r], sib, c).wait_send()
    for lane in range(2):
        small(0, lane).wait_send()
    small(3, 1).wait_send()
    for kind in (1, 2):
        for lane in range(3):
            small(kind, lane).wait_send()
    for h in range(2):
        sent_all(own_sends(h))
    finish(across_arrivals(0, 1))
    for d in range(1, lz):
        for h in range(2):
            finish(hop_arrivals(d, h))
        finish(far_arrivals(d))

    skip = jnp.where(far, last_piece - first, col_parts) if tuned else col_parts

    def sent(k):
        def act():
            for h in range(2):
                handed = remote(
                    col_at(k, h), col_at(k, h), col_send.at[1, 2 * k + h], col_recv.at[0], sib, c
                )
                pl.when(is_root | (r == root_cross))(handed.wait_send)
                over_x = remote(
                    col_at(k, h), col_at(k, h), col_send.at[0, 2 * k + h], col_recv.at[0], sib, c
                )
                pl.when(is_root)(over_x.wait_send)

        pl.when(k != skip)(act)

    over(0, col_parts, sent)
    if tuned:
        pl.when(far)(fine_sent)


def store_kernel(
    ly, lz, group,
    u_in, white_in, own_in, total_in, row_hi, row_lo, y_hi, y_lo,
    u_out, white_out, own_out, score_out, info_out,
    held, sem, row_sem,
):
    c = lax.axis_index("pcol")
    rows_piece = own_in.shape[0]
    col_parts = u_in.shape[1] // rows_piece
    tuned = is_tuned(lz, rows_piece, col_parts)
    pairs = [(own_in, own_out), (white_in, white_out)]
    pairs += [(total_in.at[0:1], score_out), (total_in.at[1:2], info_out)]
    copies = [pltpu.make_async_copy(src, dst, sem.at[1 + k]) for k, (src, dst) in enumerate(pairs)]
    if not tuned:
        copies.append(pltpu.make_async_copy(u_in, u_out, sem.at[0]))
        for copy in copies:
            copy.start()
        for copy in copies:
            copy.wait()
        return
    far, row_ids, col_ids = orders(ly, lz, lax.rem(c, group) * col_parts, c // ly, lax.rem(c, ly))
    near = jnp.logical_not(far)

    def span(k):
        return pl.ds(pl.multiple_of(k * rows_piece, rows_piece), rows_piece)

    def store_row(k, src, at, row_at, cols=range(4)):
        for j in cols:
            pltpu.make_async_copy(
                src.at[span(at), span(j)], u_out.at[span(pick(row_ids, k)), span(col_ids[j])], row_at
            ).start()

    over(0, 4, lambda k: store_row(k, u_in, k, row_sem.at[k], range(3)))
    pl.when(near)(lambda: over(0, 4, lambda k: store_row(k, u_in, k, row_sem.at[k], (3,))))
    for copy in copies:
        copy.start()

    pl.when(far)(lambda: over(4, 8, lambda k: store_row(k, u_in, k, row_sem.at[k], (0, 1))))

    def later(k, start):
        at, cols = span(k), pl.ds(start * rows_piece, (4 - start) * rows_piece)
        moved = dot3((row_hi[at, :], row_lo[at, :]), (y_hi[:, cols], y_lo[:, cols]), INNER)
        held[span(k - 4), cols] = u_in[at, cols] - moved
        store_row(k, held, k - 4, row_sem.at[k], range(start, 4))

    def corner(k):
        at, cols = span(k), pl.ds(3 * rows_piece, rows_piece)
        moved = dot3((row_hi[at, :], row_lo[at, :]), (y_hi[:, cols], y_lo[:, cols]), INNER)
        held[at, :rows_piece] = u_in[at, cols] - moved
        pltpu.make_async_copy(
            held.at[at, pl.ds(0, rows_piece)], u_out.at[span(pick(row_ids, k)), span(col_ids[3])], row_sem.at[k]
        ).start()

    pl.when(far)(lambda: over(0, 4, corner))
    pl.when(near)(lambda: over(4, 8, lambda k: later(k, 0)))
    pl.when(far)(lambda: over(4, 8, lambda k: later(k, 2)))
    for copy in copies:
        copy.wait()
    over(0, 8, lambda k: pltpu.make_async_copy(held.at[span(0), :], u_out.at[span(0), :], row_sem.at[k]).wait())


def local(diag_block, panel_cols, trailing, geno_top, geno_rest, pheno_top, pheno_rest):
    prow_size, pcol_size = lax.axis_size("prow"), lax.axis_size("pcol")
    height, width = diag_block.shape
    rows_piece = panel_cols.shape[0]
    row_count, col_count = trailing.shape
    variants = geno_top.shape[1]
    ly = 2
    lz = pcol_size // ly
    unit = min(row_count, max(rows_piece, 256))
    chunks, col_chunks = 2 * pcol_size, 2 * (col_count // rows_piece)
    f32, bf16 = jnp.float32, jnp.bfloat16
    vmem = pl.BlockSpec(memory_space=pltpu.VMEM)
    hbm = pl.BlockSpec(memory_space=pltpu.HBM)
    dma = pltpu.SemaphoreType.DMA
    wide = variants + BLOCK
    stats = (8, variants)
    arrays = [
        ((width, width), f32), ((BLOCK, 2 * BLOCK), f32), ((width, width), f32),
        ((row_count, width), f32), ((col_count, width), f32),
        ((prow_size, height, variants), f32), ((prow_size, 1, height), f32),
        ((row_count // unit, 1, unit), f32),
        ((width, wide), bf16), ((width, wide), bf16),
    ]
    arrays += [((width, width), bf16)] * 6
    arrays += [(stats, f32), ((prow_size,) + stats, f32)]
    held = pl.pallas_call(
        functools.partial(main_kernel, ly, lz, pcol_size // prow_size),
        out_shape=(
            pltpu.VMEM(trailing.shape, f32),
            pltpu.VMEM(geno_rest.shape, f32),
            pltpu.VMEM(panel_cols.shape, f32),
            pltpu.VMEM(stats, f32),
            pltpu.VMEM((row_count, width), bf16),
            pltpu.VMEM((row_count, width), bf16),
            pltpu.VMEM((width, col_count), bf16),
            pltpu.VMEM((width, col_count), bf16),
        ),
        in_specs=[hbm] * 7,
        out_specs=(vmem,) * 8,
        scratch_shapes=[pltpu.VMEM(shape, dtype) for shape, dtype in arrays]
        + [
            dma((4, 3)), dma((4, prow_size)), dma((3, chunks)), dma((chunks,)),
            dma((2, col_chunks)), dma((col_chunks,)), dma((3,)), dma((prow_size,)), dma((col_chunks + 9,)),
            dma((2, FINE)), dma((2, FINE)), dma((2, 2, FINE)), dma((2, FINE)), dma((2, FINE)),
        ],
        compiler_params=pltpu.CompilerParams(
            collective_id=0, has_side_effects=True, vmem_limit_bytes=32 * 1024 * 1024
        ),
    )(
        *(pltpu.with_memory_space_constraint(value, pltpu.HBM) for value in (
            diag_block, geno_top, pheno_top.reshape(1, height), panel_cols, trailing, geno_rest,
            pheno_rest.reshape(row_count // unit, 1, unit),
        ))
    )
    updated_block, own_factor, white_geno, score, info = order(pl.pallas_call(
        functools.partial(store_kernel, ly, lz, pcol_size // prow_size),
        out_shape=(
            jax.ShapeDtypeStruct(trailing.shape, f32),
            jax.ShapeDtypeStruct(geno_rest.shape, f32),
            jax.ShapeDtypeStruct(panel_cols.shape, f32),
            jax.ShapeDtypeStruct((1, variants), f32),
            jax.ShapeDtypeStruct((1, variants), f32),
        ),
        in_specs=[vmem] * 8,
        out_specs=(hbm,) * 5,
        scratch_shapes=[
            pltpu.VMEM((row_count // 2, col_count), f32), dma((5,)), dma((8,)),
        ],
        compiler_params=pltpu.CompilerParams(vmem_limit_bytes=12 * 1024 * 1024),
    )(*(pltpu.with_memory_space_constraint(value, pltpu.VMEM) for value in held)))
    return (updated_block, own_factor, white_geno, score.reshape(variants), info.reshape(variants))


def order(values):
    updated, white, own, score, info = values
    return updated, own, white, score, info


def solution(mesh):
    placed = (
        P("prow", None),
        P(("prow", "pcol"), None),
        P("prow", "pcol"),
        P("prow", "pcol"),
        P("prow", "pcol"),
        P("prow"),
        P("prow"),
    )
    return jax.shard_map(
        local,
        mesh=mesh,
        in_specs=placed,
        out_specs=(
            P("prow", "pcol"),
            P(("prow", "pcol"), None),
            P("prow", "pcol"),
            P("pcol"),
            P("pcol"),
        ),
        check_vma=False,
    )
```
